512 devices in a mesh: samples: 64 (over x, z, core), targets: 8 (over y).
Axes of the slice: x: 4, y: 8, z: 8, core: 2. Of those that a mesh axis runs over, the one named last changes fastest.
Arguments:
- read_depth: bfloat16 [40960, 20480], P('samples', 'targets'), may hold values from -60 to 60, as said below
- gauss_sketch: bfloat16 [20480, 256], P('targets'), may hold values from -0.0390625 to 0.0390625
- keep_mask: int32 [20480], P('targets'), may hold values 0 or 1
Outputs:
- projection: float32 [20480, 256], P(('targets', 'samples'))
The draws below stay inside these ranges and needn't reach their ends.
Inputs may be any that keep to these rules, and one draw needn't show every extreme that they name: `read_depth`: each entry is an independent rough value times a scale of its sample and a scale of its target.
All inputs are finite; a program needn't handle non-finite values. No bound on the sum of `keep_mask` on one device may be relied on, other than what follows from the above.
Results may differ from the reference program's by a relative error of at most 0.0012.
Values may be sent and summed in bfloat16 or wider, within the bound.
A program may use at most 64 MiB of HBM per device.

```python
import math
import jax
import jax.numpy as jnp
from jax import lax

K = 256
N = 20480
MD = 640
M = 40960


def draw_read_depth(key, part):
    key = jax.random.fold_in(key, 11)
    key_rows, key_cols, key_noise = jax.random.split(key, 3)
    row_lo, row_hi = (0.3, 3.0)
    noise = jnp.clip(jax.random.normal(key_noise, (M, N), jnp.float32), -6.0, 6.0)
    row_part = jnp.exp(jax.random.uniform(key_rows, (M, 1), jnp.float32, math.log(row_lo), math.log(row_hi)))
    col_part = jnp.exp(jax.random.uniform(key_cols, (1, N), jnp.float32, math.log(0.3), math.log(3.0)))
    return (noise * row_part * col_part).astype(jnp.bfloat16)


def set_ends(result, key, smallest, largest):
    place = [jax.random.randint(jax.random.fold_in(key, axis), (), 0, length) for axis, length in enumerate(result.shape)]
    widest = result.shape.index(max(result.shape))
    neighbour = place[:widest] + [(place[widest] + 1) % result.shape[widest]] + place[widest + 1:]
    return result.at[tuple(place)].set(smallest).at[tuple(neighbour)].set(largest)


def block_scale(stream_key, extent, cuts, smallest, high):
    def one(dim, blocks):
        draws = jax.random.uniform(jax.random.fold_in(jax.random.fold_in(stream_key, 6), dim), (blocks,), jnp.float32, smallest / len(cuts), high / len(cuts))
        return jnp.repeat(jnp.exp(draws), extent[dim] // blocks).reshape((-1,) + (1,) * (len(extent) - dim - 1))

    gain = one(*cuts[0])
    for cut in cuts[1:]:
        gain = gain * one(*cut)
    return gain


def centred(rng, extent, spread, bound, pieces=(), dtype=jnp.bfloat16):
    result = jax.random.normal(rng, extent, jnp.float32) * spread
    if len(pieces) > 0:
        result = block_scale(rng, extent, pieces, -0.22, 0.18) * result
    return jnp.clip(result, min=-bound, max=bound).astype(dtype)


def setup_inputs(seed: int = 0) -> dict:
    key_list = jax.random.split(jax.random.key(seed), 4)
    read_depth = draw_read_depth(jax.random.fold_in(key_list[3], 71), 0)
    gauss_sketch = centred(key_list[1], (N, K), N ** -0.5, 0.0390625, ((0, 8),))
    keep_mask = set_ends((jax.random.randint(key_list[2], (N,), 0, 10) < 9).astype(jnp.int32), jax.random.fold_in(key_list[2], 1), 0, 1)
    return dict(read_depth=read_depth, gauss_sketch=gauss_sketch, keep_mask=keep_mask)


def reference(read_depth, gauss_sketch, keep_mask):
    kept = keep_mask.astype(jnp.float32)
    kept_count = jnp.sum(kept)
    masked_sketch = jnp.where(keep_mask[:, None] > 0, gauss_sketch, jnp.zeros_like(gauss_sketch))
    raw_sketch = jnp.dot(read_depth.astype(jnp.float32), masked_sketch.astype(jnp.float32), preferred_element_type=jnp.float32)
    blocks = read_depth.reshape(M // MD, MD, N)

    def block_squares(block):
        values = block.astype(jnp.float32)
        return lax.optimization_barrier(jnp.sum(values * values * kept[None, :], axis=1))
    row_squares = lax.map(block_squares, blocks).reshape(M)
    row_scale = jnp.sqrt((row_squares + 1.0) / (kept_count + 1.0))
    sketched = raw_sketch / row_scale[:, None]
    gram_matrix = jnp.dot(sketched.T, sketched, precision=lax.Precision.HIGHEST)
    lower = jnp.linalg.cholesky(gram_matrix)
    basis = lax.linalg.triangular_solve(lower, sketched, left_side=False, lower=True, transpose_a=True)
    weighted = (basis / row_scale[:, None]).astype(jnp.bfloat16)
    projection = lax.dot_general(read_depth.astype(jnp.float32), weighted.astype(jnp.float32), (((0,), (0,)), ((), ())), preferred_element_type=jnp.float32)
    return projection * kept[:, None]
```

```python
import functools

import jax
import jax.numpy as jnp
from jax import lax
from jax.experimental import pallas as pl
from jax.experimental.pallas import tpu as pltpu
from jax.sharding import PartitionSpec as P

MESH = pl.DeviceIdType.MESH
F32 = jnp.float32
HIGH = lax.Precision.HIGHEST
STEPS = 4
TOLERANCE = 1e-3


def far_first(n):
    return sorted(range(1, n), key=lambda d: -min(d, n - d))


def whole_max(v):
    return jnp.max(jnp.max(jnp.abs(v), axis=0, keepdims=True), axis=1, keepdims=True)


def scale_code(peak):
    return jnp.ceil(jnp.log2(jnp.maximum(peak, 1e-30)) * 256.0) + 1.0


def to_fixed(v, code):
    unit = 32767.0 * jnp.exp2(code * (-1.0 / 256.0))
    return jnp.round(v * unit).astype(jnp.int32).astype(jnp.int16)


def code_rows(code, columns):
    return jnp.broadcast_to(code.astype(jnp.int32), (16, columns)).astype(jnp.int16)


def from_fixed(message, rows):
    code = message[rows:].astype(jnp.int32).astype(F32)[0:1]
    unit = jnp.exp2(code * (1.0 / 256.0)) * (1.0 / 32767.0)
    return message[:rows].astype(jnp.int32).astype(F32) * unit


def half_lower(e):
    k = e.shape[0]
    row = lax.broadcasted_iota(jnp.int32, (k, k), 0)
    col = lax.broadcasted_iota(jnp.int32, (k, k), 1)
    return jnp.where(row > col, e, jnp.where(row == col, 0.5 * e, 0.0))


def identity(k):
    row = lax.broadcasted_iota(jnp.int32, (k, k), 0)
    col = lax.broadcasted_iota(jnp.int32, (k, k), 1)
    return jnp.where(row == col, 1.0, 0.0).astype(F32)


def times_t(a, b):
    return lax.dot_general(a, b, (((1,), (1,)), ((), ())), precision=HIGH, preferred_element_type=F32)


def times(a, b):
    return lax.dot_general(a, b, (((1,), (0,)), ((), ())), precision=HIGH, preferred_element_type=F32)


def all_bytes(ref, sem):
    return pltpu.make_async_copy(ref, ref, sem)


def main_kernel(
    NX, NY, NZ, NC,
    depth_hbm, gauss_hbm, keep_ref,
    part_ref, gram_ref, inverse_ref, off_ref,
    depth, gauss, depth_t, load_sem,
    p_send, p_recv, aux_send, aux_recv, w_all,
    g_own, gx_recv, g_sum, gz_recv, g_piece, gy_recv, g_block, g_full,
    own, c_send, c_recv, x_send, x_recv, z_send, z_recv,
    send_sem, recv_sem, core_send_sem, core_recv_sem,
):
    rows, cols = depth.shape
    K = gauss.shape[1]
    RY = rows // NY
    TS = cols // (NX * NZ * NC)
    XB = NZ * TS
    NU = NX * NC
    GX = 2 * K // NU
    GZ = GX // NZ

    s = lax.axis_index("samples")
    y = lax.axis_index("targets")
    core = lax.rem(s, NC)
    z = lax.rem(s // NC, NZ)
    x = s // (NC * NZ)
    u = x * NC + core

    def at_y(d):
        return (s, lax.rem(y + d, NY))

    def place(x1, z1, c1):
        return ((x1 * NZ + z1) * NC + c1, y)

    def at_u(d):
        u1 = lax.rem(u + d, NU)
        return place(u1 // NC, z, lax.rem(u1, NC))

    def at_z(d):
        return place(x, lax.rem(z + d, NZ), core)

    def at_x(d):
        return place(lax.rem(x + d, NX), z, core)

    def send(src, dst, phase, to):
        pltpu.make_async_remote_copy(
            src_ref=src, dst_ref=dst, send_sem=send_sem.at[phase], recv_sem=recv_sem.at[phase],
            device_id=to, device_id_type=MESH,
        ).start()

    y_order, u_order, z_order, x_order = far_first(NY), far_first(NU), far_first(NZ), far_first(NX)

    def row_block(y1):
        return pl.ds(pl.multiple_of(y1 * RY, 16), RY)

    gauss_load = pltpu.make_async_copy(gauss_hbm, gauss, load_sem.at[0])
    gauss_load.start()
    loads = []
    for i, d in enumerate(y_order + [0]):
        block = row_block(lax.rem(y + d, NY))
        load = pltpu.make_async_copy(depth_hbm.at[block], depth.at[block], load_sem.at[i + 1])
        load.start()
        loads.append(load)

    barrier = pltpu.get_barrier_semaphore()
    for d in y_order:
        pl.semaphore_signal(barrier, inc=1, device_id=at_y(d), device_id_type=MESH)
    for d in u_order:
        pl.semaphore_signal(barrier, inc=1, device_id=at_u(d), device_id_type=MESH)
    for d in z_order:
        pl.semaphore_signal(barrier, inc=1, device_id=at_z(d), device_id_type=MESH)
    pl.semaphore_wait(barrier, NY + NU + NZ - 3)

    kept = keep_ref[...].astype(F32)
    count = jnp.sum(kept, axis=1, keepdims=True)
    sub = lax.broadcasted_iota(jnp.int32, (8, 128), 0)
    gauss_load.wait()

    raw_own = None
    for i, d in enumerate(y_order + [0]):
        block = row_block(lax.rem(y + d, NY))
        loads[i].wait()
        values = depth[block, :].astype(F32) * kept
        masked = values.astype(jnp.bfloat16)
        depth[block, :] = masked
        squares = values * values
        lanes = squares[:, 0:128]
        for j in range(1, cols // 128):
            lanes = lanes + squares[:, j * 128:(j + 1) * 128]
        raw = jnp.dot(masked, gauss[...], preferred_element_type=F32)
        q_row = jnp.sum(lanes.T, axis=0, keepdims=True)
        if RY < 128:
            q_row = jnp.concatenate([q_row, jnp.zeros((1, 128 - RY), F32)], axis=1)
        if d == 0:
            raw_own = raw
            peak = jnp.zeros((1, 1), F32)
        else:
            q_col = jnp.sum(lanes, axis=1, keepdims=True)
            level = raw * lax.rsqrt(jnp.maximum(q_col, 1e-30))
            peak = scale_code(whole_max(level))
            p_send[d] = to_fixed(level, peak)
        aux = jnp.where(sub == 0, q_row, jnp.where(sub == 1, peak, jnp.where(sub == 2, count, 0.0)))
        if d == 0:
            aux_recv[0] = aux
        else:
            aux_send[d] = aux
            send(aux_send.at[d], aux_recv.at[d], 0, at_y(d))
            send(p_send.at[d], p_recv.at[d], 1, at_y(d))

    def turn(j, _):
        at = pl.ds(pl.multiple_of(j * 128, 128), 128)
        depth_t[at, :] = depth[:, at].T
        return 0

    lax.fori_loop(0, cols // 128, turn, 0)

    others = pl.ds(1, NY - 1)
    all_bytes(aux_recv.at[others], recv_sem.at[0]).wait()
    all_bytes(p_recv.at[others], recv_sem.at[1]).wait()
    q_tile = aux_recv[:, 0, :]
    q_cols = q_tile.T[:RY]
    q_total = jnp.sum(q_cols, axis=1, keepdims=True)
    counts = aux_recv[0, 2:3, 0:1]
    for d in y_order:
        counts = counts + aux_recv[d, 2:3, 0:1]
    raw = raw_own
    for d in y_order:
        unit = jnp.exp2(aux_recv[d, 1:2, 0:1] * (1.0 / 256.0)) * (1.0 / 32767.0)
        root = jnp.sqrt(jnp.maximum(q_cols[:, d:d + 1], 1e-30)) * unit
        raw = raw + p_recv[d].astype(jnp.int32).astype(F32) * root
    scale = jnp.sqrt((q_total + 1.0) / (counts + 1.0))
    sketched = raw / scale
    weighted = (sketched / scale).astype(jnp.bfloat16)

    mine = row_block(y)
    w_all[mine, :] = weighted
    for d in y_order:
        send(w_all.at[mine], w_all.at[mine], 2, at_y(d))
    gram = lax.dot_general(
        sketched.T, sketched, (((1,), (0,)), ((), ())), precision=HIGH, preferred_element_type=F32
    )
    g_own[0:K, :] = gram[:, 0:128]
    g_own[K:2 * K, :] = gram[:, 128:256]
    for d in u_order:
        u1 = lax.rem(u + d, NU)
        send(g_own.at[pl.ds(pl.multiple_of(u1 * GX, 8), GX)], gx_recv.at[d], 3, at_u(d))
    all_bytes(gx_recv.at[pl.ds(1, NU - 1)], recv_sem.at[3]).wait()
    total = g_own[pl.ds(pl.multiple_of(u * GX, 8), GX), :]
    for d in u_order:
        total = total + gx_recv[d]
    g_sum[...] = total
    for d in z_order:
        z1 = lax.rem(z + d, NZ)
        send(g_sum.at[pl.ds(pl.multiple_of(z1 * GZ, 8), GZ)], gz_recv.at[d], 4, at_z(d))
    all_bytes(gz_recv.at[pl.ds(1, NZ - 1)], recv_sem.at[4]).wait()
    piece = g_sum[pl.ds(pl.multiple_of(z * GZ, 8), GZ), :]
    for d in z_order:
        piece = piece + gz_recv[d]
    g_piece[...] = piece
    for d in y_order:
        send(g_piece, gy_recv.at[d], 5, at_y(d))

    all_bytes(w_all.at[pl.ds(0, rows - RY)], recv_sem.at[2]).wait()
    c_copies = []
    for i, d in enumerate(x_order + [0]):
        x1 = lax.rem(x + d, NX)
        big = jnp.dot(
            depth_t[pl.ds(pl.multiple_of(x1 * (XB * NC), 16), XB * NC), :], w_all[...],
            preferred_element_type=F32,
        )
        even = jnp.concatenate([big[2 * j * TS:(2 * j + 1) * TS] for j in range(NZ)], axis=0)
        odd = jnp.concatenate([big[(2 * j + 1) * TS:(2 * j + 2) * TS] for j in range(NZ)], axis=0)
        keep_half = jnp.where(core == 0, even, odd)
        give_half = jnp.where(core == 0, odd, even)
        own[d] = keep_half
        code = scale_code(whole_max(give_half))
        c_send[d, 0:XB, :] = to_fixed(give_half, code)
        c_send[d, XB:XB + 16, :] = code_rows(code, K)
        copy = pltpu.make_async_remote_copy(
            src_ref=c_send.at[d], dst_ref=c_recv.at[d],
            send_sem=core_send_sem.at[d], recv_sem=core_recv_sem.at[d],
            device_id=place(x, z, 1 - core), device_id_type=MESH,
        )
        copy.start()
        c_copies.append(copy)
        if i == 0:
            all_bytes(gy_recv.at[others], recv_sem.at[5]).wait()
            piece = g_piece[...]
            for e in y_order:
                piece = piece + gy_recv[e]
            here = pl.ds(pl.multiple_of(z * GZ, 8), GZ)
            g_block[here, :] = piece
            for e in z_order:
                send(g_block.at[here], g_block.at[here], 6, at_z(e))

    all_bytes(g_block.at[pl.ds(0, GX - GZ)], recv_sem.at[6]).wait()
    there = pl.ds(pl.multiple_of(u * GX, 8), GX)
    g_full[there, :] = g_block[...]
    for d in u_order:
        send(g_block, g_full.at[there], 7, at_u(d))

    half = None
    for i, d in enumerate(x_order + [0]):
        c_copies[i].wait()
        half = own[d] + from_fixed(c_recv[d], XB)
        if d != 0:
            code = scale_code(whole_max(half))
            x_send[d, 0:XB, :] = to_fixed(half, code)
            x_send[d, XB:XB + 16, :] = code_rows(code, K)
            send(x_send.at[d], x_recv.at[d], 8, at_x(d))
    own[0] = half

    all_bytes(g_full.at[pl.ds(0, 2 * K - GX)], recv_sem.at[7]).wait()
    gram = jnp.concatenate([g_full[0:K, :], g_full[K:2 * K, :]], axis=1)
    gram_ref[...] = gram
    eye = identity(K)
    diagonal = gram * eye
    d_row = lax.rsqrt(jnp.sum(diagonal, axis=0, keepdims=True))
    d_col = lax.rsqrt(jnp.sum(diagonal, axis=1, keepdims=True))
    unit_gram = gram * d_row * d_col
    inverse = eye - half_lower(unit_gram - eye)
    error = None
    for _ in range(STEPS):
        error = times_t(times(inverse, unit_gram), inverse) - eye
        inverse = inverse - times(half_lower(error), inverse)
    inverse_ref[...] = inverse * d_row
    off_ref[...] = jnp.broadcast_to(whole_max(error), (8, 128))

    all_bytes(x_recv.at[pl.ds(1, NX - 1)], recv_sem.at[8]).wait()
    half = own[0]
    for d in x_order:
        half = half + from_fixed(x_recv[d], XB)
    code = scale_code(whole_max(half))
    last = code_rows(code, 128)
    own[0] = half
    for d in z_order:
        z1 = lax.rem(z + d, NZ)
        v = own[0, pl.ds(pl.multiple_of(z1 * TS, 8), TS), :]
        v = jnp.concatenate([v[:, 0:128], v[:, 128:256]], axis=0)
        z_send[d, 0:2 * TS, :] = to_fixed(v, code)
        z_send[d, 2 * TS:2 * TS + 16, :] = last
        send(z_send.at[d], z_recv.at[d], 9, at_z(d))
    all_bytes(z_recv.at[pl.ds(1, NZ - 1)], recv_sem.at[9]).wait()
    v = own[0, pl.ds(pl.multiple_of(z * TS, 8), TS), :]
    v = jnp.concatenate([v[:, 0:128], v[:, 128:256]], axis=0)
    for d in z_order:
        v = v + from_fixed(z_recv[d], 2 * TS)
    part_ref[...] = jnp.concatenate([v[0:TS], v[TS:2 * TS]], axis=1)

    all_bytes(aux_send.at[others], send_sem.at[0]).wait()
    all_bytes(p_send.at[others], send_sem.at[1]).wait()
    all_bytes(w_all.at[pl.ds(0, rows - RY)], send_sem.at[2]).wait()
    all_bytes(gx_recv.at[pl.ds(1, NU - 1)], send_sem.at[3]).wait()
    all_bytes(gz_recv.at[pl.ds(1, NZ - 1)], send_sem.at[4]).wait()
    all_bytes(gy_recv.at[others], send_sem.at[5]).wait()
    all_bytes(g_block.at[pl.ds(0, GX - GZ)], send_sem.at[6]).wait()
    all_bytes(g_full.at[pl.ds(0, 2 * K - GX)], send_sem.at[7]).wait()
    all_bytes(x_send.at[pl.ds(1, NX - 1)], send_sem.at[8]).wait()
    all_bytes(z_send.at[pl.ds(1, NZ - 1)], send_sem.at[9]).wait()


def last_kernel(part_ref, inverse_ref, off_ref, gram_hbm, out_ref, work, right, sem):
    K = work.shape[0]
    settled = jnp.max(off_ref[...]) < TOLERANCE

    @pl.when(settled)
    def _():
        out_ref[...] = times_t(part_ref[...], inverse_ref[...])

    @pl.when(jnp.logical_not(settled))
    def _():
        load = pltpu.make_async_copy(gram_hbm, work, sem)
        load.start()
        load.wait()
        right[...] = identity(K)
        lane = lax.broadcasted_iota(jnp.int32, (1, K), 1)
        row = lax.broadcasted_iota(jnp.int32, (K, 1), 0)

        def step(k, _):
            m = work[...]
            top = work[pl.ds(k, 1), :]
            pivot = jnp.sum(jnp.where(lane == k, top, 0.0), axis=1, keepdims=True)
            column = jnp.sum(jnp.where(lane == k, m, 0.0), axis=1, keepdims=True)
            factor = jnp.where(row > k, column / pivot, 0.0)
            r = right[...]
            r_top = right[pl.ds(k, 1), :]
            work[...] = m - factor * top
            right[...] = r - factor * r_top
            return 0

        lax.fori_loop(0, K, step, 0)
        pivots = jnp.sum(work[...] * identity(K), axis=1, keepdims=True)
        out_ref[...] = times_t(part_ref[...], right[...] / jnp.sqrt(pivots))


def solution(mesh, sizes=(4, 8, 8, 2)):
    NX, NY, NZ, NC = sizes

    def on_device(read_depth, gauss_sketch, keep_mask):
        rows, cols = read_depth.shape
        K = gauss_sketch.shape[1]
        RY = rows // NY
        TS = cols // (NX * NZ * NC)
        XB = NZ * TS
        NU = NX * NC
        GX = 2 * K // NU
        GZ = GX // NZ
        vmem = pl.BlockSpec(memory_space=pltpu.VMEM)
        hbm = pl.BlockSpec(memory_space=pl.ANY)
        i16 = jnp.int16
        part, gram, inverse, off = pl.pallas_call(
            functools.partial(main_kernel, NX, NY, NZ, NC),
            out_shape=(
                jax.ShapeDtypeStruct((TS, K), F32),
                jax.ShapeDtypeStruct((K, K), F32),
                jax.ShapeDtypeStruct((K, K), F32),
                jax.ShapeDtypeStruct((8, 128), F32),
            ),
            in_specs=[hbm, hbm, vmem],
            out_specs=(vmem, vmem, vmem, vmem),
            scratch_shapes=[
                pltpu.VMEM((rows, cols), jnp.bfloat16),
                pltpu.VMEM((cols, K), jnp.bfloat16),
                pltpu.VMEM((cols, rows), jnp.bfloat16),
                pltpu.SemaphoreType.DMA((NY + 1,)),
                pltpu.VMEM((NY, RY, K), i16),
                pltpu.VMEM((NY, RY, K), i16),
                pltpu.VMEM((NY, 8, 128), F32),
                pltpu.VMEM((NY, 8, 128), F32),
                pltpu.VMEM((rows, K), jnp.bfloat16),
                pltpu.VMEM((2 * K, 128), F32),
                pltpu.VMEM((NU, GX, 128), F32),
                pltpu.VMEM((GX, 128), F32),
                pltpu.VMEM((NZ, GZ, 128), F32),
                pltpu.VMEM((GZ, 128), F32),
                pltpu.VMEM((NY, GZ, 128), F32),
                pltpu.VMEM((GX, 128), F32),
                pltpu.VMEM((2 * K, 128), F32),
                pltpu.VMEM((NX, XB, K), F32),
                pltpu.VMEM((NX, XB + 16, K), i16),
                pltpu.VMEM((NX, XB + 16, K), i16),
                pltpu.VMEM((NX, XB + 16, K), i16),
                pltpu.VMEM((NX, XB + 16, K), i16),
                pltpu.VMEM((NZ, 2 * TS + 16, 128), i16),
                pltpu.VMEM((NZ, 2 * TS + 16, 128), i16),
                pltpu.SemaphoreType.DMA((10,)),
                pltpu.SemaphoreType.DMA((10,)),
                pltpu.SemaphoreType.DMA((NX,)),
                pltpu.SemaphoreType.DMA((NX,)),
            ],
            compiler_params=pltpu.CompilerParams(
                collective_id=0, has_side_effects=True, vmem_limit_bytes=48 << 20
            ),
        )(read_depth, gauss_sketch, keep_mask.reshape(1, cols))
        return pl.pallas_call(
            last_kernel,
            out_shape=jax.ShapeDtypeStruct((TS, K), F32),
            in_specs=[vmem, vmem, vmem, hbm],
            out_specs=vmem,
            scratch_shapes=[
                pltpu.VMEM((K, K), F32),
                pltpu.VMEM((K, K), F32),
                pltpu.SemaphoreType.DMA,
            ],
        )(part, inverse, off, gram)

    return jax.shard_map(
        on_device,
        mesh=mesh,
        in_specs=(P("samples", "targets"), P("targets", None), P("targets")),
        out_specs=P(("targets", "samples"), None),
        check_vma=False,
    )
```

```python
import functools

import jax
import jax.numpy as jnp
from jax import lax
from jax.experimental import pallas as pl
from jax.experimental.pallas import tpu as pltpu
from jax.sharding import PartitionSpec as P

MESH = pl.DeviceIdType.MESH
F32 = jnp.float32
HIGH = lax.Precision.HIGHEST
TOLERANCE = 2e-3


def far_first(n):
    return sorted(range(1, n), key=lambda d: -min(d, n - d))


def whole_max(v):
    return jnp.max(jnp.max(jnp.abs(v), axis=0, keepdims=True), axis=1, keepdims=True)


def scale_code(peak):
    return jnp.ceil(jnp.log2(jnp.maximum(peak, 1e-30)) * 256.0) + 1.0


def to_fixed(v, code):
    unit = 32767.0 * jnp.exp2(code * (-1.0 / 256.0))
    return jnp.round(v * unit).astype(jnp.int32).astype(jnp.int16)


def code_rows(code, columns):
    return jnp.broadcast_to(code.astype(jnp.int32), (16, columns)).astype(jnp.int16)


def from_fixed(message, rows):
    code = message[rows:].astype(jnp.int32).astype(F32)[0:1]
    unit = jnp.exp2(code * (1.0 / 256.0)) * (1.0 / 32767.0)
    return message[:rows].astype(jnp.int32).astype(F32) * unit


def half_lower(e):
    k = e.shape[0]
    row = lax.broadcasted_iota(jnp.int32, (k, k), 0)
    col = lax.broadcasted_iota(jnp.int32, (k, k), 1)
    return jnp.where(row > col, e, jnp.where(row == col, 0.5 * e, 0.0))


def identity(k):
    row = lax.broadcasted_iota(jnp.int32, (k, k), 0)
    col = lax.broadcasted_iota(jnp.int32, (k, k), 1)
    return jnp.where(row == col, 1.0, 0.0).astype(F32)


def halves(a):
    high = a.astype(jnp.bfloat16)
    return high, (a - high.astype(F32)).astype(jnp.bfloat16)


def dot(a, b, side):
    return lax.dot_general(a, b, (((1,), (side,)), ((), ())), preferred_element_type=F32)


def dot3(a, b, side):
    a_high, a_low = a
    b_high, b_low = b
    return dot(a_high, b_high, side) + (dot(a_high, b_low, side) + dot(a_low, b_high, side))


def times_t(a, b):
    return lax.dot_general(a, b, (((1,), (1,)), ((), ())), precision=HIGH, preferred_element_type=F32)


def all_bytes(ref, sem):
    return pltpu.make_async_copy(ref, ref, sem)


def main_kernel(
    NX, NY, NZ, NC,
    depth_hbm, gauss_hbm, keep_ref,
    out_ref, part_ref, gram_hbm, off_ref,
    depth, gauss, depth_t, load_sem,
    p_send, p_recv, aux_send, aux_recv, w_all,
    g_own, gx_recv, g_sum, gz_recv, g_piece, gy_recv, g_block, g_full, gram,
    own, c_send, c_recv, h_send, h_recv, x_send, x_recv, z_send, z_recv,
    send_sem, recv_sem, core_send_sem, core_recv_sem, h_send_sem, h_recv_sem,
):
    rows, cols = depth.shape
    K = gauss.shape[1]
    RY = rows // NY
    TS = cols // (NX * NZ * NC)
    XB = NZ * TS
    NU = NX * NC
    GX = 2 * K // NU
    GZ = GX // NZ

    s = lax.axis_index("samples")
    y = lax.axis_index("targets")
    core = lax.rem(s, NC)
    z = lax.rem(s // NC, NZ)
    x = s // (NC * NZ)
    u = x * NC + core

    def at_y(d):
        return (s, lax.rem(y + d, NY))

    def place(x1, z1, c1):
        return ((x1 * NZ + z1) * NC + c1, y)

    def at_u(d):
        u1 = lax.rem(u + d, NU)
        return place(u1 // NC, z, lax.rem(u1, NC))

    def at_z(d):
        return place(x, lax.rem(z + d, NZ), core)

    def at_x(d):
        return place(lax.rem(x + d, NX), z, core)

    def send(src, dst, phase, to):
        pltpu.make_async_remote_copy(
            src_ref=src, dst_ref=dst, send_sem=send_sem.at[phase], recv_sem=recv_sem.at[phase],
            device_id=to, device_id_type=MESH,
        ).start()

    y_order, u_order, z_order, x_order = far_first(NY), far_first(NU), far_first(NZ), far_first(NX)

    def row_block(y1):
        return pl.ds(pl.multiple_of(y1 * RY, 16), RY)

    gauss_load = pltpu.make_async_copy(gauss_hbm, gauss, load_sem.at[0])
    gauss_load.start()
    loads = []
    for i, d in enumerate(y_order + [0]):
        block = row_block(lax.rem(y + d, NY))
        load = pltpu.make_async_copy(depth_hbm.at[block], depth.at[block], load_sem.at[i + 1])
        load.start()
        loads.append(load)

    barrier = pltpu.get_barrier_semaphore()
    for d in y_order:
        pl.semaphore_signal(barrier, inc=1, device_id=at_y(d), device_id_type=MESH)
    for d in u_order:
        pl.semaphore_signal(barrier, inc=1, device_id=at_u(d), device_id_type=MESH)
    for d in z_order:
        pl.semaphore_signal(barrier, inc=1, device_id=at_z(d), device_id_type=MESH)
    pl.semaphore_wait(barrier, NY + NU + NZ - 3)

    kept = keep_ref[...].astype(F32).reshape(1, cols)
    count = jnp.sum(kept, axis=1, keepdims=True)
    sub = lax.broadcasted_iota(jnp.int32, (8, 128), 0)
    gauss_load.wait()

    raw_own = None
    for i, d in enumerate(y_order + [0]):
        block = row_block(lax.rem(y + d, NY))
        loads[i].wait()
        values = depth[block, :].astype(F32) * kept
        masked = values.astype(jnp.bfloat16)
        depth[block, :] = masked
        squares = values * values
        lanes = squares[:, 0:128]
        for j in range(1, cols // 128):
            lanes = lanes + squares[:, j * 128:(j + 1) * 128]
        raw = jnp.dot(masked, gauss[...], preferred_element_type=F32)
        q_row = jnp.sum(lanes.T, axis=0, keepdims=True)
        if RY < 128:
            q_row = jnp.concatenate([q_row, jnp.zeros((1, 128 - RY), F32)], axis=1)
        if d == 0:
            raw_own = raw
            peak = jnp.zeros((1, 1), F32)
        else:
            q_col = jnp.sum(lanes, axis=1, keepdims=True)
            level = raw * lax.rsqrt(jnp.maximum(q_col, 1e-30))
            peak = scale_code(whole_max(level))
            p_send[d] = to_fixed(level, peak)
        aux = jnp.where(sub == 0, q_row, jnp.where(sub == 1, peak, jnp.where(sub == 2, count, 0.0)))
        if d == 0:
            aux_recv[0] = aux
        else:
            aux_send[d] = aux
            send(aux_send.at[d], aux_recv.at[d], 0, at_y(d))
            send(p_send.at[d], p_recv.at[d], 1, at_y(d))

    def turn(j, _):
        at = pl.ds(pl.multiple_of(j * 128, 128), 128)
        depth_t[at, :] = depth[:, at].T
        return 0

    lax.fori_loop(0, cols // 128, turn, 0)

    others = pl.ds(1, NY - 1)
    all_bytes(aux_recv.at[others], recv_sem.at[0]).wait()
    all_bytes(p_recv.at[others], recv_sem.at[1]).wait()
    q_tile = aux_recv[:, 0, :]
    q_cols = q_tile.T[:RY]
    q_total = jnp.sum(q_cols, axis=1, keepdims=True)
    counts = aux_recv[0, 2:3, 0:1]
    for d in y_order:
        counts = counts + aux_recv[d, 2:3, 0:1]
    raw = raw_own
    for d in y_order:
        unit = jnp.exp2(aux_recv[d, 1:2, 0:1] * (1.0 / 256.0)) * (1.0 / 32767.0)
        root = jnp.sqrt(jnp.maximum(q_cols[:, d:d + 1], 1e-30)) * unit
        raw = raw + p_recv[d].astype(jnp.int32).astype(F32) * root
    scale = jnp.sqrt((q_total + 1.0) / (counts + 1.0))
    sketched = raw / scale
    weighted = (sketched / scale).astype(jnp.bfloat16)

    mine = row_block(y)
    w_all[mine, :] = weighted
    for d in y_order:
        send(w_all.at[mine], w_all.at[mine], 2, at_y(d))
    turned = sketched.T
    t_high, t_low = halves(turned)
    s_high, s_low = halves(sketched)
    own_gram = dot3((t_high, t_low), (s_high, s_low), 0)
    g_own[0:K, :] = own_gram[:, 0:128]
    g_own[K:2 * K, :] = own_gram[:, 128:256]
    for d in u_order:
        u1 = lax.rem(u + d, NU)
        send(g_own.at[pl.ds(pl.multiple_of(u1 * GX, 8), GX)], gx_recv.at[d], 3, at_u(d))
    all_bytes(gx_recv.at[pl.ds(1, NU - 1)], recv_sem.at[3]).wait()
    total = g_own[pl.ds(pl.multiple_of(u * GX, 8), GX), :]
    for d in u_order:
        total = total + gx_recv[d]
    g_sum[...] = total
    for d in z_order:
        z1 = lax.rem(z + d, NZ)
        send(g_sum.at[pl.ds(pl.multiple_of(z1 * GZ, 8), GZ)], gz_recv.at[d], 4, at_z(d))
    all_bytes(gz_recv.at[pl.ds(1, NZ - 1)], recv_sem.at[4]).wait()
    piece = g_sum[pl.ds(pl.multiple_of(z * GZ, 8), GZ), :]
    for d in z_order:
        piece = piece + gz_recv[d]
    g_piece[...] = piece
    for d in y_order:
        send(g_piece, gy_recv.at[d], 5, at_y(d))

    all_bytes(w_all.at[pl.ds(0, rows - RY)], recv_sem.at[2]).wait()
    c_copies = []
    for i, d in enumerate(x_order + [0]):
        x1 = lax.rem(x + d, NX)
        big = jnp.dot(
            depth_t[pl.ds(pl.multiple_of(x1 * (XB * NC), 16), XB * NC), :], w_all[...],
            preferred_element_type=F32,
        )
        even = jnp.concatenate([big[2 * j * TS:(2 * j + 1) * TS] for j in range(NZ)], axis=0)
        odd = jnp.concatenate([big[(2 * j + 1) * TS:(2 * j + 2) * TS] for j in range(NZ)], axis=0)
        keep_half = jnp.where(core == 0, even, odd)
        give_half = jnp.where(core == 0, odd, even)
        own[d] = keep_half
        code = scale_code(whole_max(give_half))
        c_send[d, 0:XB, :] = to_fixed(give_half, code)
        c_send[d, XB:XB + 16, :] = code_rows(code, K)
        copy = pltpu.make_async_remote_copy(
            src_ref=c_send.at[d], dst_ref=c_recv.at[d],
            send_sem=core_send_sem.at[d], recv_sem=core_recv_sem.at[d],
            device_id=place(x, z, 1 - core), device_id_type=MESH,
        )
        copy.start()
        c_copies.append(copy)

    all_bytes(gy_recv.at[others], recv_sem.at[5]).wait()
    piece = g_piece[...]
    for e in y_order:
        piece = piece + gy_recv[e]
    here = pl.ds(pl.multiple_of(z * GZ, 8), GZ)
    g_block[here, :] = piece
    for e in z_order:
        send(g_block.at[here], g_block.at[here], 6, at_z(e))

    right, left = 1, NX - 1
    H = XB // 2
    h_copies = []
    for i, d in enumerate(x_order + [0]):
        c_copies[i].wait()
        half = own[d] + from_fixed(c_recv[d], XB)
        if i > 0:
            own[d] = half
            continue
        code = scale_code(whole_max(half))
        fixed = to_fixed(half, code)
        for slot, to in ((0, right), (1, left)):
            h_send[slot, 0:H, :] = fixed[slot * H:(slot + 1) * H]
            h_send[slot, H:H + 16, :] = code_rows(code, K)
            copy = pltpu.make_async_remote_copy(
                src_ref=h_send.at[slot], dst_ref=h_recv.at[slot],
                send_sem=h_send_sem.at[slot], recv_sem=h_recv_sem.at[slot],
                device_id=at_x(to), device_id_type=MESH,
            )
            copy.start()
            h_copies.append(copy)

    all_bytes(g_block.at[pl.ds(0, GX - GZ)], recv_sem.at[6]).wait()
    there = pl.ds(pl.multiple_of(u * GX, 8), GX)
    g_full[there, :] = g_block[...]
    for d in u_order:
        send(g_block, g_full.at[there], 7, at_u(d))

    for slot, to in ((0, right), (1, left)):
        h_copies[slot].wait()
        mid = pl.ds(slot * H, H)
        own[to, mid, :] = own[to, mid, :] + from_fixed(h_recv[slot], H)
        half = own[to]
        code = scale_code(whole_max(half))
        x_send[slot, 0:XB, :] = to_fixed(half, code)
        x_send[slot, XB:XB + 16, :] = code_rows(code, K)
        send(x_send.at[slot], x_recv.at[slot], 8, at_x(to))
    all_bytes(x_recv, recv_sem.at[8]).wait()

    half = own[0] + from_fixed(x_recv[0], XB) + from_fixed(x_recv[1], XB)
    code = scale_code(whole_max(half))
    last = code_rows(code, 128)
    own[0] = half
    for d in z_order:
        z1 = lax.rem(z + d, NZ)
        v = own[0, pl.ds(pl.multiple_of(z1 * TS, 8), TS), :]
        v = jnp.concatenate([v[:, 0:128], v[:, 128:256]], axis=0)
        z_send[d, 0:2 * TS, :] = to_fixed(v, code)
        z_send[d, 2 * TS:2 * TS + 16, :] = last
        send(z_send.at[d], z_recv.at[d], 9, at_z(d))

    all_bytes(g_full.at[pl.ds(0, 2 * K - GX)], recv_sem.at[7]).wait()
    gram[:, 0:128] = g_full[0:K, :]
    gram[:, 128:256] = g_full[K:2 * K, :]
    gram_out = pltpu.make_async_copy(gram, gram_hbm, load_sem.at[0])
    gram_out.start()
    matrix = gram[...]
    eye = identity(K)
    diagonal = matrix * eye
    d_row = lax.rsqrt(jnp.sum(diagonal, axis=0, keepdims=True))
    d_col = lax.rsqrt(jnp.sum(diagonal, axis=1, keepdims=True))
    unit_gram = matrix * d_row * d_col
    unit_halves = halves(unit_gram)
    inverse = eye - half_lower(unit_gram - eye)
    rough = inverse.astype(jnp.bfloat16)
    error = dot(dot(rough, unit_halves[0], 0).astype(jnp.bfloat16), rough, 1) - eye
    inverse = inverse - dot(half_lower(error).astype(jnp.bfloat16), rough, 0)
    for _ in range(2):
        both = halves(inverse)
        error = dot3(halves(dot3(both, unit_halves, 0)), both, 1) - eye
        inverse = inverse - dot(half_lower(error).astype(jnp.bfloat16), both[0], 0)
    inverse = inverse * d_row
    off_ref[...] = jnp.broadcast_to(whole_max(error), (8, 128))
    both = halves(inverse)

    all_bytes(z_recv.at[pl.ds(1, NZ - 1)], recv_sem.at[9]).wait()
    v = own[0, pl.ds(pl.multiple_of(z * TS, 8), TS), :]
    v = jnp.concatenate([v[:, 0:128], v[:, 128:256]], axis=0)
    for d in z_order:
        v = v + from_fixed(z_recv[d], 2 * TS)
    part = jnp.concatenate([v[0:TS], v[TS:2 * TS]], axis=1)
    part_ref[...] = part
    out_ref[...] = dot3(halves(part), both, 1)
    gram_out.wait()

    all_bytes(aux_send.at[others], send_sem.at[0]).wait()
    all_bytes(p_send.at[others], send_sem.at[1]).wait()
    all_bytes(w_all.at[pl.ds(0, rows - RY)], send_sem.at[2]).wait()
    all_bytes(gx_recv.at[pl.ds(1, NU - 1)], send_sem.at[3]).wait()
    all_bytes(gz_recv.at[pl.ds(1, NZ - 1)], send_sem.at[4]).wait()
    all_bytes(gy_recv.at[others], send_sem.at[5]).wait()
    all_bytes(g_block.at[pl.ds(0, GX - GZ)], send_sem.at[6]).wait()
    all_bytes(g_full.at[pl.ds(0, 2 * K - GX)], send_sem.at[7]).wait()
    all_bytes(x_send, send_sem.at[8]).wait()
    all_bytes(z_send.at[pl.ds(1, NZ - 1)], send_sem.at[9]).wait()


def last_kernel(found_ref, off_ref, part_hbm, gram_hbm, out_ref, work, right, part, sem):
    K = work.shape[0]
    settled = jnp.max(off_ref[...]) < TOLERANCE
    out_ref[...] = found_ref[...]

    @pl.when(jnp.logical_not(settled))
    def _():
        load = pltpu.make_async_copy(gram_hbm, work, sem)
        load.start()
        load.wait()
        load = pltpu.make_async_copy(part_hbm, part, sem)
        load.start()
        load.wait()
        right[...] = identity(K)
        lane = lax.broadcasted_iota(jnp.int32, (1, K), 1)
        row = lax.broadcasted_iota(jnp.int32, (K, 1), 0)

        def step(k, _):
            m = work[...]
            top = work[pl.ds(k, 1), :]
            pivot = jnp.sum(jnp.where(lane == k, top, 0.0), axis=1, keepdims=True)
            column = jnp.sum(jnp.where(lane == k, m, 0.0), axis=1, keepdims=True)
            factor = jnp.where(row > k, column / pivot, 0.0)
            r = right[...]
            r_top = right[pl.ds(k, 1), :]
            work[...] = m - factor * top
            right[...] = r - factor * r_top
            return 0

        lax.fori_loop(0, K, step, 0)
        pivots = jnp.sum(work[...] * identity(K), axis=1, keepdims=True)
        out_ref[...] = times_t(part[...], right[...] / jnp.sqrt(pivots))


def solution(mesh, sizes=(4, 8, 8, 2)):
    NX, NY, NZ, NC = sizes

    def on_device(read_depth, gauss_sketch, keep_mask):
        rows, cols = read_depth.shape
        K = gauss_sketch.shape[1]
        RY = rows // NY
        TS = cols // (NX * NZ * NC)
        XB = NZ * TS
        NU = NX * NC
        GX = 2 * K // NU
        GZ = GX // NZ
        vmem = pl.BlockSpec(memory_space=pltpu.VMEM)
        hbm = pl.BlockSpec(memory_space=pl.ANY)
        i16 = jnp.int16
        found, part, gram, off = pl.pallas_call(
            functools.partial(main_kernel, NX, NY, NZ, NC),
            out_shape=(
                jax.ShapeDtypeStruct((TS, K), F32),
                jax.ShapeDtypeStruct((TS, K), F32),
                jax.ShapeDtypeStruct((K, K), F32),
                jax.ShapeDtypeStruct((8, 128), F32),
            ),
            in_specs=[hbm, hbm, vmem],
            out_specs=(vmem, vmem, hbm, vmem),
            scratch_shapes=[
                pltpu.VMEM((rows, cols), jnp.bfloat16),
                pltpu.VMEM((cols, K), jnp.bfloat16),
                pltpu.VMEM((cols, rows), jnp.bfloat16),
                pltpu.SemaphoreType.DMA((NY + 1,)),
                pltpu.VMEM((NY, RY, K), i16),
                pltpu.VMEM((NY, RY, K), i16),
                pltpu.VMEM((NY, 8, 128), F32),
                pltpu.VMEM((NY, 8, 128), F32),
                pltpu.VMEM((rows, K), jnp.bfloat16),
                pltpu.VMEM((2 * K, 128), F32),
                pltpu.VMEM((NU, GX, 128), F32),
                pltpu.VMEM((GX, 128), F32),
                pltpu.VMEM((NZ, GZ, 128), F32),
                pltpu.VMEM((GZ, 128), F32),
                pltpu.VMEM((NY, GZ, 128), F32),
                pltpu.VMEM((GX, 128), F32),
                pltpu.VMEM((2 * K, 128), F32),
                pltpu.VMEM((K, K), F32),
                pltpu.VMEM((NX, XB, K), F32),
                pltpu.VMEM((NX, XB + 16, K), i16),
                pltpu.VMEM((NX, XB + 16, K), i16),
                pltpu.VMEM((2, XB // 2 + 16, K), i16),
                pltpu.VMEM((2, XB // 2 + 16, K), i16),
                pltpu.VMEM((2, XB + 16, K), i16),
                pltpu.VMEM((2, XB + 16, K), i16),
                pltpu.VMEM((NZ, 2 * TS + 16, 128), i16),
                pltpu.VMEM((NZ, 2 * TS + 16, 128), i16),
                pltpu.SemaphoreType.DMA((10,)),
                pltpu.SemaphoreType.DMA((10,)),
                pltpu.SemaphoreType.DMA((NX,)),
                pltpu.SemaphoreType.DMA((NX,)),
                pltpu.SemaphoreType.DMA((2,)),
                pltpu.SemaphoreType.DMA((2,)),
            ],
            compiler_params=pltpu.CompilerParams(
                collective_id=0, has_side_effects=True, vmem_limit_bytes=60 << 20
            ),
        )(read_depth, gauss_sketch, keep_mask)
        return pl.pallas_call(
            last_kernel,
            out_shape=jax.ShapeDtypeStruct((TS, K), F32),
            in_specs=[vmem, vmem, hbm, hbm],
            out_specs=vmem,
            scratch_shapes=[
                pltpu.VMEM((K, K), F32),
                pltpu.VMEM((K, K), F32),
                pltpu.VMEM((TS, K), F32),
                pltpu.SemaphoreType.DMA,
            ],
            compiler_params=pltpu.CompilerParams(vmem_limit_bytes=60 << 20),
        )(found, off, part, gram)

    return jax.shard_map(
        on_device,
        mesh=mesh,
        in_specs=(P("samples", "targets"), P("targets", None), P("targets")),
        out_specs=P(("targets", "samples"), None),
        check_vma=False,
    )
```

```python
import functools

import jax
import jax.numpy as jnp
from jax import lax
from jax.experimental import pallas as pl
from jax.experimental.pallas import tpu as pltpu
from jax.sharding import PartitionSpec as P

MESH = pl.DeviceIdType.MESH
F32 = jnp.float32
HIGH = lax.Precision.HIGHEST
TOLERANCE = 2e-3
HALF = 128
AUX, SKETCH, ROWS, G_X, G_Z, G_Y, G_BACK_Z, G_BACK_X, G_BACK_C, SUM_X, SUM_Z, PHASES = 0, 1, 3, 5, 6, 7, 8, 9, 10, 11, 13, 15


def far_first(n):
    return sorted(range(1, n), key=lambda d: -min(d, n - d))


def whole_max(v):
    return jnp.max(jnp.max(jnp.abs(v), axis=0, keepdims=True), axis=1, keepdims=True)


def scale_code(peak):
    return jnp.ceil(jnp.log2(jnp.maximum(peak, 1e-30)) * 256.0) + 1.0


def to_fixed(v, code):
    unit = 32767.0 * jnp.exp2(code * (-1.0 / 256.0))
    return jnp.round(v * unit).astype(jnp.int32).astype(jnp.int16)


def code_rows(code, columns):
    return jnp.broadcast_to(code.astype(jnp.int32), (16, columns)).astype(jnp.int16)


def from_fixed(message, rows):
    values = message.astype(jnp.int32).astype(F32)
    unit = jnp.exp2(values[rows:rows + 1] * (1.0 / 256.0)) * (1.0 / 32767.0)
    return values[:rows] * unit


def half_lower(e):
    k = e.shape[0]
    row = lax.broadcasted_iota(jnp.int32, (k, k), 0)
    col = lax.broadcasted_iota(jnp.int32, (k, k), 1)
    return jnp.where(row > col, e, jnp.where(row == col, 0.5 * e, 0.0))


def identity(k):
    row = lax.broadcasted_iota(jnp.int32, (k, k), 0)
    col = lax.broadcasted_iota(jnp.int32, (k, k), 1)
    return jnp.where(row == col, 1.0, 0.0).astype(F32)


def halves(a):
    high = a.astype(jnp.bfloat16)
    return high, (a - high.astype(F32)).astype(jnp.bfloat16)


def dot(a, b, side):
    return lax.dot_general(a, b, (((1,), (side,)), ((), ())), preferred_element_type=F32)


def dot3(a, b, side):
    a_high, a_low = a
    b_high, b_low = b
    return dot(a_high, b_high, side) + (dot(a_high, b_low, side) + dot(a_low, b_high, side))


def times_t(a, b):
    return lax.dot_general(a, b, (((1,), (1,)), ((), ())), precision=HIGH, preferred_element_type=F32)


def all_bytes(ref, sem):
    return pltpu.make_async_copy(ref, ref, sem)


def main_kernel(
    NX, NY, NZ, NC,
    depth_hbm, gauss_hbm, keep_ref,
    out_ref, part_ref, gram_hbm, off_ref,
    depth, gauss, depth_t, load_sem,
    p_send, p_recv, aux_send, aux_recv, w_all,
    g_own, gx_recv, g_sum, gz_recv, g_piece, gy_recv, g_block, g_full, gram,
    own, c_send, c_recv, h_send, h_recv, x_send, x_recv, z_send, z_recv,
    send_sem, recv_sem, core_send_sem, core_recv_sem, h_send_sem, h_recv_sem,
):
    rows, cols = depth.shape
    K = gauss.shape[1]
    RY = rows // NY
    TS = cols // (NX * NZ * NC)
    XB = NZ * TS
    H = XB // 2
    NU = NX * NC
    GX = 2 * K // NU
    GZ = GX // NZ

    s = lax.axis_index("samples")
    y = lax.axis_index("targets")
    core = lax.rem(s, NC)
    z = lax.rem(s // NC, NZ)
    x = s // (NC * NZ)
    u = core * NX + x

    def at_y(d):
        return (s, lax.rem(y + d, NY))

    def place(x1, z1, c1):
        return ((x1 * NZ + z1) * NC + c1, y)

    def at_u(d):
        u1 = lax.rem(u + d, NU)
        return place(lax.rem(u1, NX), z, u1 // NX)

    def at_z(d):
        return place(x, lax.rem(z + d, NZ), core)

    def at_x(d):
        return place(lax.rem(x + d, NX), z, core)

    def at_core():
        return place(x, z, 1 - core)

    def send(src, dst, phase, to):
        pltpu.make_async_remote_copy(
            src_ref=src, dst_ref=dst, send_sem=send_sem.at[phase], recv_sem=recv_sem.at[phase],
            device_id=to, device_id_type=MESH,
        ).start()

    y_order, u_order, z_order, x_order = far_first(NY), far_first(NU), far_first(NZ), far_first(NX)
    others = pl.ds(1, NY - 1)

    def row_block(y1):
        return pl.ds(pl.multiple_of(y1 * RY, 16), RY)

    gauss_load = pltpu.make_async_copy(gauss_hbm, gauss, load_sem.at[0])
    gauss_load.start()
    loads = []
    for i, d in enumerate(y_order + [0]):
        block = row_block(lax.rem(y + d, NY))
        load = pltpu.make_async_copy(depth_hbm.at[block], depth.at[block], load_sem.at[i + 1])
        load.start()
        loads.append(load)

    barrier = pltpu.get_barrier_semaphore()
    for d in y_order:
        pl.semaphore_signal(barrier, inc=1, device_id=at_y(d), device_id_type=MESH)
    for d in u_order:
        pl.semaphore_signal(barrier, inc=1, device_id=at_u(d), device_id_type=MESH)
    for d in z_order:
        pl.semaphore_signal(barrier, inc=1, device_id=at_z(d), device_id_type=MESH)
    pl.semaphore_wait(barrier, NY + NU + NZ - 3)

    kept = keep_ref[...].astype(F32).reshape(1, cols)
    count = jnp.sum(kept, axis=1, keepdims=True)
    sub = lax.broadcasted_iota(jnp.int32, (8, 128), 0)
    gauss_load.wait()

    raw_own = None
    for i, d in enumerate(y_order + [0]):
        block = row_block(lax.rem(y + d, NY))
        loads[i].wait()
        values = depth[block, :].astype(F32) * kept
        masked = values.astype(jnp.bfloat16)
        depth[block, :] = masked
        squares = values * values
        lanes = squares[:, 0:128]
        for j in range(1, cols // 128):
            lanes = lanes + squares[:, j * 128:(j + 1) * 128]
        raw = jnp.dot(masked, gauss[...], preferred_element_type=F32)
        q_row = jnp.sum(lanes.T, axis=0, keepdims=True)
        if RY < 128:
            q_row = jnp.concatenate([q_row, jnp.zeros((1, 128 - RY), F32)], axis=1)
        if d == 0:
            raw_own = raw
            peak = jnp.zeros((1, 1), F32)
        else:
            q_col = jnp.sum(lanes, axis=1, keepdims=True)
            level = raw * lax.rsqrt(jnp.maximum(q_col, 1e-30))
            peak = scale_code(whole_max(level))
            fixed = to_fixed(level, peak)
            p_send[0, d] = fixed[:, :HALF]
            p_send[1, d] = fixed[:, HALF:]
        aux = jnp.where(sub == 0, q_row, jnp.where(sub == 1, peak, jnp.where(sub == 2, count, 0.0)))
        if d == 0:
            aux_recv[0] = aux
        else:
            aux_send[d] = aux
            send(aux_send.at[d], aux_recv.at[d], AUX, at_y(d))
            send(p_send.at[0, d], p_recv.at[0, d], SKETCH, at_y(d))
    for d in y_order:
        send(p_send.at[1, d], p_recv.at[1, d], SKETCH + 1, at_y(d))

    def turn(j, _):
        at = pl.ds(pl.multiple_of(j * 128, 128), 128)
        depth_t[at, :] = depth[:, at].T
        return 0

    lax.fori_loop(0, cols // 128, turn, 0)

    all_bytes(aux_recv.at[others], recv_sem.at[AUX]).wait()
    q_cols = aux_recv[:, 0, :].T[:RY]
    q_total = jnp.sum(q_cols, axis=1, keepdims=True)
    counts = aux_recv[0, 2:3, 0:1]
    for d in y_order:
        counts = counts + aux_recv[d, 2:3, 0:1]
    to_scaled = lax.rsqrt((q_total + 1.0) / (counts + 1.0))
    roots = {}
    for d in y_order:
        unit = jnp.exp2(aux_recv[d, 1:2, 0:1] * (1.0 / 256.0)) * (1.0 / 32767.0)
        roots[d] = jnp.sqrt(jnp.maximum(q_cols[:, d:d + 1], 1e-30)) * unit

    mine = row_block(y)
    sketched = []
    for h in range(2):
        all_bytes(p_recv.at[h, others], recv_sem.at[SKETCH + h]).wait()
        raw = raw_own[:, h * HALF:(h + 1) * HALF]
        for d in y_order:
            raw = raw + p_recv[h, d].astype(jnp.int32).astype(F32) * roots[d]
        scaled = raw * to_scaled
        sketched.append(scaled)
        w_all[h, mine, :] = (scaled * to_scaled).astype(jnp.bfloat16)
        for d in y_order:
            send(w_all.at[h, mine], w_all.at[h, mine], ROWS + h, at_y(d))

    sketched = jnp.concatenate(sketched, axis=1)
    own_gram = dot3(halves(sketched.T), halves(sketched), 0)
    g_own[0:K, :] = own_gram[:, :HALF]
    g_own[K:2 * K, :] = own_gram[:, HALF:]
    for d in u_order:
        u1 = lax.rem(u + d, NU)
        send(g_own.at[pl.ds(pl.multiple_of(u1 * GX, 8), GX)], gx_recv.at[d], G_X, at_u(d))
    all_bytes(gx_recv.at[pl.ds(1, NU - 1)], recv_sem.at[G_X]).wait()
    total = g_own[pl.ds(pl.multiple_of(u * GX, 8), GX), :]
    for d in u_order:
        total = total + gx_recv[d]
    g_sum[...] = total
    for d in z_order:
        z1 = lax.rem(z + d, NZ)
        send(g_sum.at[pl.ds(pl.multiple_of(z1 * GZ, 8), GZ)], gz_recv.at[d], G_Z, at_z(d))

    def gram_along_y():
        all_bytes(gz_recv.at[pl.ds(1, NZ - 1)], recv_sem.at[G_Z]).wait()
        piece = g_sum[pl.ds(pl.multiple_of(z * GZ, 8), GZ), :]
        for d in z_order:
            piece = piece + gz_recv[d]
        g_piece[...] = piece
        for d in y_order:
            send(g_piece, gy_recv.at[d], G_Y, at_y(d))

    def gram_back_along_z():
        all_bytes(gy_recv.at[others], recv_sem.at[G_Y]).wait()
        piece = g_piece[...]
        for d in y_order:
            piece = piece + gy_recv[d]
        here = pl.ds(pl.multiple_of(z * GZ, 8), GZ)
        g_block[here, :] = piece
        for d in z_order:
            send(g_block.at[here], g_block.at[here], G_BACK_Z, at_z(d))

    def gram_back_along_x():
        all_bytes(g_block.at[pl.ds(0, GX - GZ)], recv_sem.at[G_BACK_Z]).wait()
        there = pl.ds(pl.multiple_of(u * GX, 8), GX)
        g_full[there, :] = g_block[...]
        for d in x_order:
            send(g_block, g_full.at[there], G_BACK_X, at_x(d))

    side = pl.ds(pl.multiple_of(core * (NX * GX), 8), NX * GX)

    def gram_back_to_core():
        all_bytes(g_full.at[pl.ds(0, (NX - 1) * GX)], recv_sem.at[G_BACK_X]).wait()
        send(g_full.at[side], g_full.at[side], G_BACK_C, at_core())

    def core_copy(h, d):
        return pltpu.make_async_remote_copy(
            src_ref=c_send.at[h, d], dst_ref=c_recv.at[h, d],
            send_sem=core_send_sem.at[h, d], recv_sem=core_recv_sem.at[h, d],
            device_id=at_core(), device_id_type=MESH,
        )

    def back_project(h):
        all_bytes(w_all.at[h, pl.ds(0, rows - RY)], recv_sem.at[ROWS + h]).wait()
        for d in x_order + [0]:
            x1 = lax.rem(x + d, NX)
            big = jnp.dot(
                depth_t[pl.ds(pl.multiple_of(x1 * (XB * NC), 16), XB * NC), :], w_all[h],
                preferred_element_type=F32,
            )
            even = jnp.concatenate([big[2 * j * TS:(2 * j + 1) * TS] for j in range(NZ)], axis=0)
            odd = jnp.concatenate([big[(2 * j + 1) * TS:(2 * j + 2) * TS] for j in range(NZ)], axis=0)
            give = jnp.where(core == 0, odd, even)
            own[h, d] = jnp.where(core == 0, even, odd)
            code = scale_code(whole_max(give))
            c_send[h, d, 0:XB, :] = to_fixed(give, code)
            c_send[h, d, XB:XB + 16, :] = code_rows(code, HALF)
            core_copy(h, d).start()

    ways = ((0, 1), (1, NX - 1))

    def way_copy(h, slot, to):
        return pltpu.make_async_remote_copy(
            src_ref=h_send.at[h, slot], dst_ref=h_recv.at[h, slot],
            send_sem=h_send_sem.at[h, slot], recv_sem=h_recv_sem.at[h, slot],
            device_id=at_x(to), device_id_type=MESH,
        )

    def first_along_x(h):
        for i, d in enumerate(x_order + [0]):
            core_copy(h, d).wait()
            half = own[h, d] + from_fixed(c_recv[h, d], XB)
            if i > 0:
                own[h, d] = half
                continue
            code = scale_code(whole_max(half))
            fixed = to_fixed(half, code)
            for slot, to in ways:
                h_send[h, slot, 0:H, :] = fixed[slot * H:(slot + 1) * H]
                h_send[h, slot, H:H + 16, :] = code_rows(code, HALF)
                way_copy(h, slot, to).start()

    def second_along_x(h):
        for slot, to in ways:
            way_copy(h, slot, to).wait()
            mid = pl.ds(slot * H, H)
            own[h, to, mid, :] = own[h, to, mid, :] + from_fixed(h_recv[h, slot], H)
            half = own[h, to]
            code = scale_code(whole_max(half))
            x_send[h, slot, 0:XB, :] = to_fixed(half, code)
            x_send[h, slot, XB:XB + 16, :] = code_rows(code, HALF)
            send(x_send.at[h, slot], x_recv.at[h, slot], SUM_X + h, at_x(to))

    def along_z(h):
        all_bytes(x_recv.at[h], recv_sem.at[SUM_X + h]).wait()
        half = own[h, 0] + from_fixed(x_recv[h, 0], XB) + from_fixed(x_recv[h, 1], XB)
        code = scale_code(whole_max(half))
        unit = 32767.0 * jnp.exp2(code * (-1.0 / 256.0))
        tail = jnp.broadcast_to(code, (8, HALF))
        own[h, 0] = half
        for d in z_order:
            z1 = lax.rem(z + d, NZ)
            v = own[h, 0, pl.ds(pl.multiple_of(z1 * TS, 8), TS), :]
            v = jnp.concatenate([jnp.round(v * unit), tail], axis=0)
            z_send[h, d] = v.astype(jnp.int32).astype(jnp.int16)
            send(z_send.at[h, d], z_recv.at[h, d], SUM_Z + h, at_z(d))

    def total_along_z(h):
        all_bytes(z_recv.at[h, pl.ds(1, NZ - 1)], recv_sem.at[SUM_Z + h]).wait()
        v = own[h, 0, pl.ds(pl.multiple_of(z * TS, 8), TS), :]
        for d in z_order:
            v = v + from_fixed(z_recv[h, d], TS)
        return v

    gram_along_y()
    back_project(0)
    first_along_x(0)
    back_project(1)
    second_along_x(0)
    gram_back_along_z()
    first_along_x(1)
    gram_back_along_x()
    along_z(0)
    second_along_x(1)
    gram_back_to_core()
    along_z(1)

    all_bytes(g_full.at[pl.ds(0, NX * GX)], recv_sem.at[G_BACK_C]).wait()
    gram[:, 0:128] = g_full[0:K, :]
    gram[:, 128:256] = g_full[K:2 * K, :]
    gram_out = pltpu.make_async_copy(gram, gram_hbm, load_sem.at[0])
    gram_out.start()
    matrix = gram[...]
    eye = identity(K)
    diagonal = matrix * eye
    d_row = lax.rsqrt(jnp.sum(diagonal, axis=0, keepdims=True))
    d_col = lax.rsqrt(jnp.sum(diagonal, axis=1, keepdims=True))
    unit_gram = matrix * d_row * d_col
    unit_halves = halves(unit_gram)
    inverse = eye - half_lower(unit_gram - eye)
    rough = inverse.astype(jnp.bfloat16)
    error = dot(dot(rough, unit_halves[0], 0).astype(jnp.bfloat16), rough, 1) - eye
    inverse = inverse - dot(half_lower(error).astype(jnp.bfloat16), rough, 0)
    for _ in range(2):
        both = halves(inverse)
        error = dot3(halves(dot3(both, unit_halves, 0)), both, 1) - eye
        inverse = inverse - dot(half_lower(error).astype(jnp.bfloat16), both[0], 0)
    inverse = inverse * d_row
    off_ref[...] = jnp.broadcast_to(whole_max(error), (8, 128))
    both = halves(inverse)

    part = jnp.concatenate([total_along_z(0), total_along_z(1)], axis=1)
    part_ref[...] = part
    out_ref[...] = dot3(halves(part), both, 1)
    gram_out.wait()

    all_bytes(aux_send.at[others], send_sem.at[AUX]).wait()
    for h in range(2):
        all_bytes(p_send.at[h, others], send_sem.at[SKETCH + h]).wait()
        all_bytes(w_all.at[h, pl.ds(0, rows - RY)], send_sem.at[ROWS + h]).wait()
        all_bytes(x_send.at[h], send_sem.at[SUM_X + h]).wait()
        all_bytes(z_send.at[h, pl.ds(1, NZ - 1)], send_sem.at[SUM_Z + h]).wait()
    all_bytes(gx_recv.at[pl.ds(1, NU - 1)], send_sem.at[G_X]).wait()
    all_bytes(gz_recv.at[pl.ds(1, NZ - 1)], send_sem.at[G_Z]).wait()
    all_bytes(gy_recv.at[others], send_sem.at[G_Y]).wait()
    all_bytes(g_block.at[pl.ds(0, GX - GZ)], send_sem.at[G_BACK_Z]).wait()
    all_bytes(g_full.at[pl.ds(0, (NX - 1) * GX)], send_sem.at[G_BACK_X]).wait()
    all_bytes(g_full.at[side], send_sem.at[G_BACK_C]).wait()


def last_kernel(found_ref, off_ref, part_hbm, gram_hbm, out_ref, work, right, part, sem):
    K = work.shape[0]
    settled = jnp.max(off_ref[...]) < TOLERANCE
    out_ref[...] = found_ref[...]

    @pl.when(jnp.logical_not(settled))
    def _():
        load = pltpu.make_async_copy(gram_hbm, work, sem)
        load.start()
        load.wait()
        load = pltpu.make_async_copy(part_hbm, part, sem)
        load.start()
        load.wait()
        right[...] = identity(K)
        lane = lax.broadcasted_iota(jnp.int32, (1, K), 1)
        row = lax.broadcasted_iota(jnp.int32, (K, 1), 0)

        def step(k, _):
            m = work[...]
            top = work[pl.ds(k, 1), :]
            pivot = jnp.sum(jnp.where(lane == k, top, 0.0), axis=1, keepdims=True)
            column = jnp.sum(jnp.where(lane == k, m, 0.0), axis=1, keepdims=True)
            factor = jnp.where(row > k, column / pivot, 0.0)
            r = right[...]
            r_top = right[pl.ds(k, 1), :]
            work[...] = m - factor * top
            right[...] = r - factor * r_top
            return 0

        lax.fori_loop(0, K, step, 0)
        pivots = jnp.sum(work[...] * identity(K), axis=1, keepdims=True)
        out_ref[...] = times_t(part[...], right[...] / jnp.sqrt(pivots))


def solution(mesh, sizes=(4, 8, 8, 2)):
    NX, NY, NZ, NC = sizes

    def on_device(read_depth, gauss_sketch, keep_mask):
        rows, cols = read_depth.shape
        K = gauss_sketch.shape[1]
        RY = rows // NY
        TS = cols // (NX * NZ * NC)
        XB = NZ * TS
        NU = NX * NC
        GX = 2 * K // NU
        GZ = GX // NZ
        vmem = pl.BlockSpec(memory_space=pltpu.VMEM)
        hbm = pl.BlockSpec(memory_space=pl.ANY)
        i16 = jnp.int16
        found, part, gram, off = pl.pallas_call(
            functools.partial(main_kernel, NX, NY, NZ, NC),
            out_shape=(
                jax.ShapeDtypeStruct((TS, K), F32),
                jax.ShapeDtypeStruct((TS, K), F32),
                jax.ShapeDtypeStruct((K, K), F32),
                jax.ShapeDtypeStruct((8, 128), F32),
            ),
            in_specs=[hbm, hbm, vmem],
            out_specs=(vmem, vmem, hbm, vmem),
            scratch_shapes=[
                pltpu.VMEM((rows, cols), jnp.bfloat16),
                pltpu.VMEM((cols, K), jnp.bfloat16),
                pltpu.VMEM((cols, rows), jnp.bfloat16),
                pltpu.SemaphoreType.DMA((NY + 1,)),
                pltpu.VMEM((2, NY, RY, HALF), i16),
                pltpu.VMEM((2, NY, RY, HALF), i16),
                pltpu.VMEM((NY, 8, 128), F32),
                pltpu.VMEM((NY, 8, 128), F32),
                pltpu.VMEM((2, rows, HALF), jnp.bfloat16),
                pltpu.VMEM((2 * K, 128), F32),
                pltpu.VMEM((NU, GX, 128), F32),
                pltpu.VMEM((GX, 128), F32),
                pltpu.VMEM((NZ, GZ, 128), F32),
                pltpu.VMEM((GZ, 128), F32),
                pltpu.VMEM((NY, GZ, 128), F32),
                pltpu.VMEM((GX, 128), F32),
                pltpu.VMEM((2 * K, 128), F32),
                pltpu.VMEM((K, K), F32),
                pltpu.VMEM((2, NX, XB, HALF), F32),
                pltpu.VMEM((2, NX, XB + 16, HALF), i16),
                pltpu.VMEM((2, NX, XB + 16, HALF), i16),
                pltpu.VMEM((2, 2, XB // 2 + 16, HALF), i16),
                pltpu.VMEM((2, 2, XB // 2 + 16, HALF), i16),
                pltpu.VMEM((2, 2, XB + 16, HALF), i16),
                pltpu.VMEM((2, 2, XB + 16, HALF), i16),
                pltpu.VMEM((2, NZ, TS + 8, HALF), i16),
                pltpu.VMEM((2, NZ, TS + 8, HALF), i16),
                pltpu.SemaphoreType.DMA((PHASES,)),
                pltpu.SemaphoreType.DMA((PHASES,)),
                pltpu.SemaphoreType.DMA((2, NX)),
                pltpu.SemaphoreType.DMA((2, NX)),
                pltpu.SemaphoreType.DMA((2, 2)),
                pltpu.SemaphoreType.DMA((2, 2)),
            ],
            compiler_params=pltpu.CompilerParams(
                collective_id=0, has_side_effects=True, vmem_limit_bytes=60 << 20
            ),
        )(read_depth, gauss_sketch, keep_mask)
        return pl.pallas_call(
            last_kernel,
            out_shape=jax.ShapeDtypeStruct((TS, K), F32),
            in_specs=[vmem, vmem, hbm, hbm],
            out_specs=vmem,
            scratch_shapes=[
                pltpu.VMEM((K, K), F32),
                pltpu.VMEM((K, K), F32),
                pltpu.VMEM((TS, K), F32),
                pltpu.SemaphoreType.DMA,
            ],
            compiler_params=pltpu.CompilerParams(vmem_limit_bytes=60 << 20),
        )(found, off, part, gram)

    return jax.shard_map(
        on_device,
        mesh=mesh,
        in_specs=(P("samples", "targets"), P("targets", None), P("targets")),
        out_specs=P(("targets", "samples"), None),
        check_vma=False,
    )
```

```python
import functools

import jax
import jax.numpy as jnp
from jax import lax
from jax.experimental import pallas as pl
from jax.experimental.pallas import tpu as pltpu
from jax.sharding import PartitionSpec as P

MESH = pl.DeviceIdType.MESH
F32 = jnp.float32
HIGH = lax.Precision.HIGHEST
TOLERANCE = 2e-3
HALF = 128
AUX, SKETCH, ROWS, G_X, G_Z, G_Y, G_BACK_Z, G_BACK_X, G_BACK_C, SUM_X, SUM_Z, PHASES = 0, 1, 3, 5, 6, 7, 8, 9, 10, 11, 13, 15


def far_first(n):
    return sorted(range(1, n), key=lambda d: -min(d, n - d))


def whole_max(v):
    return jnp.max(jnp.max(jnp.abs(v), axis=0, keepdims=True), axis=1, keepdims=True)


def scale_code(peak):
    return jnp.ceil(jnp.log2(jnp.maximum(peak, 1e-30)) * 256.0) + 1.0


def to_fixed(v, code):
    unit = 32767.0 * jnp.exp2(code * (-1.0 / 256.0))
    return (v * unit).astype(jnp.int32).astype(jnp.int16)


def code_rows(code, columns):
    return jnp.broadcast_to(code.astype(jnp.int32), (16, columns)).astype(jnp.int16)


def from_fixed(message, rows):
    values = message.astype(jnp.int32).astype(F32)
    unit = jnp.exp2(values[rows:rows + 1] * (1.0 / 256.0)) * (1.0 / 32767.0)
    return values[:rows] * unit


def half_lower(e):
    k = e.shape[0]
    row = lax.broadcasted_iota(jnp.int32, (k, k), 0)
    col = lax.broadcasted_iota(jnp.int32, (k, k), 1)
    return jnp.where(row > col, e, jnp.where(row == col, 0.5 * e, 0.0))


def identity(k):
    row = lax.broadcasted_iota(jnp.int32, (k, k), 0)
    col = lax.broadcasted_iota(jnp.int32, (k, k), 1)
    return jnp.where(row == col, 1.0, 0.0).astype(F32)


def halves(a):
    high = a.astype(jnp.bfloat16)
    return high, (a - high.astype(F32)).astype(jnp.bfloat16)


def dot(a, b, side):
    return lax.dot_general(a, b, (((1,), (side,)), ((), ())), preferred_element_type=F32)


def dot3(a, b, side):
    a_high, a_low = a
    b_high, b_low = b
    return dot(a_high, b_high, side) + (dot(a_high, b_low, side) + dot(a_low, b_high, side))


def times_t(a, b):
    return lax.dot_general(a, b, (((1,), (1,)), ((), ())), precision=HIGH, preferred_element_type=F32)


def all_bytes(ref, sem):
    return pltpu.make_async_copy(ref, ref, sem)


def main_kernel(
    NX, NY, NZ, NC,
    depth_hbm, gauss_hbm, keep_ref,
    out_ref, part_ref, gram_hbm, off_ref,
    depth, gauss, keep_col, depth_t, load_sem,
    p_send, p_recv, aux_send, aux_recv, w_all,
    g_own, gx_recv, g_sum, gz_recv, g_piece, gy_recv, g_block, g_full, gram,
    terms, c_recv, own, h_send, h_recv, x_send, x_recv, z_send, z_recv,
    send_sem, recv_sem, core_send_sem, core_recv_sem, h_send_sem, h_recv_sem,
):
    rows, cols = depth.shape
    K = gauss.shape[1]
    RY = rows // NY
    TS = cols // (NX * NZ * NC)
    XB = NZ * TS
    H = XB // 2
    NU = NX * NC
    GX = 2 * K // NU
    GZ = GX // NZ

    s = lax.axis_index("samples")
    y = lax.axis_index("targets")
    core = lax.rem(s, NC)
    z = lax.rem(s // NC, NZ)
    x = s // (NC * NZ)
    u = core * NX + x

    def at_y(d):
        return (s, lax.rem(y + d, NY))

    def place(x1, z1, c1):
        return ((x1 * NZ + z1) * NC + c1, y)

    def at_u(d):
        u1 = lax.rem(u + d, NU)
        return place(lax.rem(u1, NX), z, u1 // NX)

    def at_z(d):
        return place(x, lax.rem(z + d, NZ), core)

    def at_x(d):
        return place(lax.rem(x + d, NX), z, core)

    def at_core():
        return place(x, z, 1 - core)

    def send(src, dst, phase, to):
        pltpu.make_async_remote_copy(
            src_ref=src, dst_ref=dst, send_sem=send_sem.at[phase], recv_sem=recv_sem.at[phase],
            device_id=to, device_id_type=MESH,
        ).start()

    y_order, u_order, z_order, x_order = far_first(NY), far_first(NU), far_first(NZ), far_first(NX)
    others = pl.ds(1, NY - 1)

    def row_block(y1):
        return pl.ds(pl.multiple_of(y1 * RY, 16), RY)

    order = y_order + [0]
    gauss_load = pltpu.make_async_copy(gauss_hbm, gauss, load_sem.at[0])
    gauss_load.start()
    loads = []
    for i, d in enumerate(order):
        load = pltpu.make_async_copy(
            depth_hbm.at[row_block(lax.rem(y + d, NY))], depth.at[pl.ds(i * RY, RY)], load_sem.at[i + 1]
        )
        load.start()
        loads.append(load)

    barrier = pltpu.get_barrier_semaphore()
    for d in y_order:
        pl.semaphore_signal(barrier, inc=1, device_id=at_y(d), device_id_type=MESH)
    for d in u_order:
        pl.semaphore_signal(barrier, inc=1, device_id=at_u(d), device_id_type=MESH)
    for d in z_order:
        pl.semaphore_signal(barrier, inc=1, device_id=at_z(d), device_id_type=MESH)

    kept = keep_ref[...].astype(F32).reshape(1, cols)
    count = jnp.sum(kept, axis=1, keepdims=True)
    sub = lax.broadcasted_iota(jnp.int32, (8, 128), 0)
    for j in range(cols // 128):
        tile = jnp.broadcast_to(kept[:, j * 128:(j + 1) * 128], (128, 128)).T
        keep_col[j * 128:(j + 1) * 128, :] = tile.astype(jnp.bfloat16)
    gauss_load.wait()
    for j in range(cols // 128):
        at = slice(j * 128, (j + 1) * 128)
        tile = keep_col[at, :]
        for h in range(2):
            gauss[at, h * HALF:(h + 1) * HALF] = gauss[at, h * HALF:(h + 1) * HALF] * tile

    raw_own = None
    group = NY // 2
    for g in range(2):
        for i in range(g * group, (g + 1) * group):
            loads[i].wait()
        values = depth[g * group * RY:(g + 1) * group * RY, :]
        raw = jnp.dot(values, gauss[...], preferred_element_type=F32)
        q = jnp.dot(values * values, keep_col[...], preferred_element_type=F32)
        invert = lax.rsqrt(jnp.maximum(q, 1e-30))
        level = [raw[:, h * HALF:(h + 1) * HALF] * invert for h in range(2)]
        peak = scale_code(jnp.maximum(whole_max(level[0]), whole_max(level[1])))
        fixed = [to_fixed(part, peak) for part in level]
        if g == 0:
            pl.semaphore_wait(barrier, NY + NU + NZ - 3)
        for i in range(g * group, (g + 1) * group):
            d = order[i]
            at = slice((i - g * group) * RY, (i - g * group + 1) * RY)
            q_row = q[at].T[0:1]
            if RY < 128:
                q_row = jnp.concatenate([q_row, jnp.zeros((1, 128 - RY), F32)], axis=1)
            aux = jnp.where(sub == 0, q_row, jnp.where(sub == 1, peak, jnp.where(sub == 2, count, 0.0)))
            if d == 0:
                raw_own = raw[at]
                aux_recv[0] = aux
            else:
                p_send[0, d] = fixed[0][at]
                p_send[1, d] = fixed[1][at]
                aux_send[d] = aux
                send(aux_send.at[d], aux_recv.at[d], AUX, at_y(d))
                send(p_send.at[0, d], p_recv.at[0, d], SKETCH, at_y(d))
    for d in y_order:
        send(p_send.at[1, d], p_recv.at[1, d], SKETCH + 1, at_y(d))

    def turn(j, _):
        at = pl.ds(pl.multiple_of(j * 128, 128), 128)
        tile = keep_col[at, :]
        depth_t[at, :] = depth[:, at].T * jnp.concatenate([tile] * (rows // 128), axis=1)
        return 0

    lax.fori_loop(0, cols // 128, turn, 0)

    all_bytes(aux_recv.at[others], recv_sem.at[AUX]).wait()
    q_cols = aux_recv[:, 0, :].T[:RY]
    q_total = jnp.sum(q_cols, axis=1, keepdims=True)
    counts = aux_recv[0, 2:3, 0:1]
    for d in y_order:
        counts = counts + aux_recv[d, 2:3, 0:1]
    to_scaled = lax.rsqrt((q_total + 1.0) / (counts + 1.0))
    roots = {}
    for d in y_order:
        unit = jnp.exp2(aux_recv[d, 1:2, 0:1] * (1.0 / 256.0)) * (1.0 / 32767.0)
        roots[d] = jnp.sqrt(jnp.maximum(q_cols[:, d:d + 1], 1e-30)) * unit

    sketched = []
    for h in range(2):
        all_bytes(p_recv.at[h, others], recv_sem.at[SKETCH + h]).wait()
        raw = raw_own[:, h * HALF:(h + 1) * HALF]
        for d in y_order:
            raw = raw + p_recv[h, d].astype(jnp.int32).astype(F32) * roots[d]
        scaled = raw * to_scaled
        sketched.append(scaled)
        w_all[h, NY - 1] = (scaled * to_scaled).astype(jnp.bfloat16)
        for d in y_order:
            send(w_all.at[h, NY - 1], w_all.at[h, order.index(NY - d)], ROWS + h, at_y(d))

    sketched = jnp.concatenate(sketched, axis=1)
    own_gram = dot3(halves(sketched.T), halves(sketched), 0)
    g_own[0:K, :] = own_gram[:, :HALF]
    g_own[K:2 * K, :] = own_gram[:, HALF:]
    for d in u_order:
        u1 = lax.rem(u + d, NU)
        send(g_own.at[pl.ds(pl.multiple_of(u1 * GX, 8), GX)], gx_recv.at[d], G_X, at_u(d))
    all_bytes(gx_recv.at[pl.ds(1, NU - 1)], recv_sem.at[G_X]).wait()
    total = g_own[pl.ds(pl.multiple_of(u * GX, 8), GX), :]
    for d in u_order:
        total = total + gx_recv[d]
    g_sum[...] = total
    for d in z_order:
        z1 = lax.rem(z + d, NZ)
        send(g_sum.at[pl.ds(pl.multiple_of(z1 * GZ, 8), GZ)], gz_recv.at[d], G_Z, at_z(d))

    def gram_along_y():
        all_bytes(gz_recv.at[pl.ds(1, NZ - 1)], recv_sem.at[G_Z]).wait()
        piece = g_sum[pl.ds(pl.multiple_of(z * GZ, 8), GZ), :]
        for d in z_order:
            piece = piece + gz_recv[d]
        g_piece[...] = piece
        for d in y_order:
            send(g_piece, gy_recv.at[d], G_Y, at_y(d))

    def gram_back_along_z():
        all_bytes(gy_recv.at[others], recv_sem.at[G_Y]).wait()
        piece = g_piece[...]
        for d in y_order:
            piece = piece + gy_recv[d]
        here = pl.ds(pl.multiple_of(z * GZ, 8), GZ)
        g_block[here, :] = piece
        for d in z_order:
            send(g_block.at[here], g_block.at[here], G_BACK_Z, at_z(d))

    def gram_back_along_x():
        all_bytes(g_block.at[pl.ds(0, GX - GZ)], recv_sem.at[G_BACK_Z]).wait()
        there = pl.ds(pl.multiple_of(u * GX, 8), GX)
        g_full[there, :] = g_block[...]
        for d in x_order:
            send(g_block, g_full.at[there], G_BACK_X, at_x(d))

    side = pl.ds(pl.multiple_of(core * (NX * GX), 8), NX * GX)

    def gram_back_to_core():
        all_bytes(g_full.at[pl.ds(0, (NX - 1) * GX)], recv_sem.at[G_BACK_X]).wait()
        send(g_full.at[side], g_full.at[side], G_BACK_C, at_core())

    def core_copy(h, d):
        return pltpu.make_async_remote_copy(
            src_ref=terms.at[h, d, :, 1 - core], dst_ref=c_recv.at[h, d],
            send_sem=core_send_sem.at[h, d], recv_sem=core_recv_sem.at[h, d],
            device_id=at_core(), device_id_type=MESH,
        )

    def back_project(h):
        all_bytes(w_all.at[h, pl.ds(0, NY - 1)], recv_sem.at[ROWS + h]).wait()
        weights = w_all[h].reshape(rows, HALF)
        for d in x_order + [0]:
            x1 = lax.rem(x + d, NX)
            block = depth_t[pl.ds(pl.multiple_of(x1 * (XB * NC), 16), XB * NC), :]
            product = jnp.dot(block, weights, preferred_element_type=F32)
            terms[h, d] = product.reshape(NZ, NC, TS, HALF)
            core_copy(h, d).start()

    ways = ((0, 1), (1, NX - 1))

    def way_copy(h, slot, to):
        return pltpu.make_async_remote_copy(
            src_ref=h_send.at[h, slot], dst_ref=h_recv.at[h, slot],
            send_sem=h_send_sem.at[h, slot], recv_sem=h_recv_sem.at[h, slot],
            device_id=at_x(to), device_id_type=MESH,
        )

    def first_along_x(h):
        for i, d in enumerate(x_order + [0]):
            core_copy(h, d).wait()
            half = (terms[h, d, :, core] + c_recv[h, d]).reshape(XB, HALF)
            if i > 0:
                own[h, d] = half
                continue
            code = scale_code(whole_max(half))
            fixed = to_fixed(half, code)
            for slot, to in ways:
                h_send[h, slot, 0:H, :] = fixed[slot * H:(slot + 1) * H]
                h_send[h, slot, H:H + 16, :] = code_rows(code, HALF)
                way_copy(h, slot, to).start()

    def second_along_x(h):
        for slot, to in ways:
            way_copy(h, slot, to).wait()
            mid = pl.ds(slot * H, H)
            own[h, to, mid, :] = own[h, to, mid, :] + from_fixed(h_recv[h, slot], H)
            half = own[h, to]
            code = scale_code(whole_max(half))
            x_send[h, slot, 0:XB, :] = to_fixed(half, code)
            x_send[h, slot, XB:XB + 16, :] = code_rows(code, HALF)
            send(x_send.at[h, slot], x_recv.at[h, slot], SUM_X + h, at_x(to))

    def along_z(h):
        all_bytes(x_recv.at[h], recv_sem.at[SUM_X + h]).wait()
        half = own[h, 0] + from_fixed(x_recv[h, 0], XB) + from_fixed(x_recv[h, 1], XB)
        code = scale_code(whole_max(half))
        unit = 32767.0 * jnp.exp2(code * (-1.0 / 256.0))
        tail = jnp.broadcast_to(code, (8, HALF))
        own[h, 0] = half
        for d in z_order:
            z1 = lax.rem(z + d, NZ)
            v = own[h, 0, pl.ds(pl.multiple_of(z1 * TS, 8), TS), :]
            v = jnp.concatenate([v * unit, tail], axis=0)
            z_send[h, d] = v.astype(jnp.int32).astype(jnp.int16)
            send(z_send.at[h, d], z_recv.at[h, d], SUM_Z + h, at_z(d))

    def total_along_z(h):
        all_bytes(z_recv.at[h, pl.ds(1, NZ - 1)], recv_sem.at[SUM_Z + h]).wait()
        v = own[h, 0, pl.ds(pl.multiple_of(z * TS, 8), TS), :]
        for d in z_order:
            v = v + from_fixed(z_recv[h, d], TS)
        return v

    gram_along_y()
    back_project(0)
    first_along_x(0)
    back_project(1)
    second_along_x(0)
    gram_back_along_z()
    first_along_x(1)
    gram_back_along_x()
    along_z(0)
    second_along_x(1)
    gram_back_to_core()
    along_z(1)

    all_bytes(g_full.at[pl.ds(0, NX * GX)], recv_sem.at[G_BACK_C]).wait()
    gram[:, 0:128] = g_full[0:K, :]
    gram[:, 128:256] = g_full[K:2 * K, :]
    gram_out = pltpu.make_async_copy(gram, gram_hbm, load_sem.at[0])
    gram_out.start()
    matrix = gram[...]
    eye = identity(K)
    diagonal = matrix * eye
    d_row = lax.rsqrt(jnp.sum(diagonal, axis=0, keepdims=True))
    d_col = lax.rsqrt(jnp.sum(diagonal, axis=1, keepdims=True))
    unit_gram = matrix * d_row * d_col
    unit_halves = halves(unit_gram)
    inverse = eye - half_lower(unit_gram - eye)
    rough = inverse.astype(jnp.bfloat16)
    error = dot(dot(rough, unit_halves[0], 0).astype(jnp.bfloat16), rough, 1) - eye
    inverse = inverse - dot(half_lower(error).astype(jnp.bfloat16), rough, 0)
    for _ in range(2):
        both = halves(inverse)
        error = dot3(halves(dot3(both, unit_halves, 0)), both, 1) - eye
        inverse = inverse - dot(half_lower(error).astype(jnp.bfloat16), both[0], 0)
    inverse = inverse * d_row
    off_ref[...] = jnp.broadcast_to(whole_max(error), (8, 128))
    both = halves(inverse)

    part = jnp.concatenate([total_along_z(0), total_along_z(1)], axis=1)
    part_ref[...] = part
    out_ref[...] = dot3(halves(part), both, 1)
    gram_out.wait()

    all_bytes(aux_send.at[others], send_sem.at[AUX]).wait()
    for h in range(2):
        all_bytes(p_send.at[h, others], send_sem.at[SKETCH + h]).wait()
        all_bytes(w_all.at[h, pl.ds(0, NY - 1)], send_sem.at[ROWS + h]).wait()
        all_bytes(x_send.at[h], send_sem.at[SUM_X + h]).wait()
        all_bytes(z_send.at[h, pl.ds(1, NZ - 1)], send_sem.at[SUM_Z + h]).wait()
    all_bytes(gx_recv.at[pl.ds(1, NU - 1)], send_sem.at[G_X]).wait()
    all_bytes(gz_recv.at[pl.ds(1, NZ - 1)], send_sem.at[G_Z]).wait()
    all_bytes(gy_recv.at[others], send_sem.at[G_Y]).wait()
    all_bytes(g_block.at[pl.ds(0, GX - GZ)], send_sem.at[G_BACK_Z]).wait()
    all_bytes(g_full.at[pl.ds(0, (NX - 1) * GX)], send_sem.at[G_BACK_X]).wait()
    all_bytes(g_full.at[side], send_sem.at[G_BACK_C]).wait()


def last_kernel(found_ref, off_ref, part_hbm, gram_hbm, out_ref, work, right, part, sem):
    K = work.shape[0]
    settled = jnp.max(off_ref[...]) < TOLERANCE
    out_ref[...] = found_ref[...]

    @pl.when(jnp.logical_not(settled))
    def _():
        load = pltpu.make_async_copy(gram_hbm, work, sem)
        load.start()
        load.wait()
        load = pltpu.make_async_copy(part_hbm, part, sem)
        load.start()
        load.wait()
        right[...] = identity(K)
        lane = lax.broadcasted_iota(jnp.int32, (1, K), 1)
        row = lax.broadcasted_iota(jnp.int32, (K, 1), 0)

        def step(k, _):
            m = work[...]
            top = work[pl.ds(k, 1), :]
            pivot = jnp.sum(jnp.where(lane == k, top, 0.0), axis=1, keepdims=True)
            column = jnp.sum(jnp.where(lane == k, m, 0.0), axis=1, keepdims=True)
            factor = jnp.where(row > k, column / pivot, 0.0)
            r = right[...]
            r_top = right[pl.ds(k, 1), :]
            work[...] = m - factor * top
            right[...] = r - factor * r_top
            return 0

        lax.fori_loop(0, K, step, 0)
        pivots = jnp.sum(work[...] * identity(K), axis=1, keepdims=True)
        out_ref[...] = times_t(part[...], right[...] / jnp.sqrt(pivots))


def solution(mesh, sizes=(4, 8, 8, 2)):
    NX, NY, NZ, NC = sizes

    def on_device(read_depth, gauss_sketch, keep_mask):
        rows, cols = read_depth.shape
        K = gauss_sketch.shape[1]
        RY = rows // NY
        TS = cols // (NX * NZ * NC)
        XB = NZ * TS
        NU = NX * NC
        GX = 2 * K // NU
        GZ = GX // NZ
        vmem = pl.BlockSpec(memory_space=pltpu.VMEM)
        hbm = pl.BlockSpec(memory_space=pl.ANY)
        i16 = jnp.int16
        found, part, gram, off = pl.pallas_call(
            functools.partial(main_kernel, NX, NY, NZ, NC),
            out_shape=(
                jax.ShapeDtypeStruct((TS, K), F32),
                jax.ShapeDtypeStruct((TS, K), F32),
                jax.ShapeDtypeStruct((K, K), F32),
                jax.ShapeDtypeStruct((8, 128), F32),
            ),
            in_specs=[hbm, hbm, vmem],
            out_specs=(vmem, vmem, hbm, vmem),
            scratch_shapes=[
                pltpu.VMEM((rows, cols), jnp.bfloat16),
                pltpu.VMEM((cols, K), jnp.bfloat16),
                pltpu.VMEM((cols, 128), jnp.bfloat16),
                pltpu.VMEM((cols, rows), jnp.bfloat16),
                pltpu.SemaphoreType.DMA((NY + 1,)),
                pltpu.VMEM((2, NY, RY, HALF), i16),
                pltpu.VMEM((2, NY, RY, HALF), i16),
                pltpu.VMEM((NY, 8, 128), F32),
                pltpu.VMEM((NY, 8, 128), F32),
                pltpu.VMEM((2, NY, RY, HALF), jnp.bfloat16),
                pltpu.VMEM((2 * K, 128), F32),
                pltpu.VMEM((NU, GX, 128), F32),
                pltpu.VMEM((GX, 128), F32),
                pltpu.VMEM((NZ, GZ, 128), F32),
                pltpu.VMEM((GZ, 128), F32),
                pltpu.VMEM((NY, GZ, 128), F32),
                pltpu.VMEM((GX, 128), F32),
                pltpu.VMEM((2 * K, 128), F32),
                pltpu.VMEM((K, K), F32),
                pltpu.VMEM((2, NX, NZ, NC, TS, HALF), F32),
                pltpu.VMEM((2, NX, NZ, TS, HALF), F32),
                pltpu.VMEM((2, NX, XB, HALF), F32),
                pltpu.VMEM((2, 2, XB // 2 + 16, HALF), i16),
                pltpu.VMEM((2, 2, XB // 2 + 16, HALF), i16),
                pltpu.VMEM((2, 2, XB + 16, HALF), i16),
                pltpu.VMEM((2, 2, XB + 16, HALF), i16),
                pltpu.VMEM((2, NZ, TS + 8, HALF), i16),
                pltpu.VMEM((2, NZ, TS + 8, HALF), i16),
                pltpu.SemaphoreType.DMA((PHASES,)),
                pltpu.SemaphoreType.DMA((PHASES,)),
                pltpu.SemaphoreType.DMA((2, NX)),
                pltpu.SemaphoreType.DMA((2, NX)),
                pltpu.SemaphoreType.DMA((2, 2)),
                pltpu.SemaphoreType.DMA((2, 2)),
            ],
            compiler_params=pltpu.CompilerParams(
                collective_id=0, has_side_effects=True, vmem_limit_bytes=60 << 20
            ),
        )(read_depth, gauss_sketch, keep_mask)
        return pl.pallas_call(
            last_kernel,
            out_shape=jax.ShapeDtypeStruct((TS, K), F32),
            in_specs=[vmem, vmem, hbm, hbm],
            out_specs=vmem,
            scratch_shapes=[
                pltpu.VMEM((K, K), F32),
                pltpu.VMEM((K, K), F32),
                pltpu.VMEM((TS, K), F32),
                pltpu.SemaphoreType.DMA,
            ],
            compiler_params=pltpu.CompilerParams(vmem_limit_bytes=60 << 20),
        )(found, off, part, gram)

    return jax.shard_map(
        on_device,
        mesh=mesh,
        in_specs=(P("samples", "targets"), P("targets", None), P("targets")),
        out_specs=P(("targets", "samples"), None),
        check_vma=False,
    )
```

```python
import functools

import jax
import jax.numpy as jnp
from jax import lax
from jax.experimental import pallas as pl
from jax.experimental.pallas import tpu as pltpu
from jax.sharding import PartitionSpec as P

MESH = pl.DeviceIdType.MESH
F32 = jnp.float32
HIGH = lax.Precision.HIGHEST
TOLERANCE = 2e-3
HALF = 128
AUX_FAR, SKETCH_FAR, AUX, SKETCH, G_X, G_Z, G_Y, G_BACK_Z, G_BACK_X, G_BACK_C = 0, 1, 2, 3, 5, 6, 7, 8, 9, 10
SUM_X, SUM_Z, ROWS_NEAR, ROWS_UP, ROWS_DOWN, ROWS_FAR, PHASES = 11, 13, 15, 17, 19, 21, 23
CUT = 48


def far_first(n):
    return sorted(range(1, n), key=lambda d: -min(d, n - d))


def whole_max(v):
    return jnp.max(jnp.max(jnp.abs(v), axis=0, keepdims=True), axis=1, keepdims=True)


def scale_code(peak):
    return jnp.ceil(jnp.log2(jnp.maximum(peak, 1e-30)) * 256.0) + 1.0


def to_fixed(v, code):
    unit = 32767.0 * jnp.exp2(code * (-1.0 / 256.0))
    return (v * unit).astype(jnp.int32).astype(jnp.int16)


def code_rows(code, columns):
    return jnp.broadcast_to(code.astype(jnp.int32), (16, columns)).astype(jnp.int16)


def from_fixed(message, rows):
    values = message.astype(jnp.int32).astype(F32)
    unit = jnp.exp2(values[rows:rows + 1] * (1.0 / 256.0)) * (1.0 / 32767.0)
    return values[:rows] * unit


def half_lower(e):
    k = e.shape[0]
    row = lax.broadcasted_iota(jnp.int32, (k, k), 0)
    col = lax.broadcasted_iota(jnp.int32, (k, k), 1)
    return jnp.where(row > col, e, jnp.where(row == col, 0.5 * e, 0.0))


def identity(k):
    row = lax.broadcasted_iota(jnp.int32, (k, k), 0)
    col = lax.broadcasted_iota(jnp.int32, (k, k), 1)
    return jnp.where(row == col, 1.0, 0.0).astype(F32)


def halves(a):
    high = a.astype(jnp.bfloat16)
    return high, (a - high.astype(F32)).astype(jnp.bfloat16)


def dot(a, b, side):
    return lax.dot_general(a, b, (((1,), (side,)), ((), ())), preferred_element_type=F32)


def dot3(a, b, side):
    a_high, a_low = a
    b_high, b_low = b
    return dot(a_high, b_high, side) + (dot(a_high, b_low, side) + dot(a_low, b_high, side))


def times_t(a, b):
    return lax.dot_general(a, b, (((1,), (1,)), ((), ())), precision=HIGH, preferred_element_type=F32)


def all_bytes(ref, sem):
    return pltpu.make_async_copy(ref, ref, sem)


def main_kernel(
    NX, NY, NZ, NC,
    depth_hbm, gauss_hbm, keep_ref,
    out_ref, part_ref, gram_hbm, off_ref,
    depth, gauss, keep_col, depth_t, load_sem,
    f_send, f_recv, fx_send, fx_recv, p_send, p_recv, aux_send, aux_recv, w_all,
    g_own, gx_recv, g_sum, gz_recv, g_piece, gy_recv, g_block, g_full, gram,
    terms, c_recv, own, h_send, h_recv, x_send, x_recv, z_send, z_recv,
    send_sem, recv_sem, core_send_sem, core_recv_sem, h_send_sem, h_recv_sem,
):
    rows, cols = depth.shape
    K = gauss.shape[1]
    RY = rows // NY
    TS = cols // (NX * NZ * NC)
    XB = NZ * TS
    H = XB // 2
    NU = NX * NC
    GX = 2 * K // NU
    GZ = GX // NZ

    s = lax.axis_index("samples")
    y = lax.axis_index("targets")
    core = lax.rem(s, NC)
    z = lax.rem(s // NC, NZ)
    x = s // (NC * NZ)
    u = core * NX + x

    def at_y(d):
        return (s, lax.rem(y + d, NY))

    def place(x1, z1, c1):
        return ((x1 * NZ + z1) * NC + c1, y)

    def at_u(d):
        u1 = lax.rem(u + d, NU)
        return place(lax.rem(u1, NX), z, u1 // NX)

    def at_z(d):
        return place(x, lax.rem(z + d, NZ), core)

    def at_x(d):
        return place(lax.rem(x + d, NX), z, core)

    def at_core():
        return place(x, z, 1 - core)

    def send(src, dst, phase, to):
        pltpu.make_async_remote_copy(
            src_ref=src, dst_ref=dst, send_sem=send_sem.at[phase], recv_sem=recv_sem.at[phase],
            device_id=to, device_id_type=MESH,
        ).start()

    y_order, u_order, z_order, x_order = far_first(NY), far_first(NU), far_first(NZ), far_first(NX)
    others = pl.ds(1, NY - 1)

    def row_block(y1):
        return pl.ds(pl.multiple_of(y1 * RY, 16), RY)

    order = y_order + [0]
    gauss_load = pltpu.make_async_copy(gauss_hbm, gauss, load_sem.at[0])
    gauss_load.start()
    loads = []
    for i, d in enumerate(order):
        load = pltpu.make_async_copy(
            depth_hbm.at[row_block(lax.rem(y + d, NY))], depth.at[pl.ds(i * RY, RY)], load_sem.at[i + 1]
        )
        load.start()
        loads.append(load)

    barrier = pltpu.get_barrier_semaphore()
    for d in y_order:
        pl.semaphore_signal(barrier, inc=1, device_id=at_y(d), device_id_type=MESH)
    for d in u_order:
        pl.semaphore_signal(barrier, inc=1, device_id=at_u(d), device_id_type=MESH)
    for d in z_order:
        pl.semaphore_signal(barrier, inc=1, device_id=at_z(d), device_id_type=MESH)

    kept = keep_ref[...].astype(F32).reshape(1, cols)
    count = jnp.sum(kept, axis=1, keepdims=True)
    sub = lax.broadcasted_iota(jnp.int32, (8, 128), 0)
    for j in range(cols // 128):
        tile = jnp.broadcast_to(kept[:, j * 128:(j + 1) * 128], (128, 128)).T
        keep_col[j * 128:(j + 1) * 128, :] = tile.astype(jnp.bfloat16)
    gauss_load.wait()
    for j in range(cols // 128):
        at = slice(j * 128, (j + 1) * 128)
        tile = keep_col[at, :]
        for h in range(2):
            gauss[at, h * HALF:(h + 1) * HALF] = gauss[at, h * HALF:(h + 1) * HALF] * tile

    def aux_of(q_row, code, number):
        return jnp.where(sub == 0, q_row, jnp.where(sub == 1, code, jnp.where(sub == 2, number, 0.0)))

    def row_of(q):
        row = q.T[0:1]
        if RY < 128:
            row = jnp.concatenate([row, jnp.zeros((1, 128 - RY), F32)], axis=1)
        return row

    def unit_of(aux):
        return jnp.exp2(aux[1:2, 0:1] * (1.0 / 256.0)) * (1.0 / 32767.0)

    def columns_of(tiles):
        tile = jnp.concatenate([t[0:1] for t in tiles] + [jnp.zeros((8 - len(tiles), 128), F32)], axis=0)
        turned = tile.T[:RY]
        return [turned[:, i:i + 1] for i in range(len(tiles))]

    def safe_root(q):
        return jnp.sqrt(jnp.maximum(q, 1e-30))

    def turn(j, _):
        at = pl.ds(pl.multiple_of(j * 128, 128), 128)
        tile = keep_col[at, :]
        depth_t[at, :] = depth[:, at].T * jnp.concatenate([tile] * (rows // 128), axis=1)
        return 0

    group = NY // 2
    raws, q_rows, q_cols = {}, {}, {}
    for g in range(2):
        for i in range(g * group, (g + 1) * group):
            loads[i].wait()
        values = depth[g * group * RY:(g + 1) * group * RY, :]
        raw = jnp.dot(values, gauss[...], preferred_element_type=F32)
        q = jnp.dot(values * values, keep_col[...], preferred_element_type=F32)
        for i in range(group):
            d = order[g * group + i]
            at = slice(i * RY, (i + 1) * RY)
            raws[d], q_rows[d], q_cols[d] = raw[at], row_of(q[at]), q[at, 0:1]
        some = slice(0, 3 * RY) if g == 0 else slice(RY, 3 * RY)
        invert = lax.rsqrt(jnp.maximum(q[some], 1e-30))
        level = [raw[some, h * HALF:(h + 1) * HALF] * invert for h in range(2)]
        code = scale_code(jnp.maximum(whole_max(level[0]), whole_max(level[1])))
        fixed = [to_fixed(part, code) for part in level]
        if g == 0:
            for i, d in enumerate((4, 3, 5)):
                for h in range(2):
                    f_send[i, :, h * HALF:(h + 1) * HALF] = fixed[h][i * RY:(i + 1) * RY]
                fx_send[i] = aux_of(q_rows[d], code, count)
            pl.semaphore_wait(barrier, NY + NU + NZ - 3)
            upper, lower = pl.ds(0, CUT), pl.ds(CUT, RY - CUT)
            send(fx_send.at[0], fx_recv.at[2], AUX_FAR, at_y(2))
            send(fx_send.at[0], fx_recv.at[3], AUX_FAR, at_y(NY - 2))
            send(f_send.at[0, upper], f_recv.at[2, upper], SKETCH_FAR, at_y(2))
            send(f_send.at[0, lower], f_recv.at[2, lower], SKETCH_FAR, at_y(NY - 2))
            for i, to in ((1, 1), (2, NY - 1)):
                send(fx_send.at[i], fx_recv.at[i - 1], AUX_FAR, at_y(to))
                send(f_send.at[i], f_recv.at[i - 1], SKETCH_FAR, at_y(to))
        else:
            for i, d in enumerate((1, NY - 1)):
                for h in range(2):
                    p_send[h, i] = fixed[h][i * RY:(i + 1) * RY]
                aux_send[i] = aux_of(q_rows[d], code, count)
                send(aux_send.at[i], aux_recv.at[i], AUX, at_y(d))
                for h in range(2):
                    send(p_send.at[h, i], p_recv.at[h, i], SKETCH + h, at_y(d))

    tiles = cols // 128
    lax.fori_loop(0, tiles // 2, turn, 0)

    all_bytes(fx_recv, recv_sem.at[AUX_FAR]).wait()
    all_bytes(f_recv, recv_sem.at[SKETCH_FAR]).wait()
    lane = lax.broadcasted_iota(jnp.int32, (1, 128), 1)
    far = [fx_recv[i] for i in range(4)]
    far_cols = columns_of(far)
    far_unit = [unit_of(t) for t in far]
    last = f_recv[2].astype(jnp.int32).astype(F32)
    row = lax.broadcasted_iota(jnp.int32, (RY, 1), 0)
    for i, d in ((0, 2), (1, NY - 2)):
        part = (row < CUT) if i == 0 else (row >= CUT)
        q_part = (lane < CUT) if i == 0 else (lane >= CUT)
        total = raws[d] + f_recv[i].astype(jnp.int32).astype(F32) * (safe_root(far_cols[i]) * far_unit[i])
        total = total + last * jnp.where(part, safe_root(far_cols[2 + i]) * far_unit[2 + i], 0.0)
        q_col = q_cols[d] + far_cols[i] + jnp.where(part, far_cols[2 + i], 0.0)
        q_row = q_rows[d] + far[i][0:1] + jnp.where(q_part, far[2 + i][0:1], 0.0)
        number = count + far[i][2:3, 0:1]
        if i == 0:
            number = number + far[2][2:3, 0:1]
        level = total * lax.rsqrt(jnp.maximum(q_col, 1e-30))
        code = scale_code(whole_max(level))
        fixed = to_fixed(level, code)
        aux_send[2 + i] = aux_of(q_row, code, number)
        send(aux_send.at[2 + i], aux_recv.at[2 + i], AUX, at_y(d))
        for h in range(2):
            p_send[h, 2 + i] = fixed[:, h * HALF:(h + 1) * HALF]
        send(p_send.at[0, 2 + i], p_recv.at[0, 2 + i], SKETCH, at_y(d))
    for i, d in ((0, 2), (1, NY - 2)):
        send(p_send.at[1, 2 + i], p_recv.at[1, 2 + i], SKETCH + 1, at_y(d))

    lax.fori_loop(tiles // 2, 3 * tiles // 4, turn, 0)

    all_bytes(aux_recv, recv_sem.at[AUX]).wait()
    near = [aux_recv[i] for i in range(4)]
    near_cols = columns_of(near)
    q_total, counts = q_cols[0], count
    for i in range(4):
        q_total = q_total + near_cols[i]
        counts = counts + near[i][2:3, 0:1]
    to_scaled = lax.rsqrt((q_total + 1.0) / (counts + 1.0))
    roots = [safe_root(near_cols[i]) * unit_of(near[i]) for i in range(4)]

    def slot(d):
        return order.index(d % NY)

    sketched = []
    for h in range(2):
        all_bytes(p_recv.at[h], recv_sem.at[SKETCH + h]).wait()
        raw = raws[0][:, h * HALF:(h + 1) * HALF]
        for i in range(4):
            raw = raw + p_recv[h, i].astype(jnp.int32).astype(F32) * roots[i]
        scaled = raw * to_scaled
        sketched.append(scaled)
        w_all[h, slot(0)] = (scaled * to_scaled).astype(jnp.bfloat16)
        for d, phase in ((2, ROWS_UP), (NY - 2, ROWS_DOWN), (1, ROWS_NEAR), (NY - 1, ROWS_NEAR)):
            send(w_all.at[h, slot(0)], w_all.at[h, slot(-d)], phase + h, at_y(d))

    def pass_on(h):
        for phase, back, part in ((ROWS_UP, -2, pl.ds(0, CUT)), (ROWS_DOWN, 2, pl.ds(CUT, RY - CUT))):
            ahead = -back // 2
            held = w_all.at[h, slot(back)]
            all_bytes(held, recv_sem.at[phase + h]).wait()
            send(held.at[part], w_all.at[h, slot(2 * back), part], ROWS_FAR + h, at_y((2 * ahead) % NY))
            send(held, w_all.at[h, slot(back - ahead)], ROWS_FAR + h, at_y(ahead % NY))

    sketched = jnp.concatenate(sketched, axis=1)
    own_gram = dot3(halves(sketched.T), halves(sketched), 0)
    g_own[0:K, :] = own_gram[:, :HALF]
    g_own[K:2 * K, :] = own_gram[:, HALF:]
    for d in u_order:
        u1 = lax.rem(u + d, NU)
        send(g_own.at[pl.ds(pl.multiple_of(u1 * GX, 8), GX)], gx_recv.at[d], G_X, at_u(d))
    lax.fori_loop(3 * tiles // 4, tiles, turn, 0)
    pass_on(0)
    all_bytes(gx_recv.at[pl.ds(1, NU - 1)], recv_sem.at[G_X]).wait()
    total = g_own[pl.ds(pl.multiple_of(u * GX, 8), GX), :]
    for d in u_order:
        total = total + gx_recv[d]
    g_sum[...] = total
    for d in z_order:
        z1 = lax.rem(z + d, NZ)
        send(g_sum.at[pl.ds(pl.multiple_of(z1 * GZ, 8), GZ)], gz_recv.at[d], G_Z, at_z(d))

    def gram_along_y():
        all_bytes(gz_recv.at[pl.ds(1, NZ - 1)], recv_sem.at[G_Z]).wait()
        piece = g_sum[pl.ds(pl.multiple_of(z * GZ, 8), GZ), :]
        for d in z_order:
            piece = piece + gz_recv[d]
        g_piece[...] = piece
        for d in y_order:
            send(g_piece, gy_recv.at[d], G_Y, at_y(d))

    def gram_back_along_z():
        all_bytes(gy_recv.at[others], recv_sem.at[G_Y]).wait()
        piece = g_piece[...]
        for d in y_order:
            piece = piece + gy_recv[d]
        here = pl.ds(pl.multiple_of(z * GZ, 8), GZ)
        g_block[here, :] = piece
        for d in z_order:
            send(g_block.at[here], g_block.at[here], G_BACK_Z, at_z(d))

    def gram_back_along_x():
        all_bytes(g_block.at[pl.ds(0, GX - GZ)], recv_sem.at[G_BACK_Z]).wait()
        there = pl.ds(pl.multiple_of(u * GX, 8), GX)
        g_full[there, :] = g_block[...]
        for d in x_order:
            send(g_block, g_full.at[there], G_BACK_X, at_x(d))

    side = pl.ds(pl.multiple_of(core * (NX * GX), 8), NX * GX)

    def gram_back_to_core():
        all_bytes(g_full.at[pl.ds(0, (NX - 1) * GX)], recv_sem.at[G_BACK_X]).wait()
        send(g_full.at[side], g_full.at[side], G_BACK_C, at_core())

    def core_copy(h, d):
        return pltpu.make_async_remote_copy(
            src_ref=terms.at[h, d, :, 1 - core], dst_ref=c_recv.at[h, d],
            send_sem=core_send_sem.at[h, d], recv_sem=core_recv_sem.at[h, d],
            device_id=at_core(), device_id_type=MESH,
        )

    def back_project(h):
        all_bytes(w_all.at[h, pl.ds(0, 2)], recv_sem.at[ROWS_NEAR + h]).wait()
        all_bytes(w_all.at[h, pl.ds(0, 3)], recv_sem.at[ROWS_FAR + h]).wait()
        weights = w_all[h].reshape(rows, HALF)
        for d in x_order + [0]:
            x1 = lax.rem(x + d, NX)
            block = depth_t[pl.ds(pl.multiple_of(x1 * (XB * NC), 16), XB * NC), :]
            product = jnp.dot(block, weights, preferred_element_type=F32)
            terms[h, d] = product.reshape(NZ, NC, TS, HALF)
            core_copy(h, d).start()

    ways = ((0, 1), (1, NX - 1))

    def way_copy(h, slot, to):
        return pltpu.make_async_remote_copy(
            src_ref=h_send.at[h, slot], dst_ref=h_recv.at[h, slot],
            send_sem=h_send_sem.at[h, slot], recv_sem=h_recv_sem.at[h, slot],
            device_id=at_x(to), device_id_type=MESH,
        )

    def first_along_x(h):
        for i, d in enumerate(x_order + [0]):
            core_copy(h, d).wait()
            half = (terms[h, d, :, core] + c_recv[h, d]).reshape(XB, HALF)
            if i > 0:
                own[h, d] = half
                continue
            code = scale_code(whole_max(half))
            fixed = to_fixed(half, code)
            for slot, to in ways:
                h_send[h, slot, 0:H, :] = fixed[slot * H:(slot + 1) * H]
                h_send[h, slot, H:H + 16, :] = code_rows(code, HALF)
                way_copy(h, slot, to).start()

    def second_along_x(h):
        for slot, to in ways:
            way_copy(h, slot, to).wait()
            mid = pl.ds(slot * H, H)
            own[h, to, mid, :] = own[h, to, mid, :] + from_fixed(h_recv[h, slot], H)
            half = own[h, to]
            code = scale_code(whole_max(half))
            x_send[h, slot, 0:XB, :] = to_fixed(half, code)
            x_send[h, slot, XB:XB + 16, :] = code_rows(code, HALF)
            send(x_send.at[h, slot], x_recv.at[h, slot], SUM_X + h, at_x(to))

    def along_z(h):
        all_bytes(x_recv.at[h], recv_sem.at[SUM_X + h]).wait()
        half = own[h, 0] + from_fixed(x_recv[h, 0], XB) + from_fixed(x_recv[h, 1], XB)
        code = scale_code(whole_max(half))
        unit = 32767.0 * jnp.exp2(code * (-1.0 / 256.0))
        tail = jnp.broadcast_to(code, (8, HALF))
        own[h, 0] = half
        for d in z_order:
            z1 = lax.rem(z + d, NZ)
            v = own[h, 0, pl.ds(pl.multiple_of(z1 * TS, 8), TS), :]
            v = jnp.concatenate([v * unit, tail], axis=0)
            z_send[h, d] = v.astype(jnp.int32).astype(jnp.int16)
            send(z_send.at[h, d], z_recv.at[h, d], SUM_Z + h, at_z(d))

    def total_along_z(h):
        all_bytes(z_recv.at[h, pl.ds(1, NZ - 1)], recv_sem.at[SUM_Z + h]).wait()
        v = own[h, 0, pl.ds(pl.multiple_of(z * TS, 8), TS), :]
        for d in z_order:
            v = v + from_fixed(z_recv[h, d], TS)
        return v

    pass_on(1)
    gram_along_y()
    back_project(0)
    first_along_x(0)
    back_project(1)
    second_along_x(0)
    gram_back_along_z()
    first_along_x(1)
    gram_back_along_x()
    along_z(0)
    second_along_x(1)
    gram_back_to_core()
    along_z(1)

    all_bytes(g_full.at[pl.ds(0, NX * GX)], recv_sem.at[G_BACK_C]).wait()
    gram[:, 0:128] = g_full[0:K, :]
    gram[:, 128:256] = g_full[K:2 * K, :]
    gram_out = pltpu.make_async_copy(gram, gram_hbm, load_sem.at[0])
    gram_out.start()
    matrix = gram[...]
    eye = identity(K)
    diagonal = matrix * eye
    d_row = lax.rsqrt(jnp.sum(diagonal, axis=0, keepdims=True))
    d_col = lax.rsqrt(jnp.sum(diagonal, axis=1, keepdims=True))
    unit_gram = matrix * d_row * d_col
    unit_halves = halves(unit_gram)
    inverse = eye - half_lower(unit_gram - eye)
    rough = inverse.astype(jnp.bfloat16)
    error = dot(dot(rough, unit_halves[0], 0).astype(jnp.bfloat16), rough, 1) - eye
    inverse = inverse - dot(half_lower(error).astype(jnp.bfloat16), rough, 0)
    for _ in range(2):
        both = halves(inverse)
        error = dot3(halves(dot3(both, unit_halves, 0)), both, 1) - eye
        inverse = inverse - dot(half_lower(error).astype(jnp.bfloat16), both[0], 0)
    inverse = inverse * d_row
    off_ref[...] = jnp.broadcast_to(whole_max(error), (8, 128))
    both = halves(inverse)

    part = jnp.concatenate([total_along_z(0), total_along_z(1)], axis=1)
    part_ref[...] = part
    out_ref[...] = dot3(halves(part), both, 1)
    gram_out.wait()

    all_bytes(fx_recv, send_sem.at[AUX_FAR]).wait()
    all_bytes(f_send, send_sem.at[SKETCH_FAR]).wait()
    all_bytes(aux_send, send_sem.at[AUX]).wait()
    for h in range(2):
        all_bytes(p_send.at[h], send_sem.at[SKETCH + h]).wait()
        all_bytes(w_all.at[h, pl.ds(0, 2)], send_sem.at[ROWS_NEAR + h]).wait()
        all_bytes(w_all.at[h, 0], send_sem.at[ROWS_UP + h]).wait()
        all_bytes(w_all.at[h, 0], send_sem.at[ROWS_DOWN + h]).wait()
        all_bytes(w_all.at[h, pl.ds(0, 3)], send_sem.at[ROWS_FAR + h]).wait()
        all_bytes(x_send.at[h], send_sem.at[SUM_X + h]).wait()
        all_bytes(z_send.at[h, pl.ds(1, NZ - 1)], send_sem.at[SUM_Z + h]).wait()
    all_bytes(gx_recv.at[pl.ds(1, NU - 1)], send_sem.at[G_X]).wait()
    all_bytes(gz_recv.at[pl.ds(1, NZ - 1)], send_sem.at[G_Z]).wait()
    all_bytes(gy_recv.at[others], send_sem.at[G_Y]).wait()
    all_bytes(g_block.at[pl.ds(0, GX - GZ)], send_sem.at[G_BACK_Z]).wait()
    all_bytes(g_full.at[pl.ds(0, (NX - 1) * GX)], send_sem.at[G_BACK_X]).wait()
    all_bytes(g_full.at[side], send_sem.at[G_BACK_C]).wait()


def last_kernel(found_ref, off_ref, part_hbm, gram_hbm, out_ref, work, right, part, sem):
    K = work.shape[0]
    settled = jnp.max(off_ref[...]) < TOLERANCE
    out_ref[...] = found_ref[...]

    @pl.when(jnp.logical_not(settled))
    def _():
        load = pltpu.make_async_copy(gram_hbm, work, sem)
        load.start()
        load.wait()
        load = pltpu.make_async_copy(part_hbm, part, sem)
        load.start()
        load.wait()
        right[...] = identity(K)
        lane = lax.broadcasted_iota(jnp.int32, (1, K), 1)
        row = lax.broadcasted_iota(jnp.int32, (K, 1), 0)

        def step(k, _):
            m = work[...]
            top = work[pl.ds(k, 1), :]
            pivot = jnp.sum(jnp.where(lane == k, top, 0.0), axis=1, keepdims=True)
            column = jnp.sum(jnp.where(lane == k, m, 0.0), axis=1, keepdims=True)
            factor = jnp.where(row > k, column / pivot, 0.0)
            r = right[...]
            r_top = right[pl.ds(k, 1), :]
            work[...] = m - factor * top
            right[...] = r - factor * r_top
            return 0

        lax.fori_loop(0, K, step, 0)
        pivots = jnp.sum(work[...] * identity(K), axis=1, keepdims=True)
        out_ref[...] = times_t(part[...], right[...] / jnp.sqrt(pivots))


def solution(mesh, sizes=(4, 8, 8, 2)):
    NX, NY, NZ, NC = sizes

    def on_device(read_depth, gauss_sketch, keep_mask):
        rows, cols = read_depth.shape
        K = gauss_sketch.shape[1]
        RY = rows // NY
        TS = cols // (NX * NZ * NC)
        XB = NZ * TS
        NU = NX * NC
        GX = 2 * K // NU
        GZ = GX // NZ
        vmem = pl.BlockSpec(memory_space=pltpu.VMEM)
        hbm = pl.BlockSpec(memory_space=pl.ANY)
        i16 = jnp.int16
        found, part, gram, off = pl.pallas_call(
            functools.partial(main_kernel, NX, NY, NZ, NC),
            out_shape=(
                jax.ShapeDtypeStruct((TS, K), F32),
                jax.ShapeDtypeStruct((TS, K), F32),
                jax.ShapeDtypeStruct((K, K), F32),
                jax.ShapeDtypeStruct((8, 128), F32),
            ),
            in_specs=[hbm, hbm, vmem],
            out_specs=(vmem, vmem, hbm, vmem),
            scratch_shapes=[
                pltpu.VMEM((rows, cols), jnp.bfloat16),
                pltpu.VMEM((cols, K), jnp.bfloat16),
                pltpu.VMEM((cols, 128), jnp.bfloat16),
                pltpu.VMEM((cols, rows), jnp.bfloat16),
                pltpu.SemaphoreType.DMA((NY + 1,)),
                pltpu.VMEM((3, RY, K), i16),
                pltpu.VMEM((3, RY, K), i16),
                pltpu.VMEM((3, 8, 128), F32),
                pltpu.VMEM((4, 8, 128), F32),
                pltpu.VMEM((2, 4, RY, HALF), i16),
                pltpu.VMEM((2, 4, RY, HALF), i16),
                pltpu.VMEM((4, 8, 128), F32),
                pltpu.VMEM((4, 8, 128), F32),
                pltpu.VMEM((2, NY, RY, HALF), jnp.bfloat16),
                pltpu.VMEM((2 * K, 128), F32),
                pltpu.VMEM((NU, GX, 128), F32),
                pltpu.VMEM((GX, 128), F32),
                pltpu.VMEM((NZ, GZ, 128), F32),
                pltpu.VMEM((GZ, 128), F32),
                pltpu.VMEM((NY, GZ, 128), F32),
                pltpu.VMEM((GX, 128), F32),
                pltpu.VMEM((2 * K, 128), F32),
                pltpu.VMEM((K, K), F32),
                pltpu.VMEM((2, NX, NZ, NC, TS, HALF), F32),
                pltpu.VMEM((2, NX, NZ, TS, HALF), F32),
                pltpu.VMEM((2, NX, XB, HALF), F32),
                pltpu.VMEM((2, 2, XB // 2 + 16, HALF), i16),
                pltpu.VMEM((2, 2, XB // 2 + 16, HALF), i16),
                pltpu.VMEM((2, 2, XB + 16, HALF), i16),
                pltpu.VMEM((2, 2, XB + 16, HALF), i16),
                pltpu.VMEM((2, NZ, TS + 8, HALF), i16),
                pltpu.VMEM((2, NZ, TS + 8, HALF), i16),
                pltpu.SemaphoreType.DMA((PHASES,)),
                pltpu.SemaphoreType.DMA((PHASES,)),
                pltpu.SemaphoreType.DMA((2, NX)),
                pltpu.SemaphoreType.DMA((2, NX)),
                pltpu.SemaphoreType.DMA((2, 2)),
                pltpu.SemaphoreType.DMA((2, 2)),
            ],
            compiler_params=pltpu.CompilerParams(
                collective_id=0, has_side_effects=True, vmem_limit_bytes=60 << 20
            ),
        )(read_depth, gauss_sketch, keep_mask)
        return pl.pallas_call(
            last_kernel,
            out_shape=jax.ShapeDtypeStruct((TS, K), F32),
            in_specs=[vmem, vmem, hbm, hbm],
            out_specs=vmem,
            scratch_shapes=[
                pltpu.VMEM((K, K), F32),
                pltpu.VMEM((K, K), F32),
                pltpu.VMEM((TS, K), F32),
                pltpu.SemaphoreType.DMA,
            ],
            compiler_params=pltpu.CompilerParams(vmem_limit_bytes=60 << 20),
        )(found, off, part, gram)

    return jax.shard_map(
        on_device,
        mesh=mesh,
        in_specs=(P("samples", "targets"), P("targets", None), P("targets")),
        out_specs=P(("targets", "samples"), None),
        check_vma=False,
    )
```

```python
import functools

import jax
import jax.numpy as jnp
from jax import lax
from jax.experimental import pallas as pl
from jax.experimental.pallas import tpu as pltpu
from jax.sharding import PartitionSpec as P

MESH = pl.DeviceIdType.MESH
F32 = jnp.float32
HIGH = lax.Precision.HIGHEST
STEPS = 3
TOLERANCE = 2e-3
HALF = 128
AUX_FAR, SKETCH_FAR, AUX, SKETCH, G_X, G_Z, G_Y, G_BACK_Z, G_BACK_X, G_BACK_C = 0, 1, 2, 3, 5, 6, 7, 8, 9, 10
SUM_X, SUM_Z, ROWS_NEAR, ROWS_UP, ROWS_DOWN, ROWS_FAR, PHASES = 11, 13, 15, 17, 19, 21, 23
CUT = 48


def far_first(n):
    return sorted(range(1, n), key=lambda d: -min(d, n - d))


def whole_max(v):
    return jnp.max(jnp.max(jnp.abs(v), axis=0, keepdims=True), axis=1, keepdims=True)


def scale_code(peak):
    return jnp.ceil(jnp.log2(jnp.maximum(peak, 1e-30)) * 256.0) + 1.0


def to_fixed(v, code):
    unit = 32767.0 * jnp.exp2(code * (-1.0 / 256.0))
    return (v * unit).astype(jnp.int32).astype(jnp.int16)


def code_rows(code, columns):
    return jnp.broadcast_to(code.astype(jnp.int32), (16, columns)).astype(jnp.int16)


def from_fixed(message, rows):
    values = message.astype(jnp.int32).astype(F32)
    unit = jnp.exp2(values[rows:rows + 1] * (1.0 / 256.0)) * (1.0 / 32767.0)
    return values[:rows] * unit


def half_lower(e):
    k = e.shape[0]
    row = lax.broadcasted_iota(jnp.int32, (k, k), 0)
    col = lax.broadcasted_iota(jnp.int32, (k, k), 1)
    return jnp.where(row > col, e, jnp.where(row == col, 0.5 * e, 0.0))


def identity(k):
    row = lax.broadcasted_iota(jnp.int32, (k, k), 0)
    col = lax.broadcasted_iota(jnp.int32, (k, k), 1)
    return jnp.where(row == col, 1.0, 0.0).astype(F32)


def halves(a):
    high = a.astype(jnp.bfloat16)
    return high, (a - high.astype(F32)).astype(jnp.bfloat16)


def dot(a, b, side):
    return lax.dot_general(a, b, (((1,), (side,)), ((), ())), preferred_element_type=F32)


def dot3(a, b, side):
    a_high, a_low = a
    b_high, b_low = b
    return dot(a_high, b_high, side) + (dot(a_high, b_low, side) + dot(a_low, b_high, side))


def times_t(a, b):
    return lax.dot_general(a, b, (((1,), (1,)), ((), ())), precision=HIGH, preferred_element_type=F32)


def all_bytes(ref, sem):
    return pltpu.make_async_copy(ref, ref, sem)


def main_kernel(
    NX, NY, NZ, NC,
    depth_hbm, gauss_hbm, keep_ref,
    out_ref, part_ref, gram_hbm, off_ref,
    depth, gauss, keep_col, depth_t, raw_sum, q_sum, inverse, load_sem,
    f_send, f_recv, fx_send, fx_recv, p_send, p_recv, aux_send, aux_recv, w_all,
    g_own, gx_recv, g_sum, gz_recv, g_piece, gy_recv, g_block, g_full, gram,
    terms, c_recv, own, h_send, h_recv, x_send, x_recv, z_send, z_recv,
    send_sem, recv_sem, core_send_sem, core_recv_sem, h_send_sem, h_recv_sem,
):
    rows, cols = depth.shape
    K = gauss.shape[1]
    RY = rows // NY
    TS = cols // (NX * NZ * NC)
    XB = NZ * TS
    H = XB // 2
    NU = NX * NC
    GX = 2 * K // NU
    GZ = GX // NZ

    s = lax.axis_index("samples")
    y = lax.axis_index("targets")
    core = lax.rem(s, NC)
    z = lax.rem(s // NC, NZ)
    x = s // (NC * NZ)
    u = core * NX + x

    def at_y(d):
        return (s, lax.rem(y + d, NY))

    def place(x1, z1, c1):
        return ((x1 * NZ + z1) * NC + c1, y)

    def at_u(d):
        u1 = lax.rem(u + d, NU)
        return place(lax.rem(u1, NX), z, u1 // NX)

    def at_z(d):
        return place(x, lax.rem(z + d, NZ), core)

    def at_x(d):
        return place(lax.rem(x + d, NX), z, core)

    def at_core():
        return place(x, z, 1 - core)

    def send(src, dst, phase, to):
        pltpu.make_async_remote_copy(
            src_ref=src, dst_ref=dst, send_sem=send_sem.at[phase], recv_sem=recv_sem.at[phase],
            device_id=to, device_id_type=MESH,
        ).start()

    y_order = far_first(NY)

    def each_far_first(n, body):
        def step(i, _):
            k = (i + 1) // 2
            body(n // 2 + jnp.where(lax.rem(i, 2) == 0, k, -k))
            return 0

        lax.fori_loop(0, n - 1, step, 0)

    def sum_over(n, first, ref):
        return lax.fori_loop(1, n, lambda d, total: total + ref[d], first)

    others = pl.ds(1, NY - 1)

    def row_block(y1):
        return pl.ds(pl.multiple_of(y1 * RY, 16), RY)

    order = y_order + [0]
    gauss_load = pltpu.make_async_copy(gauss_hbm, gauss, load_sem.at[0])
    gauss_load.start()
    loads = []
    for i, d in enumerate(order):
        load = pltpu.make_async_copy(
            depth_hbm.at[row_block(lax.rem(y + d, NY))], depth.at[pl.ds(i * RY, RY)], load_sem.at[i + 1]
        )
        load.start()
        loads.append(load)

    barrier = pltpu.get_barrier_semaphore()
    for n, at in ((NY, at_y), (NU, at_u), (NZ, at_z)):
        each_far_first(n, lambda d, at=at: pl.semaphore_signal(
            barrier, inc=1, device_id=at(d), device_id_type=MESH))

    kept = keep_ref[...].astype(F32).reshape(1, cols)
    count = jnp.sum(kept, axis=1, keepdims=True)
    sub = lax.broadcasted_iota(jnp.int32, (8, 128), 0)
    for j in range(cols // 128):
        tile = jnp.broadcast_to(kept[:, j * 128:(j + 1) * 128], (128, 128)).T
        keep_col[j * 128:(j + 1) * 128, :] = tile.astype(jnp.bfloat16)
    gauss_load.wait()
    tiles = cols // 128

    def filter_rows(j, _):
        at = pl.ds(pl.multiple_of(j * 128, 128), 128)
        tile = keep_col[at, :]
        gauss[at, :] = gauss[at, :] * jnp.concatenate([tile] * (K // 128), axis=1)
        return 0

    lax.fori_loop(0, tiles, filter_rows, 0)

    def aux_of(q_row, code, number):
        return jnp.where(sub == 0, q_row, jnp.where(sub == 1, code, jnp.where(sub == 2, number, 0.0)))

    def row_of(q):
        row = q.T[0:1]
        if RY < 128:
            row = jnp.concatenate([row, jnp.zeros((1, 128 - RY), F32)], axis=1)
        return row

    def unit_of(aux):
        return jnp.exp2(aux[1:2, 0:1] * (1.0 / 256.0)) * (1.0 / 32767.0)

    def columns_of(tiles):
        tile = jnp.concatenate([t[0:1] for t in tiles] + [jnp.zeros((8 - len(tiles), 128), F32)], axis=0)
        turned = tile.T[:RY]
        return [turned[:, i:i + 1] for i in range(len(tiles))]

    def safe_root(q):
        return jnp.sqrt(jnp.maximum(q, 1e-30))

    def turn(j, _):
        at = pl.ds(pl.multiple_of(j * 128, 128), 128)
        tile = keep_col[at, :]
        depth_t[at, :] = depth[:, at].T * jnp.concatenate([tile] * (rows // 128), axis=1)
        return 0

    group = NY // 2
    raws, q_rows, q_cols = {}, {}, {}
    for g in range(2):
        for i in range(g * group, (g + 1) * group):
            loads[i].wait()
        span = slice(g * group * RY, (g + 1) * group * RY)
        raw_sum[...] = jnp.zeros_like(raw_sum)
        q_sum[...] = jnp.zeros_like(q_sum)

        def add_columns(j, _):
            at = pl.ds(pl.multiple_of(j * 256, 256), 256)
            values = depth[span, at]
            raw_sum[...] += jnp.dot(values, gauss[at, :], preferred_element_type=F32)
            q_sum[...] += jnp.dot(values * values, keep_col[at, :], preferred_element_type=F32)
            return 0

        lax.fori_loop(0, cols // 256, add_columns, 0)
        raw = raw_sum[...]
        q = q_sum[...]
        for i in range(group):
            d = order[g * group + i]
            at = slice(i * RY, (i + 1) * RY)
            raws[d], q_rows[d], q_cols[d] = raw[at], row_of(q[at]), q[at, 0:1]
        some = slice(0, 3 * RY) if g == 0 else slice(RY, 3 * RY)
        invert = lax.rsqrt(jnp.maximum(q[some], 1e-30))
        level = [raw[some, h * HALF:(h + 1) * HALF] * invert for h in range(2)]
        code = scale_code(jnp.maximum(whole_max(level[0]), whole_max(level[1])))
        fixed = [to_fixed(part, code) for part in level]
        if g == 0:
            for i, d in enumerate((4, 3, 5)):
                for h in range(2):
                    f_send[i, :, h * HALF:(h + 1) * HALF] = fixed[h][i * RY:(i + 1) * RY]
                fx_send[i] = aux_of(q_rows[d], code, count)
            pl.semaphore_wait(barrier, NY + NU + NZ - 3)
            upper, lower = pl.ds(0, CUT), pl.ds(CUT, RY - CUT)
            send(fx_send.at[0], fx_recv.at[2], AUX_FAR, at_y(2))
            send(fx_send.at[0], fx_recv.at[3], AUX_FAR, at_y(NY - 2))
            send(f_send.at[0, upper], f_recv.at[2, upper], SKETCH_FAR, at_y(2))
            send(f_send.at[0, lower], f_recv.at[2, lower], SKETCH_FAR, at_y(NY - 2))
            for i, to in ((1, 1), (2, NY - 1)):
                send(fx_send.at[i], fx_recv.at[i - 1], AUX_FAR, at_y(to))
                send(f_send.at[i], f_recv.at[i - 1], SKETCH_FAR, at_y(to))
        else:
            for i, d in enumerate((1, NY - 1)):
                for h in range(2):
                    p_send[h, i] = fixed[h][i * RY:(i + 1) * RY]
                aux_send[i] = aux_of(q_rows[d], code, count)
                send(aux_send.at[i], aux_recv.at[i], AUX, at_y(d))
                for h in range(2):
                    send(p_send.at[h, i], p_recv.at[h, i], SKETCH + h, at_y(d))

    lax.fori_loop(0, tiles // 2, turn, 0)

    all_bytes(fx_recv, recv_sem.at[AUX_FAR]).wait()
    all_bytes(f_recv, recv_sem.at[SKETCH_FAR]).wait()
    lane = lax.broadcasted_iota(jnp.int32, (1, 128), 1)
    far = [fx_recv[i] for i in range(4)]
    far_cols = columns_of(far)
    far_unit = [unit_of(t) for t in far]
    last = f_recv[2].astype(jnp.int32).astype(F32)
    row = lax.broadcasted_iota(jnp.int32, (RY, 1), 0)
    for i, d in ((0, 2), (1, NY - 2)):
        part = (row < CUT) if i == 0 else (row >= CUT)
        q_part = (lane < CUT) if i == 0 else (lane >= CUT)
        total = raws[d] + f_recv[i].astype(jnp.int32).astype(F32) * (safe_root(far_cols[i]) * far_unit[i])
        total = total + last * jnp.where(part, safe_root(far_cols[2 + i]) * far_unit[2 + i], 0.0)
        q_col = q_cols[d] + far_cols[i] + jnp.where(part, far_cols[2 + i], 0.0)
        q_row = q_rows[d] + far[i][0:1] + jnp.where(q_part, far[2 + i][0:1], 0.0)
        number = count + far[i][2:3, 0:1]
        if i == 0:
            number = number + far[2][2:3, 0:1]
        level = total * lax.rsqrt(jnp.maximum(q_col, 1e-30))
        code = scale_code(whole_max(level))
        fixed = to_fixed(level, code)
        aux_send[2 + i] = aux_of(q_row, code, number)
        send(aux_send.at[2 + i], aux_recv.at[2 + i], AUX, at_y(d))
        for h in range(2):
            p_send[h, 2 + i] = fixed[:, h * HALF:(h + 1) * HALF]
        send(p_send.at[0, 2 + i], p_recv.at[0, 2 + i], SKETCH, at_y(d))
    for i, d in ((0, 2), (1, NY - 2)):
        send(p_send.at[1, 2 + i], p_recv.at[1, 2 + i], SKETCH + 1, at_y(d))

    lax.fori_loop(tiles // 2, 3 * tiles // 4, turn, 0)

    all_bytes(aux_recv, recv_sem.at[AUX]).wait()
    near = [aux_recv[i] for i in range(4)]
    near_cols = columns_of(near)
    q_total, counts = q_cols[0], count
    for i in range(4):
        q_total = q_total + near_cols[i]
        counts = counts + near[i][2:3, 0:1]
    to_scaled = lax.rsqrt((q_total + 1.0) / (counts + 1.0))
    roots = [safe_root(near_cols[i]) * unit_of(near[i]) for i in range(4)]

    def slot(d):
        return order.index(d % NY)

    sketched = []
    for h in range(2):
        all_bytes(p_recv.at[h], recv_sem.at[SKETCH + h]).wait()
        raw = raws[0][:, h * HALF:(h + 1) * HALF]
        for i in range(4):
            raw = raw + p_recv[h, i].astype(jnp.int32).astype(F32) * roots[i]
        scaled = raw * to_scaled
        sketched.append(scaled)
        w_all[h, slot(0)] = (scaled * to_scaled).astype(jnp.bfloat16)
        for d, phase in ((2, ROWS_UP), (NY - 2, ROWS_DOWN), (1, ROWS_NEAR), (NY - 1, ROWS_NEAR)):
            send(w_all.at[h, slot(0)], w_all.at[h, slot(-d)], phase + h, at_y(d))

    def pass_on(h):
        for phase, back, part in ((ROWS_UP, -2, pl.ds(0, CUT)), (ROWS_DOWN, 2, pl.ds(CUT, RY - CUT))):
            ahead = -back // 2
            held = w_all.at[h, slot(back)]
            all_bytes(held, recv_sem.at[phase + h]).wait()
            send(held.at[part], w_all.at[h, slot(2 * back), part], ROWS_FAR + h, at_y((2 * ahead) % NY))
            send(held, w_all.at[h, slot(back - ahead)], ROWS_FAR + h, at_y(ahead % NY))

    sketched = jnp.concatenate(sketched, axis=1)
    own_gram = dot3(halves(sketched.T), halves(sketched), 0)
    g_own[0:K, :] = own_gram[:, :HALF]
    g_own[K:2 * K, :] = own_gram[:, HALF:]
    def send_x(d):
        u1 = lax.rem(u + d, NU)
        send(g_own.at[pl.ds(pl.multiple_of(u1 * GX, 8), GX)], gx_recv.at[d], G_X, at_u(d))

    each_far_first(NU, send_x)
    lax.fori_loop(3 * tiles // 4, tiles, turn, 0)
    pass_on(0)
    all_bytes(gx_recv.at[pl.ds(1, NU - 1)], recv_sem.at[G_X]).wait()
    g_sum[...] = sum_over(NU, g_own[pl.ds(pl.multiple_of(u * GX, 8), GX), :], gx_recv)

    def send_z(d):
        z1 = lax.rem(z + d, NZ)
        send(g_sum.at[pl.ds(pl.multiple_of(z1 * GZ, 8), GZ)], gz_recv.at[d], G_Z, at_z(d))

    each_far_first(NZ, send_z)

    def gram_along_y():
        all_bytes(gz_recv.at[pl.ds(1, NZ - 1)], recv_sem.at[G_Z]).wait()
        g_piece[...] = sum_over(NZ, g_sum[pl.ds(pl.multiple_of(z * GZ, 8), GZ), :], gz_recv)
        each_far_first(NY, lambda d: send(g_piece, gy_recv.at[d], G_Y, at_y(d)))

    def gram_back_along_z():
        all_bytes(gy_recv.at[others], recv_sem.at[G_Y]).wait()
        here = pl.ds(pl.multiple_of(z * GZ, 8), GZ)
        g_block[here, :] = sum_over(NY, g_piece[...], gy_recv)
        each_far_first(NZ, lambda d: send(g_block.at[here], g_block.at[here], G_BACK_Z, at_z(d)))

    def gram_back_along_x():
        all_bytes(g_block.at[pl.ds(0, GX - GZ)], recv_sem.at[G_BACK_Z]).wait()
        there = pl.ds(pl.multiple_of(u * GX, 8), GX)
        g_full[there, :] = g_block[...]
        each_far_first(NX, lambda d: send(g_block, g_full.at[there], G_BACK_X, at_x(d)))

    side = pl.ds(pl.multiple_of(core * (NX * GX), 8), NX * GX)

    def gram_back_to_core():
        all_bytes(g_full.at[pl.ds(0, (NX - 1) * GX)], recv_sem.at[G_BACK_X]).wait()
        send(g_full.at[side], g_full.at[side], G_BACK_C, at_core())

    def core_copy(h, d):
        return pltpu.make_async_remote_copy(
            src_ref=terms.at[h, d, :, 1 - core], dst_ref=c_recv.at[h, d],
            send_sem=core_send_sem.at[h, d], recv_sem=core_recv_sem.at[h, d],
            device_id=at_core(), device_id_type=MESH,
        )

    def back_project(h):
        all_bytes(w_all.at[h, pl.ds(0, 2)], recv_sem.at[ROWS_NEAR + h]).wait()
        all_bytes(w_all.at[h, pl.ds(0, 3)], recv_sem.at[ROWS_FAR + h]).wait()
        weights = w_all[h].reshape(rows, HALF)

        def one(i, _):
            d = lax.rem(NX // 2 + i, NX)
            x1 = lax.rem(x + d, NX)
            block = depth_t[pl.ds(pl.multiple_of(x1 * (XB * NC), 16), XB * NC), :]
            product = jnp.dot(block, weights, preferred_element_type=F32)
            terms[h, d] = product.reshape(NZ, NC, TS, HALF)
            core_copy(h, d).start()
            return 0

        lax.fori_loop(0, NX, one, 0)

    ways = ((0, 1), (1, NX - 1))

    def way_copy(h, slot, to):
        return pltpu.make_async_remote_copy(
            src_ref=h_send.at[h, slot], dst_ref=h_recv.at[h, slot],
            send_sem=h_send_sem.at[h, slot], recv_sem=h_recv_sem.at[h, slot],
            device_id=at_x(to), device_id_type=MESH,
        )

    def first_along_x(h):
        def both_cores(d):
            core_copy(h, d).wait()
            return (terms[h, d, :, core] + c_recv[h, d]).reshape(XB, HALF)

        half = both_cores(NX // 2)
        code = scale_code(whole_max(half))
        fixed = to_fixed(half, code)
        for slot, to in ways:
            h_send[h, slot, 0:H, :] = fixed[slot * H:(slot + 1) * H]
            h_send[h, slot, H:H + 16, :] = code_rows(code, HALF)
            way_copy(h, slot, to).start()

        def rest(i, _):
            d = lax.rem(NX // 2 + i, NX)
            own[h, d] = both_cores(d)
            return 0

        lax.fori_loop(1, NX, rest, 0)

    def second_along_x(h):
        for slot, to in ways:
            way_copy(h, slot, to).wait()
            mid = pl.ds(slot * H, H)
            own[h, to, mid, :] = own[h, to, mid, :] + from_fixed(h_recv[h, slot], H)
            half = own[h, to]
            code = scale_code(whole_max(half))
            x_send[h, slot, 0:XB, :] = to_fixed(half, code)
            x_send[h, slot, XB:XB + 16, :] = code_rows(code, HALF)
            send(x_send.at[h, slot], x_recv.at[h, slot], SUM_X + h, at_x(to))

    def along_z(h):
        all_bytes(x_recv.at[h], recv_sem.at[SUM_X + h]).wait()
        half = own[h, 0] + from_fixed(x_recv[h, 0], XB) + from_fixed(x_recv[h, 1], XB)
        code = scale_code(whole_max(half))
        unit = 32767.0 * jnp.exp2(code * (-1.0 / 256.0))
        tail = jnp.broadcast_to(code, (8, HALF))
        own[h, 0] = half

        def one(d):
            z1 = lax.rem(z + d, NZ)
            v = own[h, 0, pl.ds(pl.multiple_of(z1 * TS, 8), TS), :]
            v = jnp.concatenate([v * unit, tail], axis=0)
            z_send[h, d] = v.astype(jnp.int32).astype(jnp.int16)
            send(z_send.at[h, d], z_recv.at[h, d], SUM_Z + h, at_z(d))

        each_far_first(NZ, one)

    def total_along_z(h):
        all_bytes(z_recv.at[h, pl.ds(1, NZ - 1)], recv_sem.at[SUM_Z + h]).wait()
        v = own[h, 0, pl.ds(pl.multiple_of(z * TS, 8), TS), :]
        return lax.fori_loop(1, NZ, lambda d, v: v + from_fixed(z_recv[h, d], TS), v)

    pass_on(1)
    gram_along_y()
    back_project(0)
    first_along_x(0)
    back_project(1)
    second_along_x(0)
    gram_back_along_z()
    first_along_x(1)
    gram_back_along_x()
    along_z(0)
    second_along_x(1)
    gram_back_to_core()
    along_z(1)

    all_bytes(g_full.at[pl.ds(0, NX * GX)], recv_sem.at[G_BACK_C]).wait()
    gram[:, 0:128] = g_full[0:K, :]
    gram[:, 128:256] = g_full[K:2 * K, :]
    gram_out = pltpu.make_async_copy(gram, gram_hbm, load_sem.at[0])
    gram_out.start()
    matrix = gram[...]
    eye = identity(K)
    diagonal = matrix * eye
    d_row = lax.rsqrt(jnp.sum(diagonal, axis=0, keepdims=True))
    d_col = lax.rsqrt(jnp.sum(diagonal, axis=1, keepdims=True))
    unit_gram = matrix * d_row * d_col
    unit_halves = halves(unit_gram)
    inverse[...] = eye - half_lower(unit_gram - eye)

    def improve(i, _):
        both = halves(inverse[...])
        error = dot3(halves(dot3(both, unit_halves, 0)), both, 1) - eye
        off_ref[...] = jnp.broadcast_to(whole_max(error), (8, 128))
        inverse[...] = inverse[...] - dot(half_lower(error).astype(jnp.bfloat16), both[0], 0)
        return 0

    lax.fori_loop(0, STEPS, improve, 0)
    both = halves(inverse[...] * d_row)

    part = jnp.concatenate([total_along_z(0), total_along_z(1)], axis=1)
    part_ref[...] = part
    out_ref[...] = dot3(halves(part), both, 1)
    gram_out.wait()

    all_bytes(fx_recv, send_sem.at[AUX_FAR]).wait()
    all_bytes(f_send, send_sem.at[SKETCH_FAR]).wait()
    all_bytes(aux_send, send_sem.at[AUX]).wait()
    for h in range(2):
        all_bytes(p_send.at[h], send_sem.at[SKETCH + h]).wait()
        all_bytes(w_all.at[h, pl.ds(0, 2)], send_sem.at[ROWS_NEAR + h]).wait()
        all_bytes(w_all.at[h, 0], send_sem.at[ROWS_UP + h]).wait()
        all_bytes(w_all.at[h, 0], send_sem.at[ROWS_DOWN + h]).wait()
        all_bytes(w_all.at[h, pl.ds(0, 3)], send_sem.at[ROWS_FAR + h]).wait()
        all_bytes(x_send.at[h], send_sem.at[SUM_X + h]).wait()
        all_bytes(z_send.at[h, pl.ds(1, NZ - 1)], send_sem.at[SUM_Z + h]).wait()
    all_bytes(gx_recv.at[pl.ds(1, NU - 1)], send_sem.at[G_X]).wait()
    all_bytes(gz_recv.at[pl.ds(1, NZ - 1)], send_sem.at[G_Z]).wait()
    all_bytes(gy_recv.at[others], send_sem.at[G_Y]).wait()
    all_bytes(g_block.at[pl.ds(0, GX - GZ)], send_sem.at[G_BACK_Z]).wait()
    all_bytes(g_full.at[pl.ds(0, (NX - 1) * GX)], send_sem.at[G_BACK_X]).wait()
    all_bytes(g_full.at[side], send_sem.at[G_BACK_C]).wait()


def last_kernel(found_ref, off_ref, part_hbm, gram_hbm, out_ref, work, right, part, sem):
    K = work.shape[0]
    settled = jnp.max(off_ref[...]) < TOLERANCE
    out_ref[...] = found_ref[...]

    @pl.when(jnp.logical_not(settled))
    def _():
        load = pltpu.make_async_copy(gram_hbm, work, sem)
        load.start()
        load.wait()
        load = pltpu.make_async_copy(part_hbm, part, sem)
        load.start()
        load.wait()
        right[...] = identity(K)
        lane = lax.broadcasted_iota(jnp.int32, (1, K), 1)
        row = lax.broadcasted_iota(jnp.int32, (K, 1), 0)

        def step(k, _):
            m = work[...]
            top = work[pl.ds(k, 1), :]
            pivot = jnp.sum(jnp.where(lane == k, top, 0.0), axis=1, keepdims=True)
            column = jnp.sum(jnp.where(lane == k, m, 0.0), axis=1, keepdims=True)
            factor = jnp.where(row > k, column / pivot, 0.0)
            r = right[...]
            r_top = right[pl.ds(k, 1), :]
            work[...] = m - factor * top
            right[...] = r - factor * r_top
            return 0

        lax.fori_loop(0, K, step, 0)
        pivots = jnp.sum(work[...] * identity(K), axis=1, keepdims=True)
        out_ref[...] = times_t(part[...], right[...] / jnp.sqrt(pivots))


def solution(mesh, sizes=(4, 8, 8, 2)):
    NX, NY, NZ, NC = sizes

    def on_device(read_depth, gauss_sketch, keep_mask):
        rows, cols = read_depth.shape
        K = gauss_sketch.shape[1]
        RY = rows // NY
        TS = cols // (NX * NZ * NC)
        XB = NZ * TS
        NU = NX * NC
        GX = 2 * K // NU
        GZ = GX // NZ
        vmem = pl.BlockSpec(memory_space=pltpu.VMEM)
        hbm = pl.BlockSpec(memory_space=pl.ANY)
        i16 = jnp.int16
        found, part, gram, off = pl.pallas_call(
            functools.partial(main_kernel, NX, NY, NZ, NC),
            out_shape=(
                jax.ShapeDtypeStruct((TS, K), F32),
                jax.ShapeDtypeStruct((TS, K), F32),
                jax.ShapeDtypeStruct((K, K), F32),
                jax.ShapeDtypeStruct((8, 128), F32),
            ),
            in_specs=[hbm, hbm, vmem],
            out_specs=(vmem, vmem, hbm, vmem),
            scratch_shapes=[
                pltpu.VMEM((rows, cols), jnp.bfloat16),
                pltpu.VMEM((cols, K), jnp.bfloat16),
                pltpu.VMEM((cols, 128), jnp.bfloat16),
                pltpu.VMEM((cols, rows), jnp.bfloat16),
                pltpu.VMEM((rows // 2, K), F32),
                pltpu.VMEM((rows // 2, 128), F32),
                pltpu.VMEM((K, K), F32),
                pltpu.SemaphoreType.DMA((NY + 1,)),
                pltpu.VMEM((3, RY, K), i16),
                pltpu.VMEM((3, RY, K), i16),
                pltpu.VMEM((3, 8, 128), F32),
                pltpu.VMEM((4, 8, 128), F32),
                pltpu.VMEM((2, 4, RY, HALF), i16),
                pltpu.VMEM((2, 4, RY, HALF), i16),
                pltpu.VMEM((4, 8, 128), F32),
                pltpu.VMEM((4, 8, 128), F32),
                pltpu.VMEM((2, NY, RY, HALF), jnp.bfloat16),
                pltpu.VMEM((2 * K, 128), F32),
                pltpu.VMEM((NU, GX, 128), F32),
                pltpu.VMEM((GX, 128), F32),
                pltpu.VMEM((NZ, GZ, 128), F32),
                pltpu.VMEM((GZ, 128), F32),
                pltpu.VMEM((NY, GZ, 128), F32),
                pltpu.VMEM((GX, 128), F32),
                pltpu.VMEM((2 * K, 128), F32),
                pltpu.VMEM((K, K), F32),
                pltpu.VMEM((2, NX, NZ, NC, TS, HALF), F32),
                pltpu.VMEM((2, NX, NZ, TS, HALF), F32),
                pltpu.VMEM((2, NX, XB, HALF), F32),
                pltpu.VMEM((2, 2, XB // 2 + 16, HALF), i16),
                pltpu.VMEM((2, 2, XB // 2 + 16, HALF), i16),
                pltpu.VMEM((2, 2, XB + 16, HALF), i16),
                pltpu.VMEM((2, 2, XB + 16, HALF), i16),
                pltpu.VMEM((2, NZ, TS + 8, HALF), i16),
                pltpu.VMEM((2, NZ, TS + 8, HALF), i16),
                pltpu.SemaphoreType.DMA((PHASES,)),
                pltpu.SemaphoreType.DMA((PHASES,)),
                pltpu.SemaphoreType.DMA((2, NX)),
                pltpu.SemaphoreType.DMA((2, NX)),
                pltpu.SemaphoreType.DMA((2, 2)),
                pltpu.SemaphoreType.DMA((2, 2)),
            ],
            compiler_params=pltpu.CompilerParams(
                collective_id=0, has_side_effects=True, vmem_limit_bytes=60 << 20
            ),
        )(read_depth, gauss_sketch, keep_mask)
        return pl.pallas_call(
            last_kernel,
            out_shape=jax.ShapeDtypeStruct((TS, K), F32),
            in_specs=[vmem, vmem, hbm, hbm],
            out_specs=vmem,
            scratch_shapes=[
                pltpu.VMEM((K, K), F32),
                pltpu.VMEM((K, K), F32),
                pltpu.VMEM((TS, K), F32),
                pltpu.SemaphoreType.DMA,
            ],
            compiler_params=pltpu.CompilerParams(vmem_limit_bytes=60 << 20),
        )(found, off, part, gram)

    return jax.shard_map(
        on_device,
        mesh=mesh,
        in_specs=(P("samples", "targets"), P("targets", None), P("targets")),
        out_specs=P(("targets", "samples"), None),
        check_vma=False,
    )
```

```python
import functools

import jax
import jax.numpy as jnp
from jax import lax
from jax.experimental import pallas as pl
from jax.experimental.pallas import tpu as pltpu
from jax.sharding import PartitionSpec as P

MESH = pl.DeviceIdType.MESH
F32 = jnp.float32
HIGH = lax.Precision.HIGHEST
TOLERANCE = 1e-2
HALF = 128
AUX_FAR, SKETCH_FAR, AUX, SKETCH, G_X, G_Z, G_Y, G_BACK_Z, G_BACK_X, G_BACK_C = 0, 1, 2, 3, 5, 6, 7, 8, 9, 10
SUM_X, SUM_Z, ROWS_NEAR, ROWS_UP, ROWS_DOWN, ROWS_FAR, PHASES = 11, 13, 15, 17, 19, 21, 23
CUT = 48


def far_first(n):
    return sorted(range(1, n), key=lambda d: -min(d, n - d))


def whole_max(v):
    return jnp.max(jnp.max(jnp.abs(v), axis=0, keepdims=True), axis=1, keepdims=True)


def scale_code(peak):
    return jnp.ceil(jnp.log2(jnp.maximum(peak, 1e-30)) * 256.0) + 1.0


def to_fixed(v, code):
    unit = 32767.0 * jnp.exp2(code * (-1.0 / 256.0))
    return (v * unit).astype(jnp.int32).astype(jnp.int16)


def code_rows(code, columns):
    return jnp.broadcast_to(code.astype(jnp.int32), (16, columns)).astype(jnp.int16)


def from_fixed(message, rows):
    values = message.astype(jnp.int32).astype(F32)
    unit = jnp.exp2(values[rows:rows + 1] * (1.0 / 256.0)) * (1.0 / 32767.0)
    return values[:rows] * unit


def half_lower(e):
    k = e.shape[0]
    row = lax.broadcasted_iota(jnp.int32, (k, k), 0)
    col = lax.broadcasted_iota(jnp.int32, (k, k), 1)
    return jnp.where(row > col, e, jnp.where(row == col, 0.5 * e, 0.0))


def identity(k):
    row = lax.broadcasted_iota(jnp.int32, (k, k), 0)
    col = lax.broadcasted_iota(jnp.int32, (k, k), 1)
    return jnp.where(row == col, 1.0, 0.0).astype(F32)


def halves(a):
    high = a.astype(jnp.bfloat16)
    return high, (a - high.astype(F32)).astype(jnp.bfloat16)


def dot(a, b, side):
    return lax.dot_general(a, b, (((1,), (side,)), ((), ())), preferred_element_type=F32)


def dot3(a, b, side):
    a_high, a_low = a
    b_high, b_low = b
    return dot(a_high, b_high, side) + (dot(a_high, b_low, side) + dot(a_low, b_high, side))


def times_t(a, b):
    return lax.dot_general(a, b, (((1,), (1,)), ((), ())), precision=HIGH, preferred_element_type=F32)


def all_bytes(ref, sem):
    return pltpu.make_async_copy(ref, ref, sem)


def main_kernel(
    NX, NY, NZ, NC,
    depth_hbm, gauss_hbm, keep_ref,
    out_ref, part_ref, gram_hbm, off_ref,
    depth, gauss, keep_col, depth_t, raw_sum, q_sum, inverse, load_sem,
    f_send, f_recv, fx_send, fx_recv, p_send, p_recv, aux_send, aux_recv, w_all,
    g_own, gx_recv, g_sum, gz_recv, g_piece, gy_recv, g_block, g_full, gram,
    terms, c_recv, own, h_send, h_recv, x_send, x_recv, z_send, z_recv,
    send_sem, recv_sem, core_send_sem, core_recv_sem, h_send_sem, h_recv_sem,
):
    rows, cols = depth.shape
    K = gauss.shape[1]
    RY = rows // NY
    TS = cols // (NX * NZ * NC)
    XB = NZ * TS
    H = XB // 2
    NU = NX * NC
    GX = 2 * K // NU
    GZ = GX // NZ

    s = lax.axis_index("samples")
    y = lax.axis_index("targets")
    core = lax.rem(s, NC)
    z = lax.rem(s // NC, NZ)
    x = s // (NC * NZ)
    u = core * NX + x

    def at_y(d):
        return (s, lax.rem(y + d, NY))

    def place(x1, z1, c1):
        return ((x1 * NZ + z1) * NC + c1, y)

    def at_u(d):
        u1 = lax.rem(u + d, NU)
        return place(lax.rem(u1, NX), z, u1 // NX)

    def at_z(d):
        return place(x, lax.rem(z + d, NZ), core)

    def at_x(d):
        return place(lax.rem(x + d, NX), z, core)

    def at_core():
        return place(x, z, 1 - core)

    def send(src, dst, phase, to):
        pltpu.make_async_remote_copy(
            src_ref=src, dst_ref=dst, send_sem=send_sem.at[phase], recv_sem=recv_sem.at[phase],
            device_id=to, device_id_type=MESH,
        ).start()

    y_order = far_first(NY)

    def each_far_first(n, body):
        def step(i, _):
            k = (i + 1) // 2
            body(n // 2 + jnp.where(lax.rem(i, 2) == 0, k, -k))
            return 0

        lax.fori_loop(0, n - 1, step, 0)

    def sum_over(n, first, ref):
        return lax.fori_loop(1, n, lambda d, total: total + ref[d], first)

    others = pl.ds(1, NY - 1)

    def row_block(y1):
        return pl.ds(pl.multiple_of(y1 * RY, 16), RY)

    order = y_order + [0]
    gauss_load = pltpu.make_async_copy(gauss_hbm, gauss, load_sem.at[0])
    gauss_load.start()
    loads = []
    for i, d in enumerate(order):
        load = pltpu.make_async_copy(
            depth_hbm.at[row_block(lax.rem(y + d, NY))], depth.at[pl.ds(i * RY, RY)], load_sem.at[i + 1]
        )
        load.start()
        loads.append(load)

    barrier = pltpu.get_barrier_semaphore()
    for n, at in ((NY, at_y), (NU, at_u), (NZ, at_z)):
        each_far_first(n, lambda d, at=at: pl.semaphore_signal(
            barrier, inc=1, device_id=at(d), device_id_type=MESH))

    kept = keep_ref[...].astype(F32).reshape(1, cols)
    count = jnp.sum(kept, axis=1, keepdims=True)
    sub = lax.broadcasted_iota(jnp.int32, (8, 128), 0)
    for j in range(cols // 128):
        tile = jnp.broadcast_to(kept[:, j * 128:(j + 1) * 128], (128, 128)).T
        keep_col[j * 128:(j + 1) * 128, :] = tile.astype(jnp.bfloat16)
    gauss_load.wait()
    tiles = cols // 128

    def filter_rows(j, _):
        at = pl.ds(pl.multiple_of(j * 128, 128), 128)
        tile = keep_col[at, :]
        gauss[at, :] = gauss[at, :] * jnp.concatenate([tile] * (K // 128), axis=1)
        return 0

    lax.fori_loop(0, tiles, filter_rows, 0)

    def aux_of(q_row, code, number):
        return jnp.where(sub == 0, q_row, jnp.where(sub == 1, code, jnp.where(sub == 2, number, 0.0)))

    def row_of(q):
        row = q.T[0:1]
        if RY < 128:
            row = jnp.concatenate([row, jnp.zeros((1, 128 - RY), F32)], axis=1)
        return row

    def unit_of(aux):
        return jnp.exp2(aux[1:2, 0:1] * (1.0 / 256.0)) * (1.0 / 32767.0)

    def columns_of(tiles):
        tile = jnp.concatenate([t[0:1] for t in tiles] + [jnp.zeros((8 - len(tiles), 128), F32)], axis=0)
        turned = tile.T[:RY]
        return [turned[:, i:i + 1] for i in range(len(tiles))]

    def safe_root(q):
        return jnp.sqrt(jnp.maximum(q, 1e-30))

    def turn(j, _):
        at = pl.ds(pl.multiple_of(j * 128, 128), 128)
        tile = keep_col[at, :]
        depth_t[at, :] = depth[:, at].T * jnp.concatenate([tile] * (rows // 128), axis=1)
        return 0

    group = NY // 2
    raws, q_rows, q_cols = {}, {}, {}
    for g in range(2):
        for i in range(g * group, (g + 1) * group):
            loads[i].wait()
        span = slice(g * group * RY, (g + 1) * group * RY)
        raw_sum[...] = jnp.zeros_like(raw_sum)
        q_sum[...] = jnp.zeros_like(q_sum)

        def add_columns(j, _):
            at = pl.ds(pl.multiple_of(j * 256, 256), 256)
            values = depth[span, at]
            raw_sum[...] += jnp.dot(values, gauss[at, :], preferred_element_type=F32)
            q_sum[...] += jnp.dot(values * values, keep_col[at, :], preferred_element_type=F32)
            return 0

        lax.fori_loop(0, cols // 256, add_columns, 0)
        raw = raw_sum[...]
        q = q_sum[...]
        for i in range(group):
            d = order[g * group + i]
            at = slice(i * RY, (i + 1) * RY)
            raws[d], q_rows[d], q_cols[d] = raw[at], row_of(q[at]), q[at, 0:1]
        some = slice(0, 3 * RY) if g == 0 else slice(RY, 3 * RY)
        invert = lax.rsqrt(jnp.maximum(q[some], 1e-30))
        level = [raw[some, h * HALF:(h + 1) * HALF] * invert for h in range(2)]
        code = scale_code(jnp.maximum(whole_max(level[0]), whole_max(level[1])))
        fixed = [to_fixed(part, code) for part in level]
        if g == 0:
            for i, d in enumerate((4, 3, 5)):
                for h in range(2):
                    f_send[i, :, h * HALF:(h + 1) * HALF] = fixed[h][i * RY:(i + 1) * RY]
                fx_send[i] = aux_of(q_rows[d], code, count)
            pl.semaphore_wait(barrier, NY + NU + NZ - 3)
            upper, lower = pl.ds(0, CUT), pl.ds(CUT, RY - CUT)
            send(fx_send.at[0], fx_recv.at[2], AUX_FAR, at_y(2))
            send(fx_send.at[0], fx_recv.at[3], AUX_FAR, at_y(NY - 2))
            send(f_send.at[0, upper], f_recv.at[2, upper], SKETCH_FAR, at_y(2))
            send(f_send.at[0, lower], f_recv.at[2, lower], SKETCH_FAR, at_y(NY - 2))
            for i, to in ((1, 1), (2, NY - 1)):
                send(fx_send.at[i], fx_recv.at[i - 1], AUX_FAR, at_y(to))
                send(f_send.at[i], f_recv.at[i - 1], SKETCH_FAR, at_y(to))
        else:
            for i, d in enumerate((1, NY - 1)):
                for h in range(2):
                    p_send[h, i] = fixed[h][i * RY:(i + 1) * RY]
                aux_send[i] = aux_of(q_rows[d], code, count)
                send(aux_send.at[i], aux_recv.at[i], AUX, at_y(d))
                for h in range(2):
                    send(p_send.at[h, i], p_recv.at[h, i], SKETCH + h, at_y(d))

    lax.fori_loop(0, tiles // 4, turn, 0)

    all_bytes(fx_recv, recv_sem.at[AUX_FAR]).wait()
    all_bytes(f_recv, recv_sem.at[SKETCH_FAR]).wait()
    lane = lax.broadcasted_iota(jnp.int32, (1, 128), 1)
    far = [fx_recv[i] for i in range(4)]
    far_cols = columns_of(far)
    far_unit = [unit_of(t) for t in far]
    last = f_recv[2].astype(jnp.int32).astype(F32)
    row = lax.broadcasted_iota(jnp.int32, (RY, 1), 0)
    for i, d in ((0, 2), (1, NY - 2)):
        part = (row < CUT) if i == 0 else (row >= CUT)
        q_part = (lane < CUT) if i == 0 else (lane >= CUT)
        total = raws[d] + f_recv[i].astype(jnp.int32).astype(F32) * (safe_root(far_cols[i]) * far_unit[i])
        total = total + last * jnp.where(part, safe_root(far_cols[2 + i]) * far_unit[2 + i], 0.0)
        q_col = q_cols[d] + far_cols[i] + jnp.where(part, far_cols[2 + i], 0.0)
        q_row = q_rows[d] + far[i][0:1] + jnp.where(q_part, far[2 + i][0:1], 0.0)
        number = count + far[i][2:3, 0:1]
        if i == 0:
            number = number + far[2][2:3, 0:1]
        level = total * lax.rsqrt(jnp.maximum(q_col, 1e-30))
        code = scale_code(whole_max(level))
        fixed = to_fixed(level, code)
        aux_send[2 + i] = aux_of(q_row, code, number)
        send(aux_send.at[2 + i], aux_recv.at[2 + i], AUX, at_y(d))
        for h in range(2):
            p_send[h, 2 + i] = fixed[:, h * HALF:(h + 1) * HALF]
        send(p_send.at[0, 2 + i], p_recv.at[0, 2 + i], SKETCH, at_y(d))
    for i, d in ((0, 2), (1, NY - 2)):
        send(p_send.at[1, 2 + i], p_recv.at[1, 2 + i], SKETCH + 1, at_y(d))

    lax.fori_loop(tiles // 4, tiles // 2, turn, 0)

    all_bytes(aux_recv, recv_sem.at[AUX]).wait()
    near = [aux_recv[i] for i in range(4)]
    near_cols = columns_of(near)
    q_total, counts = q_cols[0], count
    for i in range(4):
        q_total = q_total + near_cols[i]
        counts = counts + near[i][2:3, 0:1]
    to_scaled = lax.rsqrt((q_total + 1.0) / (counts + 1.0))
    roots = [safe_root(near_cols[i]) * unit_of(near[i]) for i in range(4)]

    def slot(d):
        return order.index(d % NY)

    sketched = []
    for h in range(2):
        all_bytes(p_recv.at[h], recv_sem.at[SKETCH + h]).wait()
        raw = raws[0][:, h * HALF:(h + 1) * HALF]
        for i in range(4):
            raw = raw + p_recv[h, i].astype(jnp.int32).astype(F32) * roots[i]
        scaled = raw * to_scaled
        sketched.append(scaled)
        w_all[h, slot(0)] = (scaled * to_scaled).astype(jnp.bfloat16)
        for d, phase in ((2, ROWS_UP), (NY - 2, ROWS_DOWN), (1, ROWS_NEAR), (NY - 1, ROWS_NEAR)):
            send(w_all.at[h, slot(0)], w_all.at[h, slot(-d)], phase + h, at_y(d))

    def pass_on(h):
        for phase, back, part in ((ROWS_UP, -2, pl.ds(0, CUT)), (ROWS_DOWN, 2, pl.ds(CUT, RY - CUT))):
            ahead = -back // 2
            held = w_all.at[h, slot(back)]
            all_bytes(held, recv_sem.at[phase + h]).wait()
            send(held.at[part], w_all.at[h, slot(2 * back), part], ROWS_FAR + h, at_y((2 * ahead) % NY))
            send(held, w_all.at[h, slot(back - ahead)], ROWS_FAR + h, at_y(ahead % NY))

    sketched = jnp.concatenate(sketched, axis=1)
    own_gram = dot3(halves(sketched.T), halves(sketched), 0)
    g_own[0:K, :] = own_gram[:, :HALF]
    g_own[K:2 * K, :] = own_gram[:, HALF:]
    def send_x(d):
        u1 = lax.rem(u + d, NU)
        send(g_own.at[pl.ds(pl.multiple_of(u1 * GX, 8), GX)], gx_recv.at[d], G_X, at_u(d))

    each_far_first(NU, send_x)
    lax.fori_loop(tiles // 2, 3 * tiles // 4, turn, 0)
    pass_on(0)
    pass_on(1)
    lax.fori_loop(3 * tiles // 4, tiles, turn, 0)
    all_bytes(gx_recv.at[pl.ds(1, NU - 1)], recv_sem.at[G_X]).wait()
    g_sum[...] = sum_over(NU, g_own[pl.ds(pl.multiple_of(u * GX, 8), GX), :], gx_recv)

    def send_z(d):
        z1 = lax.rem(z + d, NZ)
        send(g_sum.at[pl.ds(pl.multiple_of(z1 * GZ, 8), GZ)], gz_recv.at[d], G_Z, at_z(d))

    each_far_first(NZ, send_z)

    def gram_along_y():
        all_bytes(gz_recv.at[pl.ds(1, NZ - 1)], recv_sem.at[G_Z]).wait()
        g_piece[...] = sum_over(NZ, g_sum[pl.ds(pl.multiple_of(z * GZ, 8), GZ), :], gz_recv)
        each_far_first(NY, lambda d: send(g_piece, gy_recv.at[d], G_Y, at_y(d)))

    def gram_back_along_z():
        all_bytes(gy_recv.at[others], recv_sem.at[G_Y]).wait()
        here = pl.ds(pl.multiple_of(z * GZ, 8), GZ)
        g_block[here, :] = sum_over(NY, g_piece[...], gy_recv)
        each_far_first(NZ, lambda d: send(g_block.at[here], g_block.at[here], G_BACK_Z, at_z(d)))

    def gram_back_along_x():
        all_bytes(g_block.at[pl.ds(0, GX - GZ)], recv_sem.at[G_BACK_Z]).wait()
        there = pl.ds(pl.multiple_of(u * GX, 8), GX)
        g_full[there, :] = g_block[...]
        each_far_first(NX, lambda d: send(g_block, g_full.at[there], G_BACK_X, at_x(d)))

    side = pl.ds(pl.multiple_of(core * (NX * GX), 8), NX * GX)

    def gram_back_to_core():
        all_bytes(g_full.at[pl.ds(0, (NX - 1) * GX)], recv_sem.at[G_BACK_X]).wait()
        send(g_full.at[side], g_full.at[side], G_BACK_C, at_core())

    def core_copy(h, d):
        return pltpu.make_async_remote_copy(
            src_ref=terms.at[h, d, :, 1 - core], dst_ref=c_recv.at[h, d],
            send_sem=core_send_sem.at[h, d], recv_sem=core_recv_sem.at[h, d],
            device_id=at_core(), device_id_type=MESH,
        )

    def back_project(h):
        all_bytes(w_all.at[h, pl.ds(0, 2)], recv_sem.at[ROWS_NEAR + h]).wait()
        all_bytes(w_all.at[h, pl.ds(0, 3)], recv_sem.at[ROWS_FAR + h]).wait()
        weights = w_all[h].reshape(rows, HALF)

        def one(i, _):
            d = lax.rem(NX // 2 + i, NX)
            x1 = lax.rem(x + d, NX)
            block = depth_t[pl.ds(pl.multiple_of(x1 * (XB * NC), 16), XB * NC), :]
            product = jnp.dot(block, weights, preferred_element_type=F32)
            terms[h, d] = product.reshape(NZ, NC, TS, HALF)
            core_copy(h, d).start()
            return 0

        lax.fori_loop(0, NX, one, 0)

    ways = ((0, 1), (1, NX - 1))

    def way_copy(h, slot, to):
        return pltpu.make_async_remote_copy(
            src_ref=h_send.at[h, slot], dst_ref=h_recv.at[h, slot],
            send_sem=h_send_sem.at[h, slot], recv_sem=h_recv_sem.at[h, slot],
            device_id=at_x(to), device_id_type=MESH,
        )

    def first_along_x(h):
        def both_cores(d):
            core_copy(h, d).wait()
            return (terms[h, d, :, core] + c_recv[h, d]).reshape(XB, HALF)

        half = both_cores(NX // 2)
        code = scale_code(whole_max(half))
        fixed = to_fixed(half, code)
        for slot, to in ways:
            h_send[h, slot, 0:H, :] = fixed[slot * H:(slot + 1) * H]
            h_send[h, slot, H:H + 16, :] = code_rows(code, HALF)
            way_copy(h, slot, to).start()

        def rest(i, _):
            d = lax.rem(NX // 2 + i, NX)
            own[h, d] = both_cores(d)
            return 0

        lax.fori_loop(1, NX, rest, 0)

    def second_along_x(h):
        for slot, to in ways:
            way_copy(h, slot, to).wait()
            mid = pl.ds(slot * H, H)
            own[h, to, mid, :] = own[h, to, mid, :] + from_fixed(h_recv[h, slot], H)
            half = own[h, to]
            code = scale_code(whole_max(half))
            x_send[h, slot, 0:XB, :] = to_fixed(half, code)
            x_send[h, slot, XB:XB + 16, :] = code_rows(code, HALF)
            send(x_send.at[h, slot], x_recv.at[h, slot], SUM_X + h, at_x(to))

    def along_z(h):
        all_bytes(x_recv.at[h], recv_sem.at[SUM_X + h]).wait()
        half = own[h, 0] + from_fixed(x_recv[h, 0], XB) + from_fixed(x_recv[h, 1], XB)
        code = scale_code(whole_max(half))
        unit = 32767.0 * jnp.exp2(code * (-1.0 / 256.0))
        tail = jnp.broadcast_to(code, (8, HALF))
        own[h, 0] = half

        def one(d):
            z1 = lax.rem(z + d, NZ)
            v = own[h, 0, pl.ds(pl.multiple_of(z1 * TS, 8), TS), :]
            v = jnp.concatenate([v * unit, tail], axis=0)
            z_send[h, d] = v.astype(jnp.int32).astype(jnp.int16)
            send(z_send.at[h, d], z_recv.at[h, d], SUM_Z + h, at_z(d))

        each_far_first(NZ, one)

    def total_along_z(h):
        all_bytes(z_recv.at[h, pl.ds(1, NZ - 1)], recv_sem.at[SUM_Z + h]).wait()
        v = own[h, 0, pl.ds(pl.multiple_of(z * TS, 8), TS), :]
        return lax.fori_loop(1, NZ, lambda d, v: v + from_fixed(z_recv[h, d], TS), v)

    back_project(0)
    back_project(1)
    gram_along_y()
    first_along_x(0)
    first_along_x(1)
    second_along_x(0)
    gram_back_along_z()
    second_along_x(1)
    along_z(0)
    gram_back_along_x()
    along_z(1)
    gram_back_to_core()

    all_bytes(g_full.at[pl.ds(0, NX * GX)], recv_sem.at[G_BACK_C]).wait()
    gram[:, 0:128] = g_full[0:K, :]
    gram[:, 128:256] = g_full[K:2 * K, :]
    gram_out = pltpu.make_async_copy(gram, gram_hbm, load_sem.at[0])
    gram_out.start()
    matrix = gram[...]
    eye = identity(K)
    diagonal = matrix * eye
    d_row = lax.rsqrt(jnp.sum(diagonal, axis=0, keepdims=True))
    d_col = lax.rsqrt(jnp.sum(diagonal, axis=1, keepdims=True))
    unit_gram = matrix * d_row * d_col
    unit_halves = halves(unit_gram)
    start = eye - half_lower(unit_gram - eye)
    rough = start.astype(jnp.bfloat16)
    error = dot(dot(rough, unit_halves[0], 0).astype(jnp.bfloat16), rough, 1) - eye
    inverse[...] = start - dot(half_lower(error).astype(jnp.bfloat16), rough, 0)
    both = halves(inverse[...])
    error = dot3(halves(dot3(both, unit_halves, 0)), both, 1) - eye
    off_ref[...] = jnp.broadcast_to(whole_max(error), (8, 128))
    found = inverse[...] - dot(half_lower(error).astype(jnp.bfloat16), both[0], 0)
    both = halves(found * d_row)

    part = jnp.concatenate([total_along_z(0), total_along_z(1)], axis=1)
    part_ref[...] = part
    out_ref[...] = dot3(halves(part), both, 1)
    gram_out.wait()

    all_bytes(fx_recv, send_sem.at[AUX_FAR]).wait()
    all_bytes(f_send, send_sem.at[SKETCH_FAR]).wait()
    all_bytes(aux_send, send_sem.at[AUX]).wait()
    for h in range(2):
        all_bytes(p_send.at[h], send_sem.at[SKETCH + h]).wait()
        all_bytes(w_all.at[h, pl.ds(0, 2)], send_sem.at[ROWS_NEAR + h]).wait()
        all_bytes(w_all.at[h, 0], send_sem.at[ROWS_UP + h]).wait()
        all_bytes(w_all.at[h, 0], send_sem.at[ROWS_DOWN + h]).wait()
        all_bytes(w_all.at[h, pl.ds(0, 3)], send_sem.at[ROWS_FAR + h]).wait()
        all_bytes(x_send.at[h], send_sem.at[SUM_X + h]).wait()
        all_bytes(z_send.at[h, pl.ds(1, NZ - 1)], send_sem.at[SUM_Z + h]).wait()
    all_bytes(gx_recv.at[pl.ds(1, NU - 1)], send_sem.at[G_X]).wait()
    all_bytes(gz_recv.at[pl.ds(1, NZ - 1)], send_sem.at[G_Z]).wait()
    all_bytes(gy_recv.at[others], send_sem.at[G_Y]).wait()
    all_bytes(g_block.at[pl.ds(0, GX - GZ)], send_sem.at[G_BACK_Z]).wait()
    all_bytes(g_full.at[pl.ds(0, (NX - 1) * GX)], send_sem.at[G_BACK_X]).wait()
    all_bytes(g_full.at[side], send_sem.at[G_BACK_C]).wait()


def last_kernel(found_ref, off_ref, part_hbm, gram_hbm, out_ref, work, right, part, sem):
    K = work.shape[0]
    settled = jnp.max(off_ref[...]) < TOLERANCE
    out_ref[...] = found_ref[...]

    @pl.when(jnp.logical_not(settled))
    def _():
        load = pltpu.make_async_copy(gram_hbm, work, sem)
        load.start()
        load.wait()
        load = pltpu.make_async_copy(part_hbm, part, sem)
        load.start()
        load.wait()
        right[...] = identity(K)
        lane = lax.broadcasted_iota(jnp.int32, (1, K), 1)
        row = lax.broadcasted_iota(jnp.int32, (K, 1), 0)

        def step(k, _):
            m = work[...]
            top = work[pl.ds(k, 1), :]
            pivot = jnp.sum(jnp.where(lane == k, top, 0.0), axis=1, keepdims=True)
            column = jnp.sum(jnp.where(lane == k, m, 0.0), axis=1, keepdims=True)
            factor = jnp.where(row > k, column / pivot, 0.0)
            r = right[...]
            r_top = right[pl.ds(k, 1), :]
            work[...] = m - factor * top
            right[...] = r - factor * r_top
            return 0

        lax.fori_loop(0, K, step, 0)
        pivots = jnp.sum(work[...] * identity(K), axis=1, keepdims=True)
        out_ref[...] = times_t(part[...], right[...] / jnp.sqrt(pivots))


def solution(mesh, sizes=(4, 8, 8, 2)):
    NX, NY, NZ, NC = sizes

    def on_device(read_depth, gauss_sketch, keep_mask):
        rows, cols = read_depth.shape
        K = gauss_sketch.shape[1]
        RY = rows // NY
        TS = cols // (NX * NZ * NC)
        XB = NZ * TS
        NU = NX * NC
        GX = 2 * K // NU
        GZ = GX // NZ
        vmem = pl.BlockSpec(memory_space=pltpu.VMEM)
        hbm = pl.BlockSpec(memory_space=pl.ANY)
        i16 = jnp.int16
        found, part, gram, off = pl.pallas_call(
            functools.partial(main_kernel, NX, NY, NZ, NC),
            out_shape=(
                jax.ShapeDtypeStruct((TS, K), F32),
                jax.ShapeDtypeStruct((TS, K), F32),
                jax.ShapeDtypeStruct((K, K), F32),
                jax.ShapeDtypeStruct((8, 128), F32),
            ),
            in_specs=[hbm, hbm, vmem],
            out_specs=(vmem, vmem, hbm, vmem),
            scratch_shapes=[
                pltpu.VMEM((rows, cols), jnp.bfloat16),
                pltpu.VMEM((cols, K), jnp.bfloat16),
                pltpu.VMEM((cols, 128), jnp.bfloat16),
                pltpu.VMEM((cols, rows), jnp.bfloat16),
                pltpu.VMEM((rows // 2, K), F32),
                pltpu.VMEM((rows // 2, 128), F32),
                pltpu.VMEM((K, K), F32),
                pltpu.SemaphoreType.DMA((NY + 1,)),
                pltpu.VMEM((3, RY, K), i16),
                pltpu.VMEM((3, RY, K), i16),
                pltpu.VMEM((3, 8, 128), F32),
                pltpu.VMEM((4, 8, 128), F32),
                pltpu.VMEM((2, 4, RY, HALF), i16),
                pltpu.VMEM((2, 4, RY, HALF), i16),
                pltpu.VMEM((4, 8, 128), F32),
                pltpu.VMEM((4, 8, 128), F32),
                pltpu.VMEM((2, NY, RY, HALF), jnp.bfloat16),
                pltpu.VMEM((2 * K, 128), F32),
                pltpu.VMEM((NU, GX, 128), F32),
                pltpu.VMEM((GX, 128), F32),
                pltpu.VMEM((NZ, GZ, 128), F32),
                pltpu.VMEM((GZ, 128), F32),
                pltpu.VMEM((NY, GZ, 128), F32),
                pltpu.VMEM((GX, 128), F32),
                pltpu.VMEM((2 * K, 128), F32),
                pltpu.VMEM((K, K), F32),
                pltpu.VMEM((2, NX, NZ, NC, TS, HALF), F32),
                pltpu.VMEM((2, NX, NZ, TS, HALF), F32),
                pltpu.VMEM((2, NX, XB, HALF), F32),
                pltpu.VMEM((2, 2, XB // 2 + 16, HALF), i16),
                pltpu.VMEM((2, 2, XB // 2 + 16, HALF), i16),
                pltpu.VMEM((2, 2, XB + 16, HALF), i16),
                pltpu.VMEM((2, 2, XB + 16, HALF), i16),
                pltpu.VMEM((2, NZ, TS + 8, HALF), i16),
                pltpu.VMEM((2, NZ, TS + 8, HALF), i16),
                pltpu.SemaphoreType.DMA((PHASES,)),
                pltpu.SemaphoreType.DMA((PHASES,)),
                pltpu.SemaphoreType.DMA((2, NX)),
                pltpu.SemaphoreType.DMA((2, NX)),
                pltpu.SemaphoreType.DMA((2, 2)),
                pltpu.SemaphoreType.DMA((2, 2)),
            ],
            compiler_params=pltpu.CompilerParams(
                collective_id=0, has_side_effects=True, vmem_limit_bytes=60 << 20
            ),
        )(read_depth, gauss_sketch, keep_mask)
        return pl.pallas_call(
            last_kernel,
            out_shape=jax.ShapeDtypeStruct((TS, K), F32),
            in_specs=[vmem, vmem, hbm, hbm],
            out_specs=vmem,
            scratch_shapes=[
                pltpu.VMEM((K, K), F32),
                pltpu.VMEM((K, K), F32),
                pltpu.VMEM((TS, K), F32),
                pltpu.SemaphoreType.DMA,
            ],
            compiler_params=pltpu.CompilerParams(vmem_limit_bytes=60 << 20),
        )(found, off, part, gram)

    return jax.shard_map(
        on_device,
        mesh=mesh,
        in_specs=(P("samples", "targets"), P("targets", None), P("targets")),
        out_specs=P(("targets", "samples"), None),
        check_vma=False,
    )
```

```python
import functools

import jax
import jax.numpy as jnp
from jax import lax
from jax.experimental import pallas as pl
from jax.experimental.pallas import tpu as pltpu
from jax.sharding import PartitionSpec as P

MESH = pl.DeviceIdType.MESH
F32 = jnp.float32
HIGH = lax.Precision.HIGHEST
TOLERANCE = 1e-2
HALF = 128
AUX_FAR, SKETCH_FAR, AUX, SKETCH, G_X, G_Z, G_Y, G_BACK_Z, G_BACK_X, G_BACK_C = 0, 1, 2, 3, 5, 6, 7, 8, 9, 10
SUM_X, SUM_Z, ROWS_NEAR, ROWS_UP, ROWS_DOWN, ROWS_FAR, PHASES = 11, 13, 15, 17, 19, 21, 23
CUT = 48


def far_first(n):
    return sorted(range(1, n), key=lambda d: -min(d, n - d))


def whole_max(v):
    return jnp.max(jnp.max(jnp.abs(v), axis=0, keepdims=True), axis=1, keepdims=True)


def scale_code(peak):
    return jnp.ceil(jnp.log2(jnp.maximum(peak, 1e-30)) * 256.0) + 1.0


def to_fixed(v, code):
    unit = 32767.0 * jnp.exp2(code * (-1.0 / 256.0))
    return (v * unit).astype(jnp.int32).astype(jnp.int16)


def code_rows(code, columns):
    return jnp.broadcast_to(code.astype(jnp.int32), (16, columns)).astype(jnp.int16)


def from_fixed(message, rows):
    values = message.astype(jnp.int32).astype(F32)
    unit = jnp.exp2(values[rows:rows + 1] * (1.0 / 256.0)) * (1.0 / 32767.0)
    return values[:rows] * unit


def half_lower(e):
    k = e.shape[0]
    row = lax.broadcasted_iota(jnp.int32, (k, k), 0)
    col = lax.broadcasted_iota(jnp.int32, (k, k), 1)
    return jnp.where(row > col, e, jnp.where(row == col, 0.5 * e, 0.0))


def identity(k):
    row = lax.broadcasted_iota(jnp.int32, (k, k), 0)
    col = lax.broadcasted_iota(jnp.int32, (k, k), 1)
    return jnp.where(row == col, 1.0, 0.0).astype(F32)


def halves(a):
    high = a.astype(jnp.bfloat16)
    return high, (a - high.astype(F32)).astype(jnp.bfloat16)


def dot(a, b, side):
    return lax.dot_general(a, b, (((1,), (side,)), ((), ())), preferred_element_type=F32)


def dot3(a, b, side):
    a_high, a_low = a
    b_high, b_low = b
    return dot(a_high, b_high, side) + (dot(a_high, b_low, side) + dot(a_low, b_high, side))


def times_t(a, b):
    return lax.dot_general(a, b, (((1,), (1,)), ((), ())), precision=HIGH, preferred_element_type=F32)


def all_bytes(ref, sem):
    return pltpu.make_async_copy(ref, ref, sem)


def main_kernel(
    NX, NY, NZ, NC,
    depth_hbm, gauss_hbm, keep_ref,
    out_ref, part_ref, gram_hbm, off_ref,
    depth, gauss, keep_col, depth_t, raw_sum, q_sum, inverse, load_sem,
    f_send, f_recv, fx_send, fx_recv, p_send, p_recv, aux_send, aux_recv, w_all,
    g_own, gx_recv, g_sum, gz_recv, g_piece, gy_recv, g_block, g_full, gram,
    terms, c_recv, own, h_send, h_recv, x_send, x_recv, z_send, z_recv,
    send_sem, recv_sem, core_send_sem, core_recv_sem, h_send_sem, h_recv_sem,
):
    rows, cols = depth.shape
    K = gauss.shape[1]
    RY = rows // NY
    TS = cols // (NX * NZ * NC)
    XB = NZ * TS
    H = XB // 2
    NU = NX * NC
    GX = 2 * K // NU
    GZ = GX // NZ

    s = lax.axis_index("samples")
    y = lax.axis_index("targets")
    core = lax.rem(s, NC)
    z = lax.rem(s // NC, NZ)
    x = s // (NC * NZ)
    u = core * NX + x

    def at_y(d):
        return (s, lax.rem(y + d, NY))

    def place(x1, z1, c1):
        return ((x1 * NZ + z1) * NC + c1, y)

    def at_u(d):
        u1 = lax.rem(u + d, NU)
        return place(lax.rem(u1, NX), z, u1 // NX)

    def at_z(d):
        return place(x, lax.rem(z + d, NZ), core)

    def at_x(d):
        return place(lax.rem(x + d, NX), z, core)

    def at_core():
        return place(x, z, 1 - core)

    def send(src, dst, phase, to):
        pltpu.make_async_remote_copy(
            src_ref=src, dst_ref=dst, send_sem=send_sem.at[phase], recv_sem=recv_sem.at[phase],
            device_id=to, device_id_type=MESH,
        ).start()

    y_order = far_first(NY)

    def each_far_first(n, body):
        def step(i, _):
            k = (i + 1) // 2
            body(n // 2 + jnp.where(lax.rem(i, 2) == 0, k, -k))
            return 0

        lax.fori_loop(0, n - 1, step, 0)

    def sum_over(n, first, ref):
        return lax.fori_loop(1, n, lambda d, total: total + ref[d], first)

    others = pl.ds(1, NY - 1)

    def row_block(y1):
        return pl.ds(pl.multiple_of(y1 * RY, 16), RY)

    order = y_order + [0]
    gauss_load = pltpu.make_async_copy(gauss_hbm, gauss, load_sem.at[0])
    gauss_load.start()
    loads = []
    for i, d in enumerate(order):
        load = pltpu.make_async_copy(
            depth_hbm.at[row_block(lax.rem(y + d, NY))], depth.at[pl.ds(i * RY, RY)], load_sem.at[i + 1]
        )
        load.start()
        loads.append(load)

    barrier = pltpu.get_barrier_semaphore()
    for n, at in ((NY, at_y), (NU, at_u), (NZ, at_z)):
        each_far_first(n, lambda d, at=at: pl.semaphore_signal(
            barrier, inc=1, device_id=at(d), device_id_type=MESH))

    kept = keep_ref[...].astype(F32).reshape(1, cols)
    count = jnp.sum(kept, axis=1, keepdims=True)
    sub = lax.broadcasted_iota(jnp.int32, (8, 128), 0)
    for j in range(cols // 128):
        tile = jnp.broadcast_to(kept[:, j * 128:(j + 1) * 128], (128, 128)).T
        keep_col[j * 128:(j + 1) * 128, :] = tile.astype(jnp.bfloat16)
    gauss_load.wait()
    tiles = cols // 128

    def aux_of(q_row, code, number):
        return jnp.where(sub == 0, q_row, jnp.where(sub == 1, code, jnp.where(sub == 2, number, 0.0)))

    def row_of(q):
        row = q.T[0:1]
        if RY < 128:
            row = jnp.concatenate([row, jnp.zeros((1, 128 - RY), F32)], axis=1)
        return row

    def unit_of(aux):
        return jnp.exp2(aux[1:2, 0:1] * (1.0 / 256.0)) * (1.0 / 32767.0)

    def columns_of(tiles):
        tile = jnp.concatenate([t[0:1] for t in tiles] + [jnp.zeros((8 - len(tiles), 128), F32)], axis=0)
        turned = tile.T[:RY]
        return [turned[:, i:i + 1] for i in range(len(tiles))]

    def safe_root(q):
        return jnp.sqrt(jnp.maximum(q, 1e-30))

    def turn(j, _):
        at = pl.ds(pl.multiple_of(j * 128, 128), 128)
        tile = keep_col[at, :]
        depth_t[at, :] = depth[:, at].T * jnp.concatenate([tile] * (rows // 128), axis=1)
        return 0

    group = NY // 2
    raws, q_rows, q_cols = {}, {}, {}
    for g in range(2):
        for i in range(g * group, (g + 1) * group):
            loads[i].wait()
        span = slice(g * group * RY, (g + 1) * group * RY)
        raw_sum[...] = jnp.zeros_like(raw_sum)
        q_sum[...] = jnp.zeros_like(q_sum)

        def add_columns(j, _):
            at = pl.ds(pl.multiple_of(j * 256, 256), 256)
            if g == 0:
                gauss[at, :] = gauss[at, :] * jnp.concatenate([keep_col[at, :]] * (K // 128), axis=1)
            values = depth[span, at]
            raw_sum[...] += jnp.dot(values, gauss[at, :], preferred_element_type=F32)
            q_sum[...] += jnp.dot(values * values, keep_col[at, :], preferred_element_type=F32)
            return 0

        lax.fori_loop(0, cols // 256, add_columns, 0)
        raw = raw_sum[...]
        q = q_sum[...]
        for i in range(group):
            d = order[g * group + i]
            at = slice(i * RY, (i + 1) * RY)
            raws[d], q_rows[d], q_cols[d] = raw[at], row_of(q[at]), q[at, 0:1]
        some = slice(0, 3 * RY) if g == 0 else slice(RY, 3 * RY)
        invert = lax.rsqrt(jnp.maximum(q[some], 1e-30))
        level = [raw[some, h * HALF:(h + 1) * HALF] * invert for h in range(2)]
        code = scale_code(jnp.maximum(whole_max(level[0]), whole_max(level[1])))
        fixed = [to_fixed(part, code) for part in level]
        if g == 0:
            for i, d in enumerate((4, 3, 5)):
                for h in range(2):
                    f_send[i, :, h * HALF:(h + 1) * HALF] = fixed[h][i * RY:(i + 1) * RY]
                fx_send[i] = aux_of(q_rows[d], code, count)
            pl.semaphore_wait(barrier, NY + NU + NZ - 3)
            upper, lower = pl.ds(0, CUT), pl.ds(CUT, RY - CUT)
            send(fx_send.at[0], fx_recv.at[2], AUX_FAR, at_y(2))
            send(fx_send.at[0], fx_recv.at[3], AUX_FAR, at_y(NY - 2))
            send(f_send.at[0, upper], f_recv.at[2, upper], SKETCH_FAR, at_y(2))
            send(f_send.at[0, lower], f_recv.at[2, lower], SKETCH_FAR, at_y(NY - 2))
            for i, to in ((1, 1), (2, NY - 1)):
                send(fx_send.at[i], fx_recv.at[i - 1], AUX_FAR, at_y(to))
                send(f_send.at[i], f_recv.at[i - 1], SKETCH_FAR, at_y(to))
        else:
            for i, d in enumerate((1, NY - 1)):
                for h in range(2):
                    p_send[i, :, h * HALF:(h + 1) * HALF] = fixed[h][i * RY:(i + 1) * RY]
                aux_send[i] = aux_of(q_rows[d], code, count)
                send(aux_send.at[i], aux_recv.at[i], AUX, at_y(d))
                send(p_send.at[i], p_recv.at[i], SKETCH, at_y(d))

    lax.fori_loop(0, tiles // 4, turn, 0)

    all_bytes(fx_recv, recv_sem.at[AUX_FAR]).wait()
    all_bytes(f_recv, recv_sem.at[SKETCH_FAR]).wait()
    lane = lax.broadcasted_iota(jnp.int32, (1, 128), 1)
    far = [fx_recv[i] for i in range(4)]
    far_cols = columns_of(far)
    far_unit = [unit_of(t) for t in far]
    last = f_recv[2].astype(jnp.int32).astype(F32)
    row = lax.broadcasted_iota(jnp.int32, (RY, 1), 0)
    for i, d in ((0, 2), (1, NY - 2)):
        part = (row < CUT) if i == 0 else (row >= CUT)
        q_part = (lane < CUT) if i == 0 else (lane >= CUT)
        total = raws[d] + f_recv[i].astype(jnp.int32).astype(F32) * (safe_root(far_cols[i]) * far_unit[i])
        total = total + last * jnp.where(part, safe_root(far_cols[2 + i]) * far_unit[2 + i], 0.0)
        q_col = q_cols[d] + far_cols[i] + jnp.where(part, far_cols[2 + i], 0.0)
        q_row = q_rows[d] + far[i][0:1] + jnp.where(q_part, far[2 + i][0:1], 0.0)
        number = count + far[i][2:3, 0:1]
        if i == 0:
            number = number + far[2][2:3, 0:1]
        level = total * lax.rsqrt(jnp.maximum(q_col, 1e-30))
        code = scale_code(whole_max(level))
        fixed = to_fixed(level, code)
        aux_send[2 + i] = aux_of(q_row, code, number)
        send(aux_send.at[2 + i], aux_recv.at[2 + i], AUX, at_y(d))
        p_send[2 + i] = fixed
        send(p_send.at[2 + i], p_recv.at[2 + i], SKETCH, at_y(d))

    lax.fori_loop(tiles // 4, tiles // 2, turn, 0)

    all_bytes(aux_recv, recv_sem.at[AUX]).wait()
    near = [aux_recv[i] for i in range(4)]
    near_cols = columns_of(near)
    q_total, counts = q_cols[0], count
    for i in range(4):
        q_total = q_total + near_cols[i]
        counts = counts + near[i][2:3, 0:1]
    to_scaled = lax.rsqrt((q_total + 1.0) / (counts + 1.0))
    roots = [safe_root(near_cols[i]) * unit_of(near[i]) for i in range(4)]

    def slot(d):
        return order.index(d % NY)

    all_bytes(p_recv, recv_sem.at[SKETCH]).wait()
    raw = raws[0]
    for i in range(4):
        raw = raw + p_recv[i].astype(jnp.int32).astype(F32) * roots[i]
    sketched = raw * to_scaled
    w_all[slot(0)] = (sketched * to_scaled).astype(jnp.bfloat16)
    for d, phase in ((2, ROWS_UP), (NY - 2, ROWS_DOWN), (1, ROWS_NEAR), (NY - 1, ROWS_NEAR)):
        send(w_all.at[slot(0)], w_all.at[slot(-d)], phase, at_y(d))

    def pass_on():
        for phase, back, part in ((ROWS_UP, -2, pl.ds(0, CUT)), (ROWS_DOWN, 2, pl.ds(CUT, RY - CUT))):
            ahead = -back // 2
            held = w_all.at[slot(back)]
            all_bytes(held, recv_sem.at[phase]).wait()
            send(held.at[part], w_all.at[slot(2 * back), part], ROWS_FAR, at_y((2 * ahead) % NY))
            send(held, w_all.at[slot(back - ahead)], ROWS_FAR, at_y(ahead % NY))

    own_gram = dot3(halves(sketched.T), halves(sketched), 0)
    g_own[0:K, :] = own_gram[:, :HALF]
    g_own[K:2 * K, :] = own_gram[:, HALF:]
    def send_x(d):
        u1 = lax.rem(u + d, NU)
        send(g_own.at[pl.ds(pl.multiple_of(u1 * GX, 8), GX)], gx_recv.at[d], G_X, at_u(d))

    each_far_first(NU, send_x)
    lax.fori_loop(tiles // 2, 3 * tiles // 4, turn, 0)
    pass_on()
    lax.fori_loop(3 * tiles // 4, tiles, turn, 0)
    all_bytes(gx_recv.at[pl.ds(1, NU - 1)], recv_sem.at[G_X]).wait()
    g_sum[...] = sum_over(NU, g_own[pl.ds(pl.multiple_of(u * GX, 8), GX), :], gx_recv)

    def send_z(d):
        z1 = lax.rem(z + d, NZ)
        send(g_sum.at[pl.ds(pl.multiple_of(z1 * GZ, 8), GZ)], gz_recv.at[d], G_Z, at_z(d))

    each_far_first(NZ, send_z)

    def gram_along_y():
        all_bytes(gz_recv.at[pl.ds(1, NZ - 1)], recv_sem.at[G_Z]).wait()
        g_piece[...] = sum_over(NZ, g_sum[pl.ds(pl.multiple_of(z * GZ, 8), GZ), :], gz_recv)
        each_far_first(NY, lambda d: send(g_piece, gy_recv.at[d], G_Y, at_y(d)))

    def gram_back_along_z():
        all_bytes(gy_recv.at[others], recv_sem.at[G_Y]).wait()
        here = pl.ds(pl.multiple_of(z * GZ, 8), GZ)
        g_block[here, :] = sum_over(NY, g_piece[...], gy_recv)
        each_far_first(NZ, lambda d: send(g_block.at[here], g_block.at[here], G_BACK_Z, at_z(d)))

    def gram_back_along_x():
        all_bytes(g_block.at[pl.ds(0, GX - GZ)], recv_sem.at[G_BACK_Z]).wait()
        there = pl.ds(pl.multiple_of(u * GX, 8), GX)
        g_full[there, :] = g_block[...]
        each_far_first(NX, lambda d: send(g_block, g_full.at[there], G_BACK_X, at_x(d)))

    side = pl.ds(pl.multiple_of(core * (NX * GX), 8), NX * GX)

    def gram_back_to_core():
        all_bytes(g_full.at[pl.ds(0, (NX - 1) * GX)], recv_sem.at[G_BACK_X]).wait()
        send(g_full.at[side], g_full.at[side], G_BACK_C, at_core())

    def core_copy(h, d):
        return pltpu.make_async_remote_copy(
            src_ref=terms.at[h, d, :, 1 - core], dst_ref=c_recv.at[h, d],
            send_sem=core_send_sem.at[h, d], recv_sem=core_recv_sem.at[h, d],
            device_id=at_core(), device_id_type=MESH,
        )

    def back_project():
        all_bytes(w_all.at[pl.ds(0, 2)], recv_sem.at[ROWS_NEAR]).wait()
        all_bytes(w_all.at[pl.ds(0, 3)], recv_sem.at[ROWS_FAR]).wait()

        def one(i, _):
            d = lax.rem(NX // 2 + i, NX)
            x1 = lax.rem(x + d, NX)
            block = depth_t[pl.ds(pl.multiple_of(x1 * (XB * NC), 16), XB * NC), :]
            product = jnp.dot(block, w_all[...].reshape(rows, K), preferred_element_type=F32)
            for h in range(2):
                terms[h, d] = product[:, h * HALF:(h + 1) * HALF].reshape(NZ, NC, TS, HALF)
                core_copy(h, d).start()
            return 0

        lax.fori_loop(0, NX, one, 0)

    ways = ((0, 1), (1, NX - 1))

    def way_copy(h, slot, to):
        return pltpu.make_async_remote_copy(
            src_ref=h_send.at[h, slot], dst_ref=h_recv.at[h, slot],
            send_sem=h_send_sem.at[h, slot], recv_sem=h_recv_sem.at[h, slot],
            device_id=at_x(to), device_id_type=MESH,
        )

    def first_along_x(h):
        def both_cores(d):
            core_copy(h, d).wait()
            return (terms[h, d, :, core] + c_recv[h, d]).reshape(XB, HALF)

        half = both_cores(NX // 2)
        code = scale_code(whole_max(half))
        fixed = to_fixed(half, code)
        for slot, to in ways:
            h_send[h, slot, 0:H, :] = fixed[slot * H:(slot + 1) * H]
            h_send[h, slot, H:H + 16, :] = code_rows(code, HALF)
            way_copy(h, slot, to).start()

        def rest(i, _):
            d = lax.rem(NX // 2 + i, NX)
            own[h, d] = both_cores(d)
            return 0

        lax.fori_loop(1, NX, rest, 0)

    def second_along_x(h):
        for slot, to in ways:
            way_copy(h, slot, to).wait()
            mid = pl.ds(slot * H, H)
            own[h, to, mid, :] = own[h, to, mid, :] + from_fixed(h_recv[h, slot], H)
            half = own[h, to]
            code = scale_code(whole_max(half))
            x_send[h, slot, 0:XB, :] = to_fixed(half, code)
            x_send[h, slot, XB:XB + 16, :] = code_rows(code, HALF)
            send(x_send.at[h, slot], x_recv.at[h, slot], SUM_X + h, at_x(to))

    def along_z(h):
        all_bytes(x_recv.at[h], recv_sem.at[SUM_X + h]).wait()
        half = own[h, 0] + from_fixed(x_recv[h, 0], XB) + from_fixed(x_recv[h, 1], XB)
        code = scale_code(whole_max(half))
        unit = 32767.0 * jnp.exp2(code * (-1.0 / 256.0))
        tail = jnp.broadcast_to(code, (8, HALF))
        own[h, 0] = half

        def one(d):
            z1 = lax.rem(z + d, NZ)
            v = own[h, 0, pl.ds(pl.multiple_of(z1 * TS, 8), TS), :]
            v = jnp.concatenate([v * unit, tail], axis=0)
            z_send[h, d] = v.astype(jnp.int32).astype(jnp.int16)
            send(z_send.at[h, d], z_recv.at[h, d], SUM_Z + h, at_z(d))

        each_far_first(NZ, one)

    def total_along_z(h):
        all_bytes(z_recv.at[h, pl.ds(1, NZ - 1)], recv_sem.at[SUM_Z + h]).wait()
        v = own[h, 0, pl.ds(pl.multiple_of(z * TS, 8), TS), :]
        return lax.fori_loop(1, NZ, lambda d, v: v + from_fixed(z_recv[h, d], TS), v)

    back_project()
    gram_along_y()
    first_along_x(0)
    first_along_x(1)
    second_along_x(0)
    gram_back_along_z()
    second_along_x(1)
    along_z(0)
    gram_back_along_x()
    along_z(1)
    gram_back_to_core()

    all_bytes(g_full.at[pl.ds(0, NX * GX)], recv_sem.at[G_BACK_C]).wait()
    gram[:, 0:128] = g_full[0:K, :]
    gram[:, 128:256] = g_full[K:2 * K, :]
    gram_out = pltpu.make_async_copy(gram, gram_hbm, load_sem.at[0])
    gram_out.start()
    matrix = gram[...]
    eye = identity(K)
    diagonal = matrix * eye
    d_row = lax.rsqrt(jnp.sum(diagonal, axis=0, keepdims=True))
    d_col = lax.rsqrt(jnp.sum(diagonal, axis=1, keepdims=True))
    unit_gram = matrix * d_row * d_col
    unit_halves = halves(unit_gram)
    start = eye - half_lower(unit_gram - eye)
    rough = start.astype(jnp.bfloat16)
    error = dot(dot(rough, unit_halves[0], 0).astype(jnp.bfloat16), rough, 1) - eye
    inverse[...] = start - dot(half_lower(error).astype(jnp.bfloat16), rough, 0)
    both = halves(inverse[...])
    error = dot3(halves(dot3(both, unit_halves, 0)), both, 1) - eye
    off_ref[...] = jnp.broadcast_to(whole_max(error), (8, 128))
    found = inverse[...] - dot(half_lower(error).astype(jnp.bfloat16), both[0], 0)
    both = halves(found * d_row)

    part = jnp.concatenate([total_along_z(0), total_along_z(1)], axis=1)
    part_ref[...] = part
    out_ref[...] = dot3(halves(part), both, 1)
    gram_out.wait()

    all_bytes(fx_recv, send_sem.at[AUX_FAR]).wait()
    all_bytes(f_send, send_sem.at[SKETCH_FAR]).wait()
    all_bytes(aux_send, send_sem.at[AUX]).wait()
    all_bytes(p_send, send_sem.at[SKETCH]).wait()
    all_bytes(w_all.at[pl.ds(0, 2)], send_sem.at[ROWS_NEAR]).wait()
    all_bytes(w_all.at[0], send_sem.at[ROWS_UP]).wait()
    all_bytes(w_all.at[0], send_sem.at[ROWS_DOWN]).wait()
    all_bytes(w_all.at[pl.ds(0, 3)], send_sem.at[ROWS_FAR]).wait()
    for h in range(2):
        all_bytes(x_send.at[h], send_sem.at[SUM_X + h]).wait()
        all_bytes(z_send.at[h, pl.ds(1, NZ - 1)], send_sem.at[SUM_Z + h]).wait()
    all_bytes(gx_recv.at[pl.ds(1, NU - 1)], send_sem.at[G_X]).wait()
    all_bytes(gz_recv.at[pl.ds(1, NZ - 1)], send_sem.at[G_Z]).wait()
    all_bytes(gy_recv.at[others], send_sem.at[G_Y]).wait()
    all_bytes(g_block.at[pl.ds(0, GX - GZ)], send_sem.at[G_BACK_Z]).wait()
    all_bytes(g_full.at[pl.ds(0, (NX - 1) * GX)], send_sem.at[G_BACK_X]).wait()
    all_bytes(g_full.at[side], send_sem.at[G_BACK_C]).wait()


def last_kernel(found_ref, off_ref, part_hbm, gram_hbm, out_ref, work, right, part, sem):
    K = work.shape[0]
    settled = jnp.max(off_ref[...]) < TOLERANCE
    out_ref[...] = found_ref[...]

    @pl.when(jnp.logical_not(settled))
    def _():
        load = pltpu.make_async_copy(gram_hbm, work, sem)
        load.start()
        load.wait()
        load = pltpu.make_async_copy(part_hbm, part, sem)
        load.start()
        load.wait()
        right[...] = identity(K)
        lane = lax.broadcasted_iota(jnp.int32, (1, K), 1)
        row = lax.broadcasted_iota(jnp.int32, (K, 1), 0)

        def step(k, _):
            m = work[...]
            top = work[pl.ds(k, 1), :]
            pivot = jnp.sum(jnp.where(lane == k, top, 0.0), axis=1, keepdims=True)
            column = jnp.sum(jnp.where(lane == k, m, 0.0), axis=1, keepdims=True)
            factor = jnp.where(row > k, column / pivot, 0.0)
            r = right[...]
            r_top = right[pl.ds(k, 1), :]
            work[...] = m - factor * top
            right[...] = r - factor * r_top
            return 0

        lax.fori_loop(0, K, step, 0)
        pivots = jnp.sum(work[...] * identity(K), axis=1, keepdims=True)
        out_ref[...] = times_t(part[...], right[...] / jnp.sqrt(pivots))


def solution(mesh, sizes=(4, 8, 8, 2)):
    NX, NY, NZ, NC = sizes

    def on_device(read_depth, gauss_sketch, keep_mask):
        rows, cols = read_depth.shape
        K = gauss_sketch.shape[1]
        RY = rows // NY
        TS = cols // (NX * NZ * NC)
        XB = NZ * TS
        NU = NX * NC
        GX = 2 * K // NU
        GZ = GX // NZ
        vmem = pl.BlockSpec(memory_space=pltpu.VMEM)
        hbm = pl.BlockSpec(memory_space=pl.ANY)
        i16 = jnp.int16
        found, part, gram, off = pl.pallas_call(
            functools.partial(main_kernel, NX, NY, NZ, NC),
            out_shape=(
                jax.ShapeDtypeStruct((TS, K), F32),
                jax.ShapeDtypeStruct((TS, K), F32),
                jax.ShapeDtypeStruct((K, K), F32),
                jax.ShapeDtypeStruct((8, 128), F32),
            ),
            in_specs=[hbm, hbm, vmem],
            out_specs=(vmem, vmem, hbm, vmem),
            scratch_shapes=[
                pltpu.VMEM((rows, cols), jnp.bfloat16),
                pltpu.VMEM((cols, K), jnp.bfloat16),
                pltpu.VMEM((cols, 128), jnp.bfloat16),
                pltpu.VMEM((cols, rows), jnp.bfloat16),
                pltpu.VMEM((rows // 2, K), F32),
                pltpu.VMEM((rows // 2, 128), F32),
                pltpu.VMEM((K, K), F32),
                pltpu.SemaphoreType.DMA((NY + 1,)),
                pltpu.VMEM((3, RY, K), i16),
                pltpu.VMEM((3, RY, K), i16),
                pltpu.VMEM((3, 8, 128), F32),
                pltpu.VMEM((4, 8, 128), F32),
                pltpu.VMEM((4, RY, K), i16),
                pltpu.VMEM((4, RY, K), i16),
                pltpu.VMEM((4, 8, 128), F32),
                pltpu.VMEM((4, 8, 128), F32),
                pltpu.VMEM((NY, RY, K), jnp.bfloat16),
                pltpu.VMEM((2 * K, 128), F32),
                pltpu.VMEM((NU, GX, 128), F32),
                pltpu.VMEM((GX, 128), F32),
                pltpu.VMEM((NZ, GZ, 128), F32),
                pltpu.VMEM((GZ, 128), F32),
                pltpu.VMEM((NY, GZ, 128), F32),
                pltpu.VMEM((GX, 128), F32),
                pltpu.VMEM((2 * K, 128), F32),
                pltpu.VMEM((K, K), F32),
                pltpu.VMEM((2, NX, NZ, NC, TS, HALF), F32),
                pltpu.VMEM((2, NX, NZ, TS, HALF), F32),
                pltpu.VMEM((2, NX, XB, HALF), F32),
                pltpu.VMEM((2, 2, XB // 2 + 16, HALF), i16),
                pltpu.VMEM((2, 2, XB // 2 + 16, HALF), i16),
                pltpu.VMEM((2, 2, XB + 16, HALF), i16),
                pltpu.VMEM((2, 2, XB + 16, HALF), i16),
                pltpu.VMEM((2, NZ, TS + 8, HALF), i16),
                pltpu.VMEM((2, NZ, TS + 8, HALF), i16),
                pltpu.SemaphoreType.DMA((PHASES,)),
                pltpu.SemaphoreType.DMA((PHASES,)),
                pltpu.SemaphoreType.DMA((2, NX)),
                pltpu.SemaphoreType.DMA((2, NX)),
                pltpu.SemaphoreType.DMA((2, 2)),
                pltpu.SemaphoreType.DMA((2, 2)),
            ],
            compiler_params=pltpu.CompilerParams(
                collective_id=0, has_side_effects=True, vmem_limit_bytes=60 << 20
            ),
        )(read_depth, gauss_sketch, keep_mask)
        return pl.pallas_call(
            last_kernel,
            out_shape=jax.ShapeDtypeStruct((TS, K), F32),
            in_specs=[vmem, vmem, hbm, hbm],
            out_specs=vmem,
            scratch_shapes=[
                pltpu.VMEM((K, K), F32),
                pltpu.VMEM((K, K), F32),
                pltpu.VMEM((TS, K), F32),
                pltpu.SemaphoreType.DMA,
            ],
            compiler_params=pltpu.CompilerParams(vmem_limit_bytes=60 << 20),
        )(found, off, part, gram)

    return jax.shard_map(
        on_device,
        mesh=mesh,
        in_specs=(P("samples", "targets"), P("targets", None), P("targets")),
        out_specs=P(("targets", "samples"), None),
        check_vma=False,
    )
```

```python
import functools

import jax
import jax.numpy as jnp
from jax import lax
from jax.experimental import pallas as pl
from jax.experimental.pallas import tpu as pltpu
from jax.sharding import PartitionSpec as P

MESH = pl.DeviceIdType.MESH
F32 = jnp.float32
HIGH = lax.Precision.HIGHEST
TOLERANCE = 1e-2
HALF = 128
AUX_FAR, SKETCH_FAR, AUX, SKETCH, G_X, G_Z, G_Y, G_BACK_Z, G_BACK_X, G_BACK_C = 0, 1, 2, 3, 5, 6, 7, 8, 9, 10
SUM_X, SUM_Z, ROWS_NEAR, ROWS_UP, ROWS_DOWN, ROWS_FAR, PHASES = 11, 13, 15, 17, 19, 21, 23
CUT = 48


def far_first(n):
    return sorted(range(1, n), key=lambda d: -min(d, n - d))


def whole_max(v):
    return jnp.max(jnp.max(jnp.abs(v), axis=0, keepdims=True), axis=1, keepdims=True)


def scale_code(peak):
    return jnp.ceil(jnp.log2(jnp.maximum(peak, 1e-30)) * 256.0) + 1.0


def to_fixed(v, code):
    unit = 32767.0 * jnp.exp2(code * (-1.0 / 256.0))
    return (v * unit).astype(jnp.int32).astype(jnp.int16)


def code_rows(code, columns):
    return jnp.broadcast_to(code.astype(jnp.int32), (16, columns)).astype(jnp.int16)


def from_fixed(message, rows):
    values = message.astype(jnp.int32).astype(F32)
    unit = jnp.exp2(values[rows:rows + 1] * (1.0 / 256.0)) * (1.0 / 32767.0)
    return values[:rows] * unit


def half_lower(e):
    k = e.shape[0]
    row = lax.broadcasted_iota(jnp.int32, (k, k), 0)
    col = lax.broadcasted_iota(jnp.int32, (k, k), 1)
    return jnp.where(row > col, e, jnp.where(row == col, 0.5 * e, 0.0))


def identity(k):
    row = lax.broadcasted_iota(jnp.int32, (k, k), 0)
    col = lax.broadcasted_iota(jnp.int32, (k, k), 1)
    return jnp.where(row == col, 1.0, 0.0).astype(F32)


def halves(a):
    high = a.astype(jnp.bfloat16)
    return high, (a - high.astype(F32)).astype(jnp.bfloat16)


def dot(a, b, side):
    return lax.dot_general(a, b, (((1,), (side,)), ((), ())), preferred_element_type=F32)


def dot3(a, b, side):
    a_high, a_low = a
    b_high, b_low = b
    return dot(a_high, b_high, side) + (dot(a_high, b_low, side) + dot(a_low, b_high, side))


def times_t(a, b):
    return lax.dot_general(a, b, (((1,), (1,)), ((), ())), precision=HIGH, preferred_element_type=F32)


def all_bytes(ref, sem):
    return pltpu.make_async_copy(ref, ref, sem)


def main_kernel(
    NX, NY, NZ, NC,
    depth_hbm, gauss_hbm, keep_ref,
    out_ref, part_ref, gram_hbm, off_ref,
    depth, gauss, keep_col, depth_t, raw_sum, q_sum, inverse, load_sem,
    f_send, f_recv, fx_send, fx_recv, p_send, p_recv, aux_send, aux_recv, w_all,
    g_own, gx_recv, g_sum, gz_recv, g_piece, gy_recv, g_block, g_full, gram,
    terms, c_recv, own, h_send, h_recv, x_send, x_recv, z_send, z_recv,
    send_sem, recv_sem, core_send_sem, core_recv_sem, h_send_sem, h_recv_sem,
):
    rows, cols = depth.shape
    K = gauss.shape[1]
    RY = rows // NY
    TS = cols // (NX * NZ * NC)
    XB = NZ * TS
    H = XB // 2
    NU = NX * NC
    GX = 2 * K // NU
    GZ = GX // NZ

    s = lax.axis_index("samples")
    y = lax.axis_index("targets")
    core = lax.rem(s, NC)
    z = lax.rem(s // NC, NZ)
    x = s // (NC * NZ)
    u = core * NX + x

    def at_y(d):
        return (s, lax.rem(y + d, NY))

    def place(x1, z1, c1):
        return ((x1 * NZ + z1) * NC + c1, y)

    def at_u(d):
        u1 = lax.rem(u + d, NU)
        return place(lax.rem(u1, NX), z, u1 // NX)

    def at_z(d):
        return place(x, lax.rem(z + d, NZ), core)

    def at_x(d):
        return place(lax.rem(x + d, NX), z, core)

    def at_core():
        return place(x, z, 1 - core)

    def send(src, dst, phase, to):
        pltpu.make_async_remote_copy(
            src_ref=src, dst_ref=dst, send_sem=send_sem.at[phase], recv_sem=recv_sem.at[phase],
            device_id=to, device_id_type=MESH,
        ).start()

    y_order = far_first(NY)

    def each_far_first(n, body):
        def step(i, _):
            k = (i + 1) // 2
            body(n // 2 + jnp.where(lax.rem(i, 2) == 0, k, -k))
            return 0

        lax.fori_loop(0, n - 1, step, 0)

    def sum_over(n, first, ref):
        return lax.fori_loop(1, n, lambda d, total: total + ref[d], first)

    others = pl.ds(1, NY - 1)

    def row_block(y1):
        return pl.ds(pl.multiple_of(y1 * RY, 16), RY)

    order = y_order + [0]
    gauss_load = pltpu.make_async_copy(gauss_hbm, gauss, load_sem.at[0])
    gauss_load.start()
    loads = []
    for i, d in enumerate(order):
        load = pltpu.make_async_copy(
            depth_hbm.at[row_block(lax.rem(y + d, NY))], depth.at[pl.ds(i * RY, RY)], load_sem.at[i + 1]
        )
        load.start()
        loads.append(load)

    barrier = pltpu.get_barrier_semaphore()
    for n, at in ((NY, at_y), (NU, at_u), (NZ, at_z)):
        each_far_first(n, lambda d, at=at: pl.semaphore_signal(
            barrier, inc=1, device_id=at(d), device_id_type=MESH))

    kept = keep_ref[...].astype(F32).reshape(1, cols)
    count = jnp.sum(kept, axis=1, keepdims=True)
    sub = lax.broadcasted_iota(jnp.int32, (8, 128), 0)
    for j in range(cols // 128):
        tile = jnp.broadcast_to(kept[:, j * 128:(j + 1) * 128], (128, 128)).T
        keep_col[j * 128:(j + 1) * 128, :] = tile.astype(jnp.bfloat16)
    gauss_load.wait()
    tiles = cols // 128

    def aux_of(q_row, code, number):
        return jnp.where(sub == 0, q_row, jnp.where(sub == 1, code, jnp.where(sub == 2, number, 0.0)))

    def row_of(q):
        row = q.T[0:1]
        if RY < 128:
            row = jnp.concatenate([row, jnp.zeros((1, 128 - RY), F32)], axis=1)
        return row

    def unit_of(aux):
        return jnp.exp2(aux[1:2, 0:1] * (1.0 / 256.0)) * (1.0 / 32767.0)

    def columns_of(tiles):
        tile = jnp.concatenate([t[0:1] for t in tiles] + [jnp.zeros((8 - len(tiles), 128), F32)], axis=0)
        turned = tile.T[:RY]
        return [turned[:, i:i + 1] for i in range(len(tiles))]

    def safe_root(q):
        return jnp.sqrt(jnp.maximum(q, 1e-30))

    def turn(j, _):
        at = pl.ds(pl.multiple_of(j * 128, 128), 128)
        tile = keep_col[at, :]
        depth_t[at, :] = depth[:, at].T * jnp.concatenate([tile] * (rows // 128), axis=1)
        return 0

    group = NY // 2
    raws, q_rows, q_cols = {}, {}, {}
    for g in range(2):
        for i in range(g * group, (g + 1) * group):
            loads[i].wait()
        span = slice(g * group * RY, (g + 1) * group * RY)
        raw_sum[...] = jnp.zeros_like(raw_sum)
        q_sum[...] = jnp.zeros_like(q_sum)

        def add_columns(j, _):
            at = pl.ds(pl.multiple_of(j * 256, 256), 256)
            if g == 0:
                gauss[at, :] = gauss[at, :] * jnp.concatenate([keep_col[at, :]] * (K // 128), axis=1)
            values = depth[span, at]
            raw_sum[...] += jnp.dot(values, gauss[at, :], preferred_element_type=F32)
            q_sum[...] += jnp.dot(values * values, keep_col[at, :], preferred_element_type=F32)
            return 0

        lax.fori_loop(0, cols // 256, add_columns, 0)
        raw = raw_sum[...]
        q = q_sum[...]
        for i in range(group):
            d = order[g * group + i]
            at = slice(i * RY, (i + 1) * RY)
            raws[d], q_rows[d], q_cols[d] = raw[at], row_of(q[at]), q[at, 0:1]
        some = slice(0, 3 * RY) if g == 0 else slice(RY, 3 * RY)
        invert = lax.rsqrt(jnp.maximum(q[some], 1e-30))
        level = [raw[some, h * HALF:(h + 1) * HALF] * invert for h in range(2)]
        code = scale_code(jnp.maximum(whole_max(level[0]), whole_max(level[1])))
        fixed = [to_fixed(part, code) for part in level]
        if g == 0:
            for i, d in enumerate((4, 3, 5)):
                for h in range(2):
                    f_send[i, :, h * HALF:(h + 1) * HALF] = fixed[h][i * RY:(i + 1) * RY]
                fx_send[i] = aux_of(q_rows[d], code, count)
            pl.semaphore_wait(barrier, NY + NU + NZ - 3)
            upper, lower = pl.ds(0, CUT), pl.ds(CUT, RY - CUT)
            send(fx_send.at[0], fx_recv.at[2], AUX_FAR, at_y(2))
            send(fx_send.at[0], fx_recv.at[3], AUX_FAR, at_y(NY - 2))
            send(f_send.at[0, upper], f_recv.at[2, upper], SKETCH_FAR, at_y(2))
            send(f_send.at[0, lower], f_recv.at[2, lower], SKETCH_FAR, at_y(NY - 2))
            for i, to in ((1, 1), (2, NY - 1)):
                send(fx_send.at[i], fx_recv.at[i - 1], AUX_FAR, at_y(to))
                send(f_send.at[i], f_recv.at[i - 1], SKETCH_FAR, at_y(to))
        else:
            for i, d in enumerate((1, NY - 1)):
                for h in range(2):
                    p_send[i, :, h * HALF:(h + 1) * HALF] = fixed[h][i * RY:(i + 1) * RY]
                aux_send[i] = aux_of(q_rows[d], code, count)
                send(aux_send.at[i], aux_recv.at[i], AUX, at_y(d))
                send(p_send.at[i], p_recv.at[i], SKETCH, at_y(d))

    lax.fori_loop(0, tiles // 4, turn, 0)

    all_bytes(fx_recv, recv_sem.at[AUX_FAR]).wait()
    all_bytes(f_recv, recv_sem.at[SKETCH_FAR]).wait()
    lane = lax.broadcasted_iota(jnp.int32, (1, 128), 1)
    far = [fx_recv[i] for i in range(4)]
    far_cols = columns_of(far)
    far_unit = [unit_of(t) for t in far]
    last = f_recv[2].astype(jnp.int32).astype(F32)
    row = lax.broadcasted_iota(jnp.int32, (RY, 1), 0)
    for i, d in ((0, 2), (1, NY - 2)):
        part = (row < CUT) if i == 0 else (row >= CUT)
        q_part = (lane < CUT) if i == 0 else (lane >= CUT)
        total = raws[d] + f_recv[i].astype(jnp.int32).astype(F32) * (safe_root(far_cols[i]) * far_unit[i])
        total = total + last * jnp.where(part, safe_root(far_cols[2 + i]) * far_unit[2 + i], 0.0)
        q_col = q_cols[d] + far_cols[i] + jnp.where(part, far_cols[2 + i], 0.0)
        q_row = q_rows[d] + far[i][0:1] + jnp.where(q_part, far[2 + i][0:1], 0.0)
        number = count + far[i][2:3, 0:1]
        if i == 0:
            number = number + far[2][2:3, 0:1]
        level = total * lax.rsqrt(jnp.maximum(q_col, 1e-30))
        code = scale_code(whole_max(level))
        fixed = to_fixed(level, code)
        aux_send[2 + i] = aux_of(q_row, code, number)
        send(aux_send.at[2 + i], aux_recv.at[2 + i], AUX, at_y(d))
        p_send[2 + i] = fixed
        send(p_send.at[2 + i], p_recv.at[2 + i], SKETCH, at_y(d))

    lax.fori_loop(tiles // 4, tiles // 2, turn, 0)

    all_bytes(aux_recv, recv_sem.at[AUX]).wait()
    near = [aux_recv[i] for i in range(4)]
    near_cols = columns_of(near)
    q_total, counts = q_cols[0], count
    for i in range(4):
        q_total = q_total + near_cols[i]
        counts = counts + near[i][2:3, 0:1]
    to_scaled = lax.rsqrt((q_total + 1.0) / (counts + 1.0))
    roots = [safe_root(near_cols[i]) * unit_of(near[i]) for i in range(4)]

    def slot(d):
        return order.index(d % NY)

    all_bytes(p_recv, recv_sem.at[SKETCH]).wait()
    raw = raws[0]
    for i in range(4):
        raw = raw + p_recv[i].astype(jnp.int32).astype(F32) * roots[i]
    sketched = raw * to_scaled
    w_all[slot(0)] = (sketched * to_scaled).astype(jnp.bfloat16)
    for d, phase in ((2, ROWS_UP), (NY - 2, ROWS_DOWN), (1, ROWS_NEAR), (NY - 1, ROWS_NEAR)):
        send(w_all.at[slot(0)], w_all.at[slot(-d)], phase, at_y(d))

    def pass_on():
        for phase, back, part in ((ROWS_UP, -2, pl.ds(0, CUT)), (ROWS_DOWN, 2, pl.ds(CUT, RY - CUT))):
            ahead = -back // 2
            held = w_all.at[slot(back)]
            all_bytes(held, recv_sem.at[phase]).wait()
            send(held.at[part], w_all.at[slot(2 * back), part], ROWS_FAR, at_y((2 * ahead) % NY))
            send(held, w_all.at[slot(back - ahead)], ROWS_FAR, at_y(ahead % NY))

    own_gram = dot3(halves(sketched.T), halves(sketched), 0)
    g_own[0:K, :] = own_gram[:, :HALF]
    g_own[K:2 * K, :] = own_gram[:, HALF:]
    def send_x(d):
        u1 = lax.rem(u + d, NU)
        send(g_own.at[pl.ds(pl.multiple_of(u1 * GX, 8), GX)], gx_recv.at[d], G_X, at_u(d))

    each_far_first(NU, send_x)
    lax.fori_loop(tiles // 2, 3 * tiles // 4, turn, 0)
    pass_on()
    lax.fori_loop(3 * tiles // 4, tiles, turn, 0)
    all_bytes(gx_recv.at[pl.ds(1, NU - 1)], recv_sem.at[G_X]).wait()
    g_sum[...] = sum_over(NU, g_own[pl.ds(pl.multiple_of(u * GX, 8), GX), :], gx_recv)

    def send_z(d):
        z1 = lax.rem(z + d, NZ)
        send(g_sum.at[pl.ds(pl.multiple_of(z1 * GZ, 8), GZ)], gz_recv.at[d], G_Z, at_z(d))

    each_far_first(NZ, send_z)

    def gram_along_y():
        all_bytes(gz_recv.at[pl.ds(1, NZ - 1)], recv_sem.at[G_Z]).wait()
        g_piece[...] = sum_over(NZ, g_sum[pl.ds(pl.multiple_of(z * GZ, 8), GZ), :], gz_recv)
        each_far_first(NY, lambda d: send(g_piece, gy_recv.at[d], G_Y, at_y(d)))

    def gram_back_along_z():
        all_bytes(gy_recv.at[others], recv_sem.at[G_Y]).wait()
        here = pl.ds(pl.multiple_of(z * GZ, 8), GZ)
        g_block[here, :] = sum_over(NY, g_piece[...], gy_recv)
        each_far_first(NZ, lambda d: send(g_block.at[here], g_block.at[here], G_BACK_Z, at_z(d)))

    def gram_back_along_x():
        all_bytes(g_block.at[pl.ds(0, GX - GZ)], recv_sem.at[G_BACK_Z]).wait()
        there = pl.ds(pl.multiple_of(u * GX, 8), GX)
        g_full[there, :] = g_block[...]
        each_far_first(NX, lambda d: send(g_block, g_full.at[there], G_BACK_X, at_x(d)))

    side = pl.ds(pl.multiple_of(core * (NX * GX), 8), NX * GX)

    def gram_back_to_core():
        all_bytes(g_full.at[pl.ds(0, (NX - 1) * GX)], recv_sem.at[G_BACK_X]).wait()
        send(g_full.at[side], g_full.at[side], G_BACK_C, at_core())

    def core_copy(h, d):
        return pltpu.make_async_remote_copy(
            src_ref=terms.at[h, d, :, 1 - core], dst_ref=c_recv.at[h, d],
            send_sem=core_send_sem.at[h, d], recv_sem=core_recv_sem.at[h, d],
            device_id=at_core(), device_id_type=MESH,
        )

    def back_project():
        all_bytes(w_all.at[pl.ds(0, 2)], recv_sem.at[ROWS_NEAR]).wait()
        all_bytes(w_all.at[pl.ds(0, 3)], recv_sem.at[ROWS_FAR]).wait()

        def one(i, _):
            d = lax.rem(NX // 2 + i, NX)
            x1 = lax.rem(x + d, NX)
            block = depth_t[pl.ds(pl.multiple_of(x1 * (XB * NC), 16), XB * NC), :]
            product = jnp.dot(block, w_all[...].reshape(rows, K), preferred_element_type=F32)
            for h in range(2):
                terms[h, d] = product[:, h * HALF:(h + 1) * HALF].reshape(NZ, NC, TS, HALF)
                core_copy(h, d).start()
            return 0

        lax.fori_loop(0, NX, one, 0)

    ways = ((0, 1), (1, NX - 1))

    def way_copy(h, slot, to):
        return pltpu.make_async_remote_copy(
            src_ref=h_send.at[h, slot], dst_ref=h_recv.at[h, slot],
            send_sem=h_send_sem.at[h, slot], recv_sem=h_recv_sem.at[h, slot],
            device_id=at_x(to), device_id_type=MESH,
        )

    def first_along_x(h):
        def both_cores(d):
            core_copy(h, d).wait()
            return (terms[h, d, :, core] + c_recv[h, d]).reshape(XB, HALF)

        half = both_cores(NX // 2)
        code = scale_code(whole_max(half))
        fixed = to_fixed(half, code)
        for slot, to in ways:
            h_send[h, slot, 0:H, :] = fixed[slot * H:(slot + 1) * H]
            h_send[h, slot, H:H + 16, :] = code_rows(code, HALF)
            way_copy(h, slot, to).start()

        def rest(i, _):
            d = lax.rem(NX // 2 + i, NX)
            own[h, d] = both_cores(d)
            return 0

        lax.fori_loop(1, NX, rest, 0)

    def second_along_x(h):
        for slot, to in ways:
            way_copy(h, slot, to).wait()
            mid = pl.ds(slot * H, H)
            own[h, to, mid, :] = own[h, to, mid, :] + from_fixed(h_recv[h, slot], H)
            half = own[h, to]
            code = scale_code(whole_max(half))
            x_send[h, slot, 0:XB, :] = to_fixed(half, code)
            x_send[h, slot, XB:XB + 16, :] = code_rows(code, HALF)
            send(x_send.at[h, slot], x_recv.at[h, slot], SUM_X + h, at_x(to))

    def along_z(h):
        all_bytes(x_recv.at[h], recv_sem.at[SUM_X + h]).wait()
        half = own[h, 0] + from_fixed(x_recv[h, 0], XB) + from_fixed(x_recv[h, 1], XB)
        code = scale_code(whole_max(half))
        unit = 32767.0 * jnp.exp2(code * (-1.0 / 256.0))
        tail = jnp.broadcast_to(code, (8, HALF))
        own[h, 0] = half

        def one(d):
            z1 = lax.rem(z + d, NZ)
            v = own[h, 0, pl.ds(pl.multiple_of(z1 * TS, 8), TS), :]
            v = jnp.concatenate([v * unit, tail], axis=0)
            z_send[h, d] = v.astype(jnp.int32).astype(jnp.int16)
            send(z_send.at[h, d], z_recv.at[h, d], SUM_Z + h, at_z(d))

        each_far_first(NZ, one)

    def total_along_z(h):
        all_bytes(z_recv.at[h, pl.ds(1, NZ - 1)], recv_sem.at[SUM_Z + h]).wait()
        v = own[h, 0, pl.ds(pl.multiple_of(z * TS, 8), TS), :]
        return lax.fori_loop(1, NZ, lambda d, v: v + from_fixed(z_recv[h, d], TS), v)

    back_project()
    gram_along_y()
    first_along_x(0)
    first_along_x(1)
    second_along_x(0)
    gram_back_along_z()
    second_along_x(1)
    along_z(0)
    gram_back_along_x()
    along_z(1)
    gram_back_to_core()

    left_part = total_along_z(0)

    all_bytes(g_full.at[pl.ds(0, NX * GX)], recv_sem.at[G_BACK_C]).wait()
    gram[:, 0:128] = g_full[0:K, :]
    gram[:, 128:256] = g_full[K:2 * K, :]
    gram_out = pltpu.make_async_copy(gram, gram_hbm, load_sem.at[0])
    gram_out.start()
    matrix = gram[...]
    eye = identity(K)
    diagonal = matrix * eye
    d_row = lax.rsqrt(jnp.sum(diagonal, axis=0, keepdims=True))
    d_col = lax.rsqrt(jnp.sum(diagonal, axis=1, keepdims=True))
    unit_gram = matrix * d_row * d_col
    unit_halves = halves(unit_gram)
    start = eye - half_lower(unit_gram - eye)
    rough = start.astype(jnp.bfloat16)
    error = dot(dot(rough, unit_halves[0], 0).astype(jnp.bfloat16), rough, 1) - eye
    inverse[...] = start - dot(half_lower(error).astype(jnp.bfloat16), rough, 0)
    both = halves(inverse[...])
    error = dot3(halves(dot3(both, unit_halves, 0)), both, 1) - eye
    off_ref[...] = jnp.broadcast_to(whole_max(error), (8, 128))
    found = inverse[...] - dot(half_lower(error).astype(jnp.bfloat16), both[0], 0)
    both = halves(found * d_row)

    part = jnp.concatenate([left_part, total_along_z(1)], axis=1)
    part_ref[...] = part
    out_ref[...] = dot3(halves(part), both, 1)
    gram_out.wait()

    all_bytes(fx_recv, send_sem.at[AUX_FAR]).wait()
    all_bytes(f_send, send_sem.at[SKETCH_FAR]).wait()
    all_bytes(aux_send, send_sem.at[AUX]).wait()
    all_bytes(p_send, send_sem.at[SKETCH]).wait()
    all_bytes(w_all.at[pl.ds(0, 2)], send_sem.at[ROWS_NEAR]).wait()
    all_bytes(w_all.at[0], send_sem.at[ROWS_UP]).wait()
    all_bytes(w_all.at[0], send_sem.at[ROWS_DOWN]).wait()
    all_bytes(w_all.at[pl.ds(0, 3)], send_sem.at[ROWS_FAR]).wait()
    for h in range(2):
        all_bytes(x_send.at[h], send_sem.at[SUM_X + h]).wait()
        all_bytes(z_send.at[h, pl.ds(1, NZ - 1)], send_sem.at[SUM_Z + h]).wait()
    all_bytes(gx_recv.at[pl.ds(1, NU - 1)], send_sem.at[G_X]).wait()
    all_bytes(gz_recv.at[pl.ds(1, NZ - 1)], send_sem.at[G_Z]).wait()
    all_bytes(gy_recv.at[others], send_sem.at[G_Y]).wait()
    all_bytes(g_block.at[pl.ds(0, GX - GZ)], send_sem.at[G_BACK_Z]).wait()
    all_bytes(g_full.at[pl.ds(0, (NX - 1) * GX)], send_sem.at[G_BACK_X]).wait()
    all_bytes(g_full.at[side], send_sem.at[G_BACK_C]).wait()


def last_kernel(found_hbm, off_hbm, part_hbm, gram_hbm, out_hbm, off, work, right, part, out, sem, take_sem):
    K = work.shape[0]
    take = pltpu.make_async_copy(found_hbm, out_hbm, take_sem)
    take.start()
    load = pltpu.make_async_copy(off_hbm, off, sem)
    load.start()
    load.wait()
    settled = jnp.max(off[...]) < TOLERANCE
    take.wait()

    @pl.when(jnp.logical_not(settled))
    def _():
        load = pltpu.make_async_copy(gram_hbm, work, sem)
        load.start()
        load.wait()
        load = pltpu.make_async_copy(part_hbm, part, sem)
        load.start()
        load.wait()
        right[...] = identity(K)
        lane = lax.broadcasted_iota(jnp.int32, (1, K), 1)
        row = lax.broadcasted_iota(jnp.int32, (K, 1), 0)

        def step(k, _):
            m = work[...]
            top = work[pl.ds(k, 1), :]
            pivot = jnp.sum(jnp.where(lane == k, top, 0.0), axis=1, keepdims=True)
            column = jnp.sum(jnp.where(lane == k, m, 0.0), axis=1, keepdims=True)
            factor = jnp.where(row > k, column / pivot, 0.0)
            r = right[...]
            r_top = right[pl.ds(k, 1), :]
            work[...] = m - factor * top
            right[...] = r - factor * r_top
            return 0

        lax.fori_loop(0, K, step, 0)
        pivots = jnp.sum(work[...] * identity(K), axis=1, keepdims=True)
        out[...] = times_t(part[...], right[...] / jnp.sqrt(pivots))
        store = pltpu.make_async_copy(out, out_hbm, sem)
        store.start()
        store.wait()


def solution(mesh, sizes=(4, 8, 8, 2)):
    NX, NY, NZ, NC = sizes

    def on_device(read_depth, gauss_sketch, keep_mask):
        rows, cols = read_depth.shape
        K = gauss_sketch.shape[1]
        RY = rows // NY
        TS = cols // (NX * NZ * NC)
        XB = NZ * TS
        NU = NX * NC
        GX = 2 * K // NU
        GZ = GX // NZ
        vmem = pl.BlockSpec(memory_space=pltpu.VMEM)
        hbm = pl.BlockSpec(memory_space=pl.ANY)
        i16 = jnp.int16
        found, part, gram, off = pl.pallas_call(
            functools.partial(main_kernel, NX, NY, NZ, NC),
            out_shape=(
                jax.ShapeDtypeStruct((TS, K), F32),
                jax.ShapeDtypeStruct((TS, K), F32),
                jax.ShapeDtypeStruct((K, K), F32),
                jax.ShapeDtypeStruct((8, 128), F32),
            ),
            in_specs=[hbm, hbm, vmem],
            out_specs=(vmem, vmem, hbm, vmem),
            scratch_shapes=[
                pltpu.VMEM((rows, cols), jnp.bfloat16),
                pltpu.VMEM((cols, K), jnp.bfloat16),
                pltpu.VMEM((cols, 128), jnp.bfloat16),
                pltpu.VMEM((cols, rows), jnp.bfloat16),
                pltpu.VMEM((rows // 2, K), F32),
                pltpu.VMEM((rows // 2, 128), F32),
                pltpu.VMEM((K, K), F32),
                pltpu.SemaphoreType.DMA((NY + 1,)),
                pltpu.VMEM((3, RY, K), i16),
                pltpu.VMEM((3, RY, K), i16),
                pltpu.VMEM((3, 8, 128), F32),
                pltpu.VMEM((4, 8, 128), F32),
                pltpu.VMEM((4, RY, K), i16),
                pltpu.VMEM((4, RY, K), i16),
                pltpu.VMEM((4, 8, 128), F32),
                pltpu.VMEM((4, 8, 128), F32),
                pltpu.VMEM((NY, RY, K), jnp.bfloat16),
                pltpu.VMEM((2 * K, 128), F32),
                pltpu.VMEM((NU, GX, 128), F32),
                pltpu.VMEM((GX, 128), F32),
                pltpu.VMEM((NZ, GZ, 128), F32),
                pltpu.VMEM((GZ, 128), F32),
                pltpu.VMEM((NY, GZ, 128), F32),
                pltpu.VMEM((GX, 128), F32),
                pltpu.VMEM((2 * K, 128), F32),
                pltpu.VMEM((K, K), F32),
                pltpu.VMEM((2, NX, NZ, NC, TS, HALF), F32),
                pltpu.VMEM((2, NX, NZ, TS, HALF), F32),
                pltpu.VMEM((2, NX, XB, HALF), F32),
                pltpu.VMEM((2, 2, XB // 2 + 16, HALF), i16),
                pltpu.VMEM((2, 2, XB // 2 + 16, HALF), i16),
                pltpu.VMEM((2, 2, XB + 16, HALF), i16),
                pltpu.VMEM((2, 2, XB + 16, HALF), i16),
                pltpu.VMEM((2, NZ, TS + 8, HALF), i16),
                pltpu.VMEM((2, NZ, TS + 8, HALF), i16),
                pltpu.SemaphoreType.DMA((PHASES,)),
                pltpu.SemaphoreType.DMA((PHASES,)),
                pltpu.SemaphoreType.DMA((2, NX)),
                pltpu.SemaphoreType.DMA((2, NX)),
                pltpu.SemaphoreType.DMA((2, 2)),
                pltpu.SemaphoreType.DMA((2, 2)),
            ],
            compiler_params=pltpu.CompilerParams(
                collective_id=0, has_side_effects=True, vmem_limit_bytes=60 << 20
            ),
        )(read_depth, gauss_sketch, keep_mask)
        return pl.pallas_call(
            last_kernel,
            out_shape=jax.ShapeDtypeStruct((TS, K), F32),
            in_specs=[hbm, hbm, hbm, hbm],
            out_specs=hbm,
            scratch_shapes=[
                pltpu.VMEM((8, 128), F32),
                pltpu.VMEM((K, K), F32),
                pltpu.VMEM((K, K), F32),
                pltpu.VMEM((TS, K), F32),
                pltpu.VMEM((TS, K), F32),
                pltpu.SemaphoreType.DMA,
                pltpu.SemaphoreType.DMA,
            ],
            compiler_params=pltpu.CompilerParams(vmem_limit_bytes=60 << 20),
        )(found, off, part, gram)

    return jax.shard_map(
        on_device,
        mesh=mesh,
        in_specs=(P("samples", "targets"), P("targets", None), P("targets")),
        out_specs=P(("targets", "samples"), None),
        check_vma=False,
    )
```
